32 devices in a mesh: leaf: 8 (over y, x, core), row: 4 (over z).
Axes of the slice: x: 2, y: 2, z: 4, core: 2. Of those that a mesh axis runs over, the one named last changes fastest.
Arguments:
- rhs: bfloat16 [8, 4, 720, 512], P('leaf', 'row'), may hold values from -6 to 6
- inv_diag: bfloat16 [8, 4, 720, 1536], P('leaf', 'row'), may hold values from -0.15625 to 0.15625
- off_diag: bfloat16 [8, 4, 384, 6528], P('leaf', 'row'), may hold values from -0.078125 to 0.078125
- pair_mask: int32 [8, 4, 6], P('leaf', 'row'), may hold values 0 or 1
Outputs:
- solution: float32 [8, 4, 720, 512], P('leaf', 'row')
The draws below stay inside these ranges and needn't reach their ends.
All inputs are finite; a program needn't handle non-finite values. No bound on the sum of `pair_mask` on one device may be relied on, other than what follows from the above.
Results may differ from the reference program's by a relative error of at most 0.0065.
Values may be sent and summed in bfloat16 or wider, within the bound.
A program may use at most 64 MiB of HBM per device.

```python
import jax
import jax.numpy as jnp

W = 1536
R = 512
LEVELS = 3
PACK = 720
QCOLS = 6528
PAIRS = 6
N_LEAF = 8
N_ROW = 4


def with_ends(drawn, own_key, smallest, high):
    longest = drawn.shape.index(max(drawn.shape))
    spots = []
    for shift in (0, 1):
        where = [jax.random.randint(jax.random.fold_in(own_key, axis), (), 0, length) for axis, length in enumerate(drawn.shape)]
        where[longest] = (where[longest] + shift) % drawn.shape[longest]
        spots.append(tuple(where))
    return drawn.at[spots[0]].set(smallest).at[spots[1]].set(high)


def levels(rng, shape, pieces, smallest, largest):
    factor_of = 1.0
    for dim, blocks in pieces:
        draws = jax.random.uniform(jax.random.fold_in(jax.random.fold_in(rng, 6), dim), (blocks,), jnp.float32, smallest / len(pieces), largest / len(pieces))
        factor_of = factor_of * jnp.repeat(jnp.exp(draws), shape[dim] // blocks).reshape((-1,) + (1,) * (len(shape) - 1 - dim))
    return factor_of


def noise(rng, shape, scale, bound, cuts=(), dtype=jnp.bfloat16):
    values = scale * jax.random.normal(rng, shape, jnp.float32)
    if cuts:
        values = values * levels(rng, shape, cuts, -0.22, 0.18)
    return jnp.clip(values, -bound, bound).astype(dtype)


def setup_inputs(seed: int = 0) -> dict:
    splits = jax.random.split(jax.random.key(seed), 5)
    rhs = noise(splits[0], (N_LEAF, N_ROW, PACK, R), 1.0, 6.0, ((0, 8), (1, 4)))
    inv_diag = noise(splits[1], (N_LEAF, N_ROW, PACK, W), W ** -0.5, 0.15625, ((0, 8), (1, 4)))
    off_diag = noise(splits[2], (N_LEAF, N_ROW, W // N_ROW, QCOLS), (W * N_LEAF // 2) ** -0.5, 0.078125, ((0, 8), (1, 4)))
    pair_mask = with_ends((jax.random.randint(splits[3], (N_LEAF, N_ROW, PAIRS), 0, 4) < 3).astype(jnp.int32), jax.random.fold_in(splits[3], 1), 0, 1)
    return dict(rhs=rhs, inv_diag=inv_diag, off_diag=off_diag, pair_mask=pair_mask)


def split_level(packed, height_lv):
    height = W // (2 ** height_lv * N_ROW)
    offset = 0
    for below in range(height_lv):
        offset += W // (2 ** below * N_ROW)
    sliced = packed[:, :, offset:offset + height, :]
    node_count = N_LEAF // 2 ** height_lv
    return sliced.reshape(node_count, W, sliced.shape[-1])


def join_level(nodes_arr, height_lv):
    height = W // (2 ** height_lv * N_ROW)
    return nodes_arr.reshape(N_LEAF, N_ROW, height, nodes_arr.shape[-1])


def column_start(ancestor, source):
    offset = 0
    for higher in range(1, ancestor):
        for within in range(higher):
            offset += W // 2 ** within
    for within in range(source):
        offset += W // 2 ** within
    return offset


def ancestor_update(off_diag, pair_mask, rounded, ancestor):
    strip_rows = W // N_ROW
    summed = jnp.zeros((N_LEAF, N_ROW, strip_rows, R), jnp.float32)
    for source in range(ancestor):
        span_cols = W // 2 ** source
        first_col = column_start(ancestor, source)
        panel_part = off_diag[:, :, :, first_col:first_col + span_cols].astype(jnp.float32)
        pair_live = pair_mask[:, :, ancestor * (ancestor - 1) // 2 + source].astype(jnp.float32)
        leaf_parts = rounded[source].reshape(N_LEAF, span_cols, R).astype(jnp.float32)
        product = jnp.einsum('gpqc,gcn->gpqn', panel_part, leaf_parts)
        summed = summed + product * pair_live[:, :, None, None]
    height = W // (2 ** ancestor * N_ROW)
    node_count = N_LEAF // 2 ** ancestor
    summed = summed.reshape(node_count, 2 ** ancestor, N_ROW, 2 ** ancestor, height, R).sum(axis=1)
    return jnp.transpose(summed, (0, 2, 1, 3, 4)).reshape(node_count, W, R)


def reference(rhs, inv_diag, off_diag, pair_mask):
    solutions = []
    rounded = []
    for ancestor in range(LEVELS + 1):
        right_side = split_level(rhs, ancestor).astype(jnp.float32)
        if ancestor > 0:
            right_side = right_side - ancestor_update(off_diag, pair_mask, rounded, ancestor)
        reduced = right_side.astype(jnp.bfloat16)
        inverse = split_level(inv_diag, ancestor).astype(jnp.float32)
        solved = jnp.einsum('jvw,jwn->jvn', inverse, reduced.astype(jnp.float32))
        rounded.append(solved.astype(jnp.bfloat16))
        solutions.append(join_level(solved, ancestor))
    return jnp.concatenate(solutions, axis=2)
```

```python
import functools

import jax
import jax.numpy as jnp
from jax import lax
from jax.experimental import pallas as pl
from jax.experimental.pallas import tpu as pltpu
from jax.sharding import PartitionSpec as P

LANES = 128
ROW_TILE = 16
CHUNKS = 2
TREE_LEVELS = 3
MESH = pl.DeviceIdType.MESH


def partner_2(block, axis, bit):
    count = lax.axis_size(axis)
    route = []
    for low in range(count):
        high = low | 1 << bit
        if high != low and high < count:
            route += [(low, high), (high, low)]
    return lax.ppermute(block, axis, route)


def column_start(ancestor, width_all):
    offset = 0
    for higher in range(1, ancestor):
        for within in range(higher):
            offset += width_all // 2**within
    return offset


def shards(rhs, inv_diag, off_diag, pair_mask):
    rows_n = lax.axis_size("row")
    leaves = lax.axis_size("leaf")
    levels_n = leaves.bit_length() - 1
    leaf_index = lax.axis_index("leaf")
    width_all = inv_diag.shape[3]
    right_all = rhs[0, 0]
    inverse_all = inv_diag[0, 0]
    panels = off_diag[0, 0]
    live_pairs = pair_mask[0, 0].astype(jnp.bfloat16)
    known_parts = []
    outputs = []
    offset = 0
    for ancestor in range(levels_n + 1):
        height = width_all // (2**ancestor * rows_n)
        own_rhs = right_all[offset : offset + height]
        own_inv = inverse_all[offset : offset + height]
        offset += height
        if ancestor > 0:
            stacked = jnp.concatenate(
                [
                    known_parts[source] * live_pairs[ancestor * (ancestor - 1) // 2 + source]
                    for source in range(ancestor)
                ],
                axis=0,
            )
            first_col = column_start(ancestor, width_all)
            span_cols = stacked.shape[0]
            update = jnp.dot(
                panels[:, first_col : first_col + span_cols],
                stacked,
                preferred_element_type=jnp.float32,
            )
        if ancestor > 0:
            current = update
            for bit_pos in reversed(range(ancestor)):
                half_rows = current.shape[0] // 2
                upper_half = leaf_index // 2**bit_pos % 2 == 1
                kept_rows = jnp.where(upper_half, current[half_rows:], current[:half_rows])
                sent_rows = jnp.where(upper_half, current[:half_rows], current[half_rows:])
                current = kept_rows + partner_2(
                    sent_rows.astype(jnp.bfloat16), "leaf", bit_pos
                ).astype(sent_rows.dtype)
            reduced = (own_rhs.astype(jnp.float32) - current).astype(jnp.bfloat16)
        else:
            reduced = own_rhs
        gathered = lax.all_gather(reduced, "row", axis=0, tiled=True)
        for bit_pos in range(ancestor):
            partner = partner_2(gathered, "leaf", bit_pos)
            upper_half = leaf_index // 2**bit_pos % 2 == 1
            gathered = jnp.where(
                upper_half,
                jnp.concatenate([partner, gathered], axis=0),
                jnp.concatenate([gathered, partner], axis=0),
            )
        solved = jnp.dot(own_inv, gathered, preferred_element_type=jnp.float32)
        outputs.append(solved)
        if ancestor < levels_n:
            leaf_part = lax.all_gather(solved.astype(jnp.bfloat16), "row", axis=0, tiled=True)
            known_parts.append(leaf_part)
    return jnp.concatenate(outputs, axis=0)[None, None]


def dot32(left, right):
    return jnp.dot(left, right, preferred_element_type=jnp.float32)


GATHERS = ["z0a", "z0b", "y0a", "y0b", "z1a", "z1b", "y1a", "y1b", "z2", "y2", "z3"]
SWAPS = ["b1a", "b1b", "b2", "b3", "d1", "d2", "d3", "u1a", "u1b", "u2", "u3", "y1a", "y1b", "y2", "y3"]
LOCALS = ["z0a", "z0b", "d0", "p1", "p2", "p3", "d1", "d2", "d3", "b1a", "b1b", "b2", "b3"]


def tree_kernel(
    rows_n, leaves_n,
    mask, rhs, inv, pan, out,
    d0, d1, d2, d3, p1, p2, p3, b1, b2, b3,
    z0, z1, z2, z3, y0, y1, y2,
    u1, u2, u3, u1s, u2s, u3s, u1r, u2r, u3r, y1s, y2s, y3s, y3r,
    up_sem, down_sem, land_sem, swap_send, swap_recv, local_sem,
):
    leaf = lax.axis_index("leaf")
    row = lax.axis_index("row")
    height = p1.shape[0]
    right_n = u2.shape[1]
    chunk = right_n // CHUNKS
    heights = [height // 2**m for m in range(TREE_LEVELS + 1)]
    starts = [sum(heights[:m]) for m in range(TREE_LEVELS + 1)]
    wide = LANES
    suffix = "ab"
    pending = []
    place = [leaf % 2**m for m in range(TREE_LEVELS + 1)]

    def at_cols(index):
        return pl.ds(pl.multiple_of(index * wide, wide), wide)

    def level_rows(m):
        return pl.ds(starts[m], heights[m])

    barrier = pltpu.get_barrier_semaphore()

    @pl.when(row < rows_n - 1)
    def _():
        pl.semaphore_signal(barrier, inc=1, device_id=(leaf, row + 1), device_id_type=MESH)

    @pl.when(row > 0)
    def _():
        pl.semaphore_signal(barrier, inc=1, device_id=(leaf, row - 1), device_id_type=MESH)

    for d in range(1, leaves_n):
        pl.semaphore_signal(barrier, inc=1, device_id=((leaf + d) % leaves_n, row), device_id_type=MESH)

    def local(name, src, dst):
        return pltpu.make_async_copy(src, dst, local_sem.at[LOCALS.index(name)])

    local_copies = {}
    for c in range(CHUNKS):
        local_copies["z0" + suffix[c]] = local(
            "z0" + suffix[c], rhs.at[pl.ds(0, height), pl.ds(c * chunk, chunk)], z0.at[c, row])
    local_copies["d0"] = local("d0", inv.at[pl.ds(0, height)], d0)
    for m, held in ((1, p1), (2, p2), (3, p3)):
        local_copies["p%d" % m] = local(
            "p%d" % m, pan.at[:, pl.ds(column_start(m, d0.shape[1]), held.shape[1])], held)
    for m, held in ((1, d1), (2, d2), (3, d3)):
        local_copies["d%d" % m] = local("d%d" % m, inv.at[level_rows(m)], held.at[place[m]])
    for c in range(CHUNKS):
        local_copies["b1" + suffix[c]] = local(
            "b1" + suffix[c], rhs.at[level_rows(1), at_cols(2 * c + place[1])], b1.at[c, place[1]])
    local_copies["b2"] = local("b2", rhs.at[level_rows(2), at_cols(place[2])], b2.at[place[2]])
    local_copies["b3"] = local("b3", rhs.at[level_rows(3), at_cols(place[3] // 2)], b3.at[place[3]])
    for name in LOCALS:
        local_copies[name].start()

    def hops():
        return jnp.where(row > 0, 1, 0) + jnp.where(row < rows_n - 1, 1, 0)

    pl.semaphore_wait(barrier, hops() + leaves_n - 1)

    def hop(name, src, dst, step, source, way):
        k = GATHERS.index(name)
        sem = up_sem if way > 0 else down_sem
        return pltpu.make_async_remote_copy(
            src_ref=src, dst_ref=dst, send_sem=sem.at[k, step], recv_sem=land_sem.at[k, source],
            device_id=(leaf, row + way), device_id_type=MESH)

    def gather_start(name, slot, src=None):
        for way, can in ((1, row < rows_n - 1), (-1, row > 0)):
            def make(way=way):
                return hop(name, slot(row) if src is None else src, slot(row), 0, row, way)

            @pl.when(can)
            def _(make=make):
                make().start()

            pending.append((can, make))

    def gather_step(name, slot, step):
        for way, can in ((1, row < rows_n - 1), (-1, row > 0)):
            source = row - way * step
            there = (source >= 0) if way > 0 else (source < rows_n)

            def make(way=way, source=source):
                return hop(name, slot(source), slot(source), step, source, way)

            @pl.when(there)
            def _(make=make):
                make().wait_recv()

            if step < rows_n - 1:
                both = jnp.logical_and(there, can)

                @pl.when(both)
                def _(make=make):
                    make().start()

                pending.append((both, make))

    def peer(m, d):
        size = 2**m
        return leaf - place[m] + (place[m] + d) % size

    def swap(name, m, d, src, dst):
        k = SWAPS.index(name)
        return pltpu.make_async_remote_copy(
            src_ref=src, dst_ref=dst, send_sem=swap_send.at[k, d], recv_sem=swap_recv.at[k, d],
            device_id=(peer(m, d), row), device_id_type=MESH)

    def swap_start(name, m, src, dst, when=None):
        size = 2**m
        for d in range(1, size):
            target = (place[m] + d) % size

            def make(d=d, target=target):
                return swap(name, m, d, src(target), dst(place[m], d))

            if when is None:
                make().start()
                pending.append((None, make))
            else:
                can = when(target)

                @pl.when(can)
                def _(make=make):
                    make().start()

                pending.append((can, make))

    def swap_wait(name, m, src, dst):
        size = 2**m
        for d in range(1, size):
            sender = (place[m] - d + size) % size
            swap(name, m, d, src(place[m]), dst(sender, d)).wait_recv()

    def z0_slot(c):
        return lambda q: z0.at[c, q]

    def y0_slot(c):
        return lambda q: y0.at[c, q]

    def z1_slot(c):
        return lambda q: z1.at[c, :, q]

    def y1_slot(c):
        return lambda q: y1.at[c, q]

    def z2_slot(q):
        return z2.at[:, q]

    def y2_slot(q):
        return y2.at[q]

    def z3_slot(q):
        return z3.at[:, q]

    for c in range(CHUNKS):
        gather_start("z0" + suffix[c], z0_slot(c), rhs.at[pl.ds(0, height), pl.ds(c * chunk, chunk)])

    fixed = []
    for c in range(CHUNKS):
        fixed.append((
            "b1" + suffix[c], 1,
            lambda target, c=c: rhs.at[level_rows(1), at_cols(2 * c + target)],
            lambda sender, d, c=c: b1.at[c, sender]))
    fixed.append(("d1", 1, lambda target: inv.at[level_rows(1)], lambda sender, d: d1.at[sender]))
    fixed.append(("b2", 2, lambda target: rhs.at[level_rows(2), at_cols(target)], lambda sender, d: b2.at[sender]))
    fixed.append(("d2", 2, lambda target: inv.at[level_rows(2)], lambda sender, d: d2.at[sender]))
    fixed.append(("b3", 3, lambda target: rhs.at[level_rows(3), at_cols(target // 2)], lambda sender, d: b3.at[sender]))
    fixed.append(("d3", 3, lambda target: inv.at[level_rows(3)], lambda sender, d: d3.at[sender]))
    for entry in fixed:
        swap_start(*entry)

    def live(pair):
        return mask[pair].astype(jnp.float32)

    def cols_of(c):
        return pl.ds(c * chunk, chunk)

    for step in range(1, rows_n - 1):
        for c in range(CHUNKS):
            gather_step("z0" + suffix[c], z0_slot(c), step)
    local_copies["d0"].wait()
    whole = d0.shape[1]
    for c in range(CHUNKS):
        local_copies["z0" + suffix[c]].wait()
        gather_step("z0" + suffix[c], z0_slot(c), rows_n - 1)
        solved = dot32(d0[...], z0[c].reshape(whole, chunk))
        y0[c, row] = solved.astype(jnp.bfloat16)
        gather_start("y0" + suffix[c], y0_slot(c))
        out[pl.ds(0, height), cols_of(c)] = solved
    for step in range(1, rows_n - 1):
        for c in range(CHUNKS):
            gather_step("y0" + suffix[c], y0_slot(c), step)
    for name in ("p1", "p2", "p3"):
        local_copies[name].wait()

    for c in range(CHUNKS):
        gather_step("y0" + suffix[c], y0_slot(c), rows_n - 1)
        known = y0[c].reshape(whole, chunk)
        update = dot32(p1[...], known) * live(0)
        u1[c] = update
        u1s[c] = update.astype(jnp.bfloat16)
        name = "u1" + suffix[c]
        src = lambda target, c=c: u1s.at[c, :, at_cols(target)]
        dst = lambda sender, d, c=c: u1r.at[c, d - 1]
        swap_start(name, 1, src, dst)
        u2[:, cols_of(c)] = dot32(p2[:, :whole], known) * live(1)
        local_copies["b1" + suffix[c]].wait()
        swap_wait(*fixed[c])
        swap_wait(name, 1, src, dst)
        total = u1[c, :, at_cols(place[1])] + u1r[c, 0].astype(jnp.float32)
        reduced = (b1[c].reshape(height, wide).astype(jnp.float32) - total).astype(jnp.bfloat16)
        for s in range(2):
            z1[c, s, row] = reduced[s * heights[1] : (s + 1) * heights[1]]
        gather_start("z1" + suffix[c], z1_slot(c))
        u3[:, cols_of(c)] = dot32(p3[:, :whole], known) * live(3)
    for step in range(1, rows_n - 1):
        for c in range(CHUNKS):
            gather_step("z1" + suffix[c], z1_slot(c), step)
    local_copies["d1"].wait()
    swap_wait(*fixed[CHUNKS])
    y1_src = [lambda target, c=c: y1s.at[c, target] for c in range(CHUNKS)]
    y1_dst = [lambda sender, d, c=c: y1.at[c, row, :, at_cols(sender)] for c in range(CHUNKS)]
    for c in range(CHUNKS):
        gather_step("z1" + suffix[c], z1_slot(c), rows_n - 1)
        solved = dot32(d1[...].reshape(height, whole), z1[c].reshape(whole, wide)).astype(jnp.bfloat16)
        y1s[c] = solved.reshape(2, heights[1], wide)
        swap_start("y1" + suffix[c], 1, y1_src[c], y1_dst[c])
        y1[c, row, :, at_cols(place[1])] = y1s[c, place[1]]
        swap_wait("y1" + suffix[c], 1, y1_src[c], y1_dst[c])
        gather_start("y1" + suffix[c], y1_slot(c))
        out[level_rows(1), cols_of(c)] = y1[c, row].astype(jnp.float32)
    for step in range(1, rows_n - 1):
        for c in range(CHUNKS):
            gather_step("y1" + suffix[c], y1_slot(c), step)

    half = whole // 2
    u2_src = lambda target: u2s.at[:, at_cols(target)]
    u2_dst = lambda sender, d: u2r.at[d - 1]
    for c in range(CHUNKS):
        gather_step("y1" + suffix[c], y1_slot(c), rows_n - 1)
        known = y1[c].reshape(half, chunk)
        update = u2[:, cols_of(c)] + dot32(p2[:, whole:], known) * live(2)
        u2[:, cols_of(c)] = update
        u2s[:, cols_of(c)] = update.astype(jnp.bfloat16)
        swap_start("u2", 2, u2_src, u2_dst, lambda target, c=c: target // 2 == c)
        u3[:, cols_of(c)] += dot32(p3[:, whole : whole + half], known) * live(4)
    local_copies["b2"].wait()
    swap_wait(*fixed[CHUNKS + 1])
    swap_wait("u2", 2, u2_src, u2_dst)
    total = u2[:, at_cols(place[2])]
    for d in range(3):
        total = total + u2r[d].astype(jnp.float32)
    reduced = (b2[...].reshape(height, wide).astype(jnp.float32) - total).astype(jnp.bfloat16)
    for s in range(4):
        z2[s, row] = reduced[s * heights[2] : (s + 1) * heights[2]]
    gather_start("z2", z2_slot)
    local_copies["d2"].wait()
    swap_wait(*fixed[CHUNKS + 2])
    for step in range(1, rows_n):
        gather_step("z2", z2_slot, step)
    solved = dot32(d2[...].reshape(height, whole), z2[...].reshape(whole, wide)).astype(jnp.bfloat16)
    y2s[...] = solved.reshape(4, heights[2], wide)
    y2_src = lambda target: y2s.at[target]
    y2_dst = lambda sender, d: y2.at[row, :, at_cols(sender)]
    swap_start("y2", 2, y2_src, y2_dst)
    y2[row, :, at_cols(place[2])] = y2s[place[2]]
    swap_wait("y2", 2, y2_src, y2_dst)
    gather_start("y2", y2_slot)
    out[level_rows(2), :] = y2[row].astype(jnp.float32)
    for step in range(1, rows_n):
        gather_step("y2", y2_slot, step)

    update = u3[...] + dot32(p3[:, whole + half :], y2[...].reshape(whole // 4, right_n)) * live(5)
    fold = height // 2
    low = lax.broadcasted_iota(jnp.int32, (fold, wide), 1) < wide // 2
    def folded(top, bottom):
        return (
            jnp.where(low, top, pltpu.roll(bottom, wide // 2, 1)),
            jnp.where(low, pltpu.roll(top, wide // 2, 1), bottom),
        )
    for k in range(leaves_n // 2):
        pair = folded(update[:fold, k * wide : (k + 1) * wide], update[fold:, k * wide : (k + 1) * wide])
        for side in range(2):
            u3s[2 * k + side] = pair[side].astype(jnp.bfloat16)
    u3_src = lambda target: u3s.at[target]
    u3_dst = lambda sender, d: u3r.at[d - 1]
    swap_start("u3", 3, u3_src, u3_dst)
    local_copies["b3"].wait()
    swap_wait(*fixed[CHUNKS + 3])
    own_b = b3[...].astype(jnp.float32)
    sides = folded(own_b[:4].reshape(fold, wide), own_b[4:].reshape(fold, wide))
    own_b = jnp.where(place[3] % 2 == 0, sides[0], sides[1])
    swap_wait("u3", 3, u3_src, u3_dst)
    total = u3s[place[3]].astype(jnp.float32)
    for d in range(leaves_n - 1):
        total = total + u3r[d].astype(jnp.float32)
    reduced = (own_b - total).astype(jnp.bfloat16)
    for s in range(4):
        z3[s, row] = reduced[s * heights[3] : (s + 1) * heights[3]]
    gather_start("z3", z3_slot)
    local_copies["d3"].wait()
    swap_wait(*fixed[CHUNKS + 4])
    for step in range(1, rows_n):
        gather_step("z3", z3_slot, step)
    known = z3[...].reshape(half, wide)
    left = dot32(d3[:, :, :half].reshape(height, half), known)
    right = dot32(d3[:, :, half:].reshape(height, half), known)
    solved = left + pltpu.roll(right, wide // 2, 1)
    low_all = lax.broadcasted_iota(jnp.int32, (height, wide), 1) < wide // 2
    solved = jnp.where(low_all, solved, pltpu.roll(solved, wide // 2, 1))
    y3s[...] = solved.astype(jnp.bfloat16).reshape(leaves_n, heights[3], wide)
    y3_src = lambda target: y3s.at[target]
    y3_dst = lambda sender, d: y3r.at[sender]
    swap_start("y3", 3, y3_src, y3_dst)
    y3r[place[3]] = y3s[place[3]]
    swap_wait("y3", 3, y3_src, y3_dst)
    low_out = lax.broadcasted_iota(jnp.int32, (heights[3], wide), 1) < wide // 2
    for k in range(leaves_n // 2):
        out[level_rows(3), pl.ds(k * wide, wide)] = jnp.where(
            low_out, y3r[2 * k].astype(jnp.float32), y3r[2 * k + 1].astype(jnp.float32))

    for can, make in pending:
        if can is None:
            make().wait_send()
        else:
            @pl.when(can)
            def _(make=make):
                make().wait_send()


def fits(rows_n, leaves_n, rhs, inv_diag, off_diag):
    whole = inv_diag.shape[3]
    right_n = rhs.shape[3]
    return (
        leaves_n == 2**TREE_LEVELS
        and rows_n > 1
        and whole % (leaves_n * rows_n * ROW_TILE) == 0
        and whole % (4 * LANES) == 0
        and right_n == 4 * LANES
    )


def tree_shards(rhs, inv_diag, off_diag, pair_mask):
    rows_n = lax.axis_size("row")
    leaves_n = lax.axis_size("leaf")
    whole = inv_diag.shape[3]
    right_n = rhs.shape[3]
    height = off_diag.shape[2]
    chunk = right_n // CHUNKS
    hs = [height // 2**m for m in range(TREE_LEVELS + 1)]
    bf16, f32 = jnp.bfloat16, jnp.float32
    vm = pltpu.VMEM
    scratch = [
        vm((height, whole), bf16),
        vm((2, hs[1], whole), bf16), vm((4, hs[2], whole), bf16), vm((8, hs[3], whole), bf16),
        vm((height, whole), bf16), vm((height, whole + whole // 2), bf16),
        vm((height, whole + whole // 2 + whole // 4), bf16),
        vm((CHUNKS, 2, hs[1], LANES), bf16), vm((4, hs[2], LANES), bf16), vm((8, hs[3], LANES), bf16),
        vm((CHUNKS, rows_n, height, chunk), bf16),
        vm((CHUNKS, 2, rows_n, hs[1], LANES), bf16),
        vm((4, rows_n, hs[2], LANES), bf16),
        vm((4, rows_n, hs[3], LANES), bf16),
        vm((CHUNKS, rows_n, height, chunk), bf16),
        vm((CHUNKS, rows_n, hs[1], chunk), bf16),
        vm((rows_n, hs[2], right_n), bf16),
        vm((CHUNKS, height, chunk), f32), vm((height, right_n), f32), vm((height, right_n), f32),
        vm((CHUNKS, height, chunk), bf16), vm((height, right_n), bf16),
        vm((leaves_n, height // 2, LANES), bf16),
        vm((CHUNKS, 1, height, LANES), bf16), vm((3, height, LANES), bf16),
        vm((leaves_n - 1, height // 2, LANES), bf16),
        vm((CHUNKS, 2, hs[1], LANES), bf16), vm((4, hs[2], LANES), bf16),
        vm((leaves_n, hs[3], LANES), bf16), vm((leaves_n, hs[3], LANES), bf16),
        pltpu.SemaphoreType.DMA((len(GATHERS), rows_n)),
        pltpu.SemaphoreType.DMA((len(GATHERS), rows_n)),
        pltpu.SemaphoreType.DMA((len(GATHERS), rows_n)),
        pltpu.SemaphoreType.DMA((len(SWAPS), leaves_n)),
        pltpu.SemaphoreType.DMA((len(SWAPS), leaves_n)),
        pltpu.SemaphoreType.DMA((len(LOCALS),)),
    ]
    pack = rhs.shape[2]
    flops = 2 * right_n * (pack * whole + height * off_diag.shape[3])
    moved = 2 * (pack * whole + height * off_diag.shape[3] + 3 * pack * right_n)
    solved = pl.pallas_call(
        functools.partial(tree_kernel, rows_n, leaves_n),
        out_shape=jax.ShapeDtypeStruct((pack, right_n), f32),
        in_specs=[pl.BlockSpec(memory_space=pltpu.SMEM)] + [pl.BlockSpec(memory_space=pl.ANY)] * 3,
        out_specs=pl.BlockSpec(memory_space=pltpu.VMEM),
        scratch_shapes=scratch,
        compiler_params=pltpu.CompilerParams(
            collective_id=0, has_side_effects=True, vmem_limit_bytes=48 * 2**20),
        cost_estimate=pl.CostEstimate(flops=flops, bytes_accessed=moved, transcendentals=0),
    )(pair_mask[0, 0], rhs[0, 0], inv_diag[0, 0], off_diag[0, 0])
    return solved[None, None]


def solution(mesh):
    in_specs = (
        P("leaf", "row", None, None),
        P("leaf", "row", None, None),
        P("leaf", "row", None, None),
        P("leaf", "row", None),
    )
    out_specs = P("leaf", "row", None, None)

    def run(rhs, inv_diag, off_diag, pair_mask):
        fit = fits(mesh.shape["row"], mesh.shape["leaf"], rhs, inv_diag, off_diag)
        body = tree_shards if fit else shards
        return jax.shard_map(body, mesh=mesh, in_specs=in_specs, out_specs=out_specs, check_vma=False)(
            rhs, inv_diag, off_diag, pair_mask
        )

    return run
```

```python
import functools

import jax
import jax.numpy as jnp
from jax import lax
from jax.experimental import pallas as pl
from jax.experimental.pallas import tpu as pltpu
from jax.sharding import PartitionSpec as P

LANES = 128
ROW_TILE = 16
CHUNKS = 2
TREE_LEVELS = 3
MESH = pl.DeviceIdType.MESH


def partner_2(block, axis, bit):
    count = lax.axis_size(axis)
    route = []
    for low in range(count):
        high = low | 1 << bit
        if high != low and high < count:
            route += [(low, high), (high, low)]
    return lax.ppermute(block, axis, route)


def column_start(ancestor, width_all):
    offset = 0
    for higher in range(1, ancestor):
        for within in range(higher):
            offset += width_all // 2**within
    return offset


def shards(rhs, inv_diag, off_diag, pair_mask):
    rows_n = lax.axis_size("row")
    leaves = lax.axis_size("leaf")
    levels_n = leaves.bit_length() - 1
    leaf_index = lax.axis_index("leaf")
    width_all = inv_diag.shape[3]
    right_all = rhs[0, 0]
    inverse_all = inv_diag[0, 0]
    panels = off_diag[0, 0]
    live_pairs = pair_mask[0, 0].astype(jnp.bfloat16)
    known_parts = []
    outputs = []
    offset = 0
    for ancestor in range(levels_n + 1):
        height = width_all // (2**ancestor * rows_n)
        own_rhs = right_all[offset : offset + height]
        own_inv = inverse_all[offset : offset + height]
        offset += height
        if ancestor > 0:
            stacked = jnp.concatenate(
                [
                    known_parts[source] * live_pairs[ancestor * (ancestor - 1) // 2 + source]
                    for source in range(ancestor)
                ],
                axis=0,
            )
            first_col = column_start(ancestor, width_all)
            span_cols = stacked.shape[0]
            update = jnp.dot(
                panels[:, first_col : first_col + span_cols],
                stacked,
                preferred_element_type=jnp.float32,
            )
        if ancestor > 0:
            current = update
            for bit_pos in reversed(range(ancestor)):
                half_rows = current.shape[0] // 2
                upper_half = leaf_index // 2**bit_pos % 2 == 1
                kept_rows = jnp.where(upper_half, current[half_rows:], current[:half_rows])
                sent_rows = jnp.where(upper_half, current[:half_rows], current[half_rows:])
                current = kept_rows + partner_2(
                    sent_rows.astype(jnp.bfloat16), "leaf", bit_pos
                ).astype(sent_rows.dtype)
            reduced = (own_rhs.astype(jnp.float32) - current).astype(jnp.bfloat16)
        else:
            reduced = own_rhs
        gathered = lax.all_gather(reduced, "row", axis=0, tiled=True)
        for bit_pos in range(ancestor):
            partner = partner_2(gathered, "leaf", bit_pos)
            upper_half = leaf_index // 2**bit_pos % 2 == 1
            gathered = jnp.where(
                upper_half,
                jnp.concatenate([partner, gathered], axis=0),
                jnp.concatenate([gathered, partner], axis=0),
            )
        solved = jnp.dot(own_inv, gathered, preferred_element_type=jnp.float32)
        outputs.append(solved)
        if ancestor < levels_n:
            leaf_part = lax.all_gather(solved.astype(jnp.bfloat16), "row", axis=0, tiled=True)
            known_parts.append(leaf_part)
    return jnp.concatenate(outputs, axis=0)[None, None]


def dot32(left, right):
    return jnp.dot(left, right, preferred_element_type=jnp.float32)


GATHERS = ["z0a", "z0b", "y0a", "y0b", "z1a", "z1b", "y1a", "y1b", "z2", "z3"]
SWAPS = ["b1a", "b1b", "b2", "b3", "d1", "d2", "d3", "u1a", "u1b", "u2", "u3", "y1a", "y1b", "y3"]
LOCALS = ["z0a", "z0b", "d0", "p1", "p2", "p3", "d1", "d2", "d3", "b1a", "b1b", "b2", "b3"]


def tree_kernel(
    rows_n, leaves_n,
    mask, rhs, inv, pan, out,
    d0, d1, d2, d3, p1, p2, p3, b1, b2, b3,
    z0, z1, z2, z3, y0, y1, y2,
    u1, u2, u3, u1s, u2s, u3s, u1r, u2r, u3r, y1s, y2s, y3s, y3r,
    up_sem, down_sem, land_sem, swap_send, swap_recv, local_sem, spread_send, spread_recv,
):
    leaf = lax.axis_index("leaf")
    row = lax.axis_index("row")
    height = p1.shape[0]
    right_n = u2.shape[1]
    chunk = right_n // CHUNKS
    heights = [height // 2**m for m in range(TREE_LEVELS + 1)]
    starts = [sum(heights[:m]) for m in range(TREE_LEVELS + 1)]
    wide = LANES
    suffix = "ab"
    pending = []
    place = [leaf % 2**m for m in range(TREE_LEVELS + 1)]
    own_chunk = leaf % 2

    def block_of(position):
        return 2 * (position % 2) + position // 2 % 2

    def at_cols(index):
        return pl.ds(pl.multiple_of(index * wide, wide), wide)

    def level_rows(m):
        return pl.ds(starts[m], heights[m])

    barrier = pltpu.get_barrier_semaphore()

    for e in range(1, rows_n):
        for d in range(4):
            pl.semaphore_signal(
                barrier, inc=1, device_id=(leaf - place[2] + (place[2] + d) % 4, (row + e) % rows_n),
                device_id_type=MESH)
    for d in range(1, leaves_n):
        pl.semaphore_signal(barrier, inc=1, device_id=((leaf + d) % leaves_n, row), device_id_type=MESH)

    def local(name, src, dst):
        return pltpu.make_async_copy(src, dst, local_sem.at[LOCALS.index(name)])

    local_copies = {}
    for c in range(CHUNKS):
        local_copies["z0" + suffix[c]] = local(
            "z0" + suffix[c], rhs.at[pl.ds(0, height), pl.ds(c * chunk, chunk)], z0.at[c, row])
    local_copies["d0"] = local("d0", inv.at[pl.ds(0, height)], d0)
    for m, held in ((1, p1), (2, p2), (3, p3)):
        local_copies["p%d" % m] = local(
            "p%d" % m, pan.at[:, pl.ds(column_start(m, d0.shape[1]), held.shape[1])], held)
    for m, held in ((1, d1), (2, d2), (3, d3)):
        local_copies["d%d" % m] = local("d%d" % m, inv.at[level_rows(m)], held.at[place[m]])
    for c in range(CHUNKS):
        local_copies["b1" + suffix[c]] = local(
            "b1" + suffix[c], rhs.at[level_rows(1), at_cols(2 * c + place[1])], b1.at[c, place[1]])
    local_copies["b2"] = local("b2", rhs.at[level_rows(2), at_cols(block_of(place[2]))], b2.at[place[2]])
    local_copies["b3"] = local("b3", rhs.at[level_rows(3), at_cols(block_of(place[3]))], b3.at[place[3]])
    for name in LOCALS:
        local_copies[name].start()

    pl.semaphore_wait(barrier, 4 * (rows_n - 1) + leaves_n - 1)

    def begin(can, make):
        if can is None:
            make().start()
        else:
            @pl.when(can)
            def _():
                make().start()
        pending.append((can, make))

    def hop(name, src, dst, step, source, way):
        k = GATHERS.index(name)
        sem = up_sem if way > 0 else down_sem
        return pltpu.make_async_remote_copy(
            src_ref=src, dst_ref=dst, send_sem=sem.at[k, step], recv_sem=land_sem.at[k, source],
            device_id=(leaf, row + way), device_id_type=MESH)

    def gather_start(name, slot, src=None):
        for way, can in ((1, row < rows_n - 1), (-1, row > 0)):
            def make(way=way):
                return hop(name, slot(row) if src is None else src, slot(row), 0, row, way)

            @pl.when(can)
            def _(make=make):
                make().start()

            pending.append((can, make))

    def gather_step(name, slot, step):
        for way, can in ((1, row < rows_n - 1), (-1, row > 0)):
            source = row - way * step
            there = (source >= 0) if way > 0 else (source < rows_n)

            def make(way=way, source=source):
                return hop(name, slot(source), slot(source), step, source, way)

            @pl.when(there)
            def _(make=make):
                make().wait_recv()

            if step < rows_n - 1:
                both = jnp.logical_and(there, can)

                @pl.when(both)
                def _(make=make):
                    make().start()

                pending.append((both, make))

    def direct(name, slot, e):
        k = GATHERS.index(name)
        return pltpu.make_async_remote_copy(
            src_ref=slot(row), dst_ref=slot(row), send_sem=up_sem.at[k, e], recv_sem=land_sem.at[k, e],
            device_id=(leaf, (row + e) % rows_n), device_id_type=MESH)

    def direct_start(name, slot, can):
        for e in range(1, rows_n):
            begin(can, lambda e=e: direct(name, slot, e))

    def direct_wait(name, slot):
        k = GATHERS.index(name)
        for e in range(1, rows_n):
            there = slot((row - e + rows_n) % rows_n)
            pltpu.make_async_remote_copy(
                src_ref=there, dst_ref=there, send_sem=up_sem.at[k, e], recv_sem=land_sem.at[k, e],
                device_id=(leaf, (row + e) % rows_n), device_id_type=MESH).wait_recv()

    def peer(m, d):
        size = 2**m
        return leaf - place[m] + (place[m] + d) % size

    def swap(name, m, d, src, dst):
        k = SWAPS.index(name)
        return pltpu.make_async_remote_copy(
            src_ref=src, dst_ref=dst, send_sem=swap_send.at[k, d], recv_sem=swap_recv.at[k, d],
            device_id=(peer(m, d), row), device_id_type=MESH)

    def swap_start(name, m, src, dst, when=None):
        size = 2**m
        for d in range(1, size):
            target = (place[m] + d) % size

            def make(d=d, target=target):
                return swap(name, m, d, src(target), dst(place[m], d))

            begin(None if when is None else when(target), make)

    def swap_wait(name, m, src, dst):
        size = 2**m
        for d in range(1, size):
            sender = (place[m] - d + size) % size
            swap(name, m, d, src(place[m]), dst(sender, d)).wait_recv()

    def z0_slot(c):
        return lambda q: z0.at[c, q]

    def y0_slot(c):
        return lambda q: y0.at[c, q]

    def z1_slot(c):
        return lambda q: z1.at[c, :, q]

    def y1_slot(c):
        return lambda q: y1.at[c, q]

    def z2_slot(q):
        return z2.at[:, q]

    def z3_slot(q):
        return z3.at[:, q]

    for c in range(CHUNKS):
        gather_start("z0" + suffix[c], z0_slot(c), rhs.at[pl.ds(0, height), pl.ds(c * chunk, chunk)])

    fixed = []
    for c in range(CHUNKS):
        fixed.append((
            "b1" + suffix[c], 1,
            lambda target, c=c: rhs.at[level_rows(1), at_cols(2 * c + target)],
            lambda sender, d, c=c: b1.at[c, sender]))
    fixed.append(("d1", 1, lambda target: inv.at[level_rows(1)], lambda sender, d: d1.at[sender]))
    fixed.append(("b2", 2, lambda target: rhs.at[level_rows(2), at_cols(block_of(target))], lambda sender, d: b2.at[sender]))
    fixed.append(("d2", 2, lambda target: inv.at[level_rows(2)], lambda sender, d: d2.at[sender]))
    fixed.append(("b3", 3, lambda target: rhs.at[level_rows(3), at_cols(block_of(target))], lambda sender, d: b3.at[sender]))
    fixed.append(("d3", 3, lambda target: inv.at[level_rows(3)], lambda sender, d: d3.at[sender]))
    for entry in fixed:
        swap_start(*entry)

    def live(pair):
        return mask[pair].astype(jnp.float32)

    def cols_of(c):
        return pl.ds(c * chunk, chunk)

    for step in range(1, rows_n - 1):
        for c in range(CHUNKS):
            gather_step("z0" + suffix[c], z0_slot(c), step)
    local_copies["d0"].wait()
    whole = d0.shape[1]
    for c in range(CHUNKS):
        local_copies["z0" + suffix[c]].wait()
        gather_step("z0" + suffix[c], z0_slot(c), rows_n - 1)
        solved = dot32(d0[...], z0[c].reshape(whole, chunk))
        y0[c, row] = solved.astype(jnp.bfloat16)
        gather_start("y0" + suffix[c], y0_slot(c))
        out[pl.ds(0, height), cols_of(c)] = solved
    for step in range(1, rows_n - 1):
        for c in range(CHUNKS):
            gather_step("y0" + suffix[c], y0_slot(c), step)
    for name in ("p1", "p2", "p3"):
        local_copies[name].wait()

    half = whole // 2
    u1_src = [lambda target, c=c: u1s.at[c, :, at_cols(target)] for c in range(CHUNKS)]
    u1_dst = [lambda sender, d, c=c: u1r.at[c, d - 1] for c in range(CHUNKS)]
    y1_src = [lambda target, c=c: y1s.at[c, target] for c in range(CHUNKS)]
    y1_dst = [lambda sender, d, c=c: y1.at[c, row, :, at_cols(sender)] for c in range(CHUNKS)]

    def update_1(c):
        gather_step("y0" + suffix[c], y0_slot(c), rows_n - 1)
        update = dot32(p1[...], y0[c].reshape(whole, chunk)) * live(0)
        u1[c] = update
        u1s[c] = update.astype(jnp.bfloat16)
        swap_start("u1" + suffix[c], 1, u1_src[c], u1_dst[c])

    def reduce_1(c):
        local_copies["b1" + suffix[c]].wait()
        swap_wait(*fixed[c])
        swap_wait("u1" + suffix[c], 1, u1_src[c], u1_dst[c])
        total = u1[c, :, at_cols(place[1])] + u1r[c, 0].astype(jnp.float32)
        reduced = (b1[c].reshape(height, wide).astype(jnp.float32) - total).astype(jnp.bfloat16)
        for s in range(2):
            z1[c, s, row] = reduced[s * heights[1] : (s + 1) * heights[1]]
        gather_start("z1" + suffix[c], z1_slot(c))

    def early_2(c):
        u2[:, cols_of(c)] = dot32(p2[:, :whole], y0[c].reshape(whole, chunk)) * live(1)

    def early_3(c):
        u3[:, cols_of(c)] = dot32(p3[:, :whole], y0[c].reshape(whole, chunk)) * live(3)

    def solve_1(c):
        gather_step("z1" + suffix[c], z1_slot(c), rows_n - 1)
        solved = dot32(d1[...].reshape(height, whole), z1[c].reshape(whole, wide)).astype(jnp.bfloat16)
        y1s[c] = solved.reshape(2, heights[1], wide)
        swap_start("y1" + suffix[c], 1, y1_src[c], y1_dst[c])
        y1[c, row, :, at_cols(place[1])] = y1s[c, place[1]]

    def spread_1(c):
        swap_wait("y1" + suffix[c], 1, y1_src[c], y1_dst[c])
        gather_start("y1" + suffix[c], y1_slot(c))

    u2_src = lambda target: u2s.at[:, at_cols(block_of(target))]
    u2_dst = lambda sender, d: u2r.at[d - 1]

    def update_2(c):
        gather_step("y1" + suffix[c], y1_slot(c), rows_n - 1)
        update = u2[:, cols_of(c)] + dot32(p2[:, whole:], y1[c].reshape(half, chunk)) * live(2)
        u2[:, cols_of(c)] = update
        u2s[:, cols_of(c)] = update.astype(jnp.bfloat16)
        swap_start("u2", 2, u2_src, u2_dst, lambda target: target % 2 == c)

    def later_3(c):
        u3[:, cols_of(c)] += dot32(p3[:, whole : whole + half], y1[c].reshape(half, chunk)) * live(4)

    def reduce_2(c):
        @pl.when(own_chunk == c)
        def _():
            swap_wait("u2", 2, u2_src, u2_dst)
            total = u2[:, at_cols(block_of(place[2]))]
            for d in range(3):
                total = total + u2r[d].astype(jnp.float32)
            reduced = (b2[...].reshape(height, wide).astype(jnp.float32) - total).astype(jnp.bfloat16)
            for s in range(4):
                z2[s, row] = reduced[s * heights[2] : (s + 1) * heights[2]]

        direct_start("z2", z2_slot, own_chunk == c)

    def spread(d, e, position):
        here = leaf - place[2] + (place[2] + d) % 4
        dst = y2.at[(row if position is None else (row - e + rows_n) % rows_n), :,
                    at_cols(block_of(place[2] if position is None else position))]
        src = y2s.at[(place[2] + d) % 4]
        return pltpu.make_async_remote_copy(
            src_ref=src, dst_ref=dst, send_sem=spread_send.at[d, e], recv_sem=spread_recv.at[d, e],
            device_id=(here, (row + e) % rows_n), device_id_type=MESH)

    others = [(d, e) for e in reversed(range(rows_n)) for d in range(4) if d or e]

    def solve_2(c):
        @pl.when(own_chunk == c)
        def _():
            direct_wait("z2", z2_slot)
            solved = dot32(d2[...].reshape(height, whole), z2[...].reshape(whole, wide)).astype(jnp.bfloat16)
            y2s[...] = solved.reshape(4, heights[2], wide)

        for d, e in others:
            begin(own_chunk == c, lambda d=d, e=e: spread(d, e, None))

        @pl.when(own_chunk == c)
        def _():
            y2[row, :, at_cols(block_of(place[2]))] = y2s[place[2]]

    fold = height // 2
    low = lax.broadcasted_iota(jnp.int32, (fold, wide), 1) < wide // 2

    def folded(top, bottom):
        return (
            jnp.where(low, top, pltpu.roll(bottom, wide // 2, 1)),
            jnp.where(low, pltpu.roll(top, wide // 2, 1), bottom),
        )

    u3_src = lambda target: u3s.at[target]
    u3_dst = lambda sender, d: u3r.at[d - 1]

    def update_3(c):
        for d, e in others:
            sender = (place[2] - d + 4) % 4

            @pl.when(sender % 2 == c)
            def _(d=d, e=e, sender=sender):
                spread(d, e, sender).wait_recv()

        known = y2[:, :, c * chunk : (c + 1) * chunk].reshape(whole // 4, chunk)
        update = u3[:, cols_of(c)] + dot32(p3[:, whole + half :], known) * live(5)
        for k in range(2):
            block = update[:, k * wide : (k + 1) * wide]
            sides = folded(block[:fold], block[fold:])
            for side in range(2):
                u3s[4 * side + 2 * k + c] = sides[side].astype(jnp.bfloat16)
        swap_start("u3", 3, u3_src, u3_dst, lambda target: target % 2 == c)

    def reduce_3(c):
        @pl.when(own_chunk == c)
        def _():
            own_b = b3[...].astype(jnp.float32)
            sides = folded(own_b[:4].reshape(fold, wide), own_b[4:].reshape(fold, wide))
            own_b = jnp.where(place[3] < leaves_n // 2, sides[0], sides[1])
            swap_wait("u3", 3, u3_src, u3_dst)
            total = u3s[place[3]].astype(jnp.float32)
            for d in range(leaves_n - 1):
                total = total + u3r[d].astype(jnp.float32)
            reduced = (own_b - total).astype(jnp.bfloat16)
            for s in range(4):
                z3[s, row] = reduced[s * heights[3] : (s + 1) * heights[3]]

        direct_start("z3", z3_slot, own_chunk == c)

    y3_src = lambda target: y3s.at[target]
    y3_dst = lambda sender, d: y3r.at[sender]

    def solve_3():
        direct_wait("z3", z3_slot)
        known = z3[...].reshape(half, wide)
        left = dot32(d3[:, :, :half].reshape(height, half), known)
        right = dot32(d3[:, :, half:].reshape(height, half), known)
        solved = left + pltpu.roll(right, wide // 2, 1)
        low_all = lax.broadcasted_iota(jnp.int32, (height, wide), 1) < wide // 2
        solved = jnp.where(low_all, solved, pltpu.roll(solved, wide // 2, 1))
        y3s[...] = solved.astype(jnp.bfloat16).reshape(leaves_n, heights[3], wide)
        swap_start("y3", 3, y3_src, y3_dst)
        y3r[place[3]] = y3s[place[3]]

    update_1(0)
    early_2(0)
    reduce_1(0)
    early_3(0)
    update_1(1)
    gather_step("z1a", z1_slot(0), 1)
    reduce_1(1)
    early_2(1)
    early_3(1)
    for step in range(2, rows_n - 1):
        gather_step("z1a", z1_slot(0), step)
        gather_step("z1b", z1_slot(1), step - 1)
    local_copies["d1"].wait()
    swap_wait(*fixed[CHUNKS])
    solve_1(0)
    gather_step("z1b", z1_slot(1), rows_n - 2)
    spread_1(0)
    solve_1(1)
    gather_step("y1a", y1_slot(0), 1)
    spread_1(1)
    for step in range(2, rows_n - 1):
        gather_step("y1a", y1_slot(0), step)
        gather_step("y1b", y1_slot(1), step - 1)
    local_copies["b2"].wait()
    swap_wait(*fixed[CHUNKS + 1])
    update_2(0)
    gather_step("y1b", y1_slot(1), rows_n - 2)
    later_3(0)
    reduce_2(0)
    update_2(1)
    local_copies["d2"].wait()
    swap_wait(*fixed[CHUNKS + 2])
    reduce_2(1)
    later_3(1)
    for c in range(CHUNKS):
        out[level_rows(1), cols_of(c)] = y1[c, row].astype(jnp.float32)
    local_copies["b3"].wait()
    swap_wait(*fixed[CHUNKS + 3])
    local_copies["d3"].wait()
    swap_wait(*fixed[CHUNKS + 4])
    solve_2(0)
    solve_2(1)
    update_3(0)
    reduce_3(0)
    update_3(1)
    reduce_3(1)
    out[level_rows(2), :] = y2[row].astype(jnp.float32)
    solve_3()
    swap_wait("y3", 3, y3_src, y3_dst)
    low_out = lax.broadcasted_iota(jnp.int32, (heights[3], wide), 1) < wide // 2
    for k in range(leaves_n // 2):
        first = 2 * (k % 2) + k // 2
        out[level_rows(3), pl.ds(k * wide, wide)] = jnp.where(
            low_out, y3r[first].astype(jnp.float32), y3r[first + leaves_n // 2].astype(jnp.float32))

    for can, make in pending:
        if can is None:
            make().wait_send()
        else:
            @pl.when(can)
            def _(make=make):
                make().wait_send()


def fits(rows_n, leaves_n, rhs, inv_diag, off_diag):
    whole = inv_diag.shape[3]
    right_n = rhs.shape[3]
    return (
        leaves_n == 2**TREE_LEVELS
        and rows_n > 2
        and whole % (leaves_n * rows_n * ROW_TILE) == 0
        and whole % (4 * LANES) == 0
        and right_n == 4 * LANES
    )


def tree_shards(rhs, inv_diag, off_diag, pair_mask):
    rows_n = lax.axis_size("row")
    leaves_n = lax.axis_size("leaf")
    whole = inv_diag.shape[3]
    right_n = rhs.shape[3]
    height = off_diag.shape[2]
    chunk = right_n // CHUNKS
    hs = [height // 2**m for m in range(TREE_LEVELS + 1)]
    bf16, f32 = jnp.bfloat16, jnp.float32
    vm = pltpu.VMEM
    scratch = [
        vm((height, whole), bf16),
        vm((2, hs[1], whole), bf16), vm((4, hs[2], whole), bf16), vm((8, hs[3], whole), bf16),
        vm((height, whole), bf16), vm((height, whole + whole // 2), bf16),
        vm((height, whole + whole // 2 + whole // 4), bf16),
        vm((CHUNKS, 2, hs[1], LANES), bf16), vm((4, hs[2], LANES), bf16), vm((8, hs[3], LANES), bf16),
        vm((CHUNKS, rows_n, height, chunk), bf16),
        vm((CHUNKS, 2, rows_n, hs[1], LANES), bf16),
        vm((4, rows_n, hs[2], LANES), bf16),
        vm((4, rows_n, hs[3], LANES), bf16),
        vm((CHUNKS, rows_n, height, chunk), bf16),
        vm((CHUNKS, rows_n, hs[1], chunk), bf16),
        vm((rows_n, hs[2], right_n), bf16),
        vm((CHUNKS, height, chunk), f32), vm((height, right_n), f32), vm((height, right_n), f32),
        vm((CHUNKS, height, chunk), bf16), vm((height, right_n), bf16),
        vm((leaves_n, height // 2, LANES), bf16),
        vm((CHUNKS, 1, height, LANES), bf16), vm((3, height, LANES), bf16),
        vm((leaves_n - 1, height // 2, LANES), bf16),
        vm((CHUNKS, 2, hs[1], LANES), bf16), vm((4, hs[2], LANES), bf16),
        vm((leaves_n, hs[3], LANES), bf16), vm((leaves_n, hs[3], LANES), bf16),
        pltpu.SemaphoreType.DMA((len(GATHERS), rows_n)),
        pltpu.SemaphoreType.DMA((len(GATHERS), rows_n)),
        pltpu.SemaphoreType.DMA((len(GATHERS), rows_n)),
        pltpu.SemaphoreType.DMA((len(SWAPS), leaves_n)),
        pltpu.SemaphoreType.DMA((len(SWAPS), leaves_n)),
        pltpu.SemaphoreType.DMA((len(LOCALS),)),
        pltpu.SemaphoreType.DMA((4, rows_n)),
        pltpu.SemaphoreType.DMA((4, rows_n)),
    ]
    pack = rhs.shape[2]
    flops = 2 * right_n * (pack * whole + height * off_diag.shape[3])
    moved = 2 * (pack * whole + height * off_diag.shape[3] + 3 * pack * right_n)
    solved = pl.pallas_call(
        functools.partial(tree_kernel, rows_n, leaves_n),
        out_shape=jax.ShapeDtypeStruct((pack, right_n), f32),
        in_specs=[pl.BlockSpec(memory_space=pltpu.SMEM)] + [pl.BlockSpec(memory_space=pltpu.HBM)] * 3,
        out_specs=pl.BlockSpec(memory_space=pltpu.VMEM),
        scratch_shapes=scratch,
        compiler_params=pltpu.CompilerParams(
            collective_id=0, has_side_effects=True, vmem_limit_bytes=48 * 2**20),
        cost_estimate=pl.CostEstimate(flops=flops, bytes_accessed=moved, transcendentals=0),
    )(pair_mask[0, 0], rhs[0, 0], inv_diag[0, 0], off_diag[0, 0])
    return solved[None, None]


def solution(mesh):
    in_specs = (
        P("leaf", "row", None, None),
        P("leaf", "row", None, None),
        P("leaf", "row", None, None),
        P("leaf", "row", None),
    )
    out_specs = P("leaf", "row", None, None)

    def run(rhs, inv_diag, off_diag, pair_mask):
        fit = fits(mesh.shape["row"], mesh.shape["leaf"], rhs, inv_diag, off_diag)
        body = tree_shards if fit else shards
        return jax.shard_map(body, mesh=mesh, in_specs=in_specs, out_specs=out_specs, check_vma=False)(
            rhs, inv_diag, off_diag, pair_mask
        )

    return run
```

```python
import functools

import jax
import jax.numpy as jnp
from jax import lax
from jax.experimental import pallas as pl
from jax.experimental.pallas import tpu as pltpu
from jax.sharding import PartitionSpec as P

LANES = 128
ROW_TILE = 16
CHUNKS = 2
TREE_LEVELS = 3
MESH = pl.DeviceIdType.MESH


def partner_2(block, axis, bit):
    count = lax.axis_size(axis)
    route = []
    for low in range(count):
        high = low | 1 << bit
        if high != low and high < count:
            route += [(low, high), (high, low)]
    return lax.ppermute(block, axis, route)


def column_start(ancestor, width_all):
    offset = 0
    for higher in range(1, ancestor):
        for within in range(higher):
            offset += width_all // 2**within
    return offset


def shards(rhs, inv_diag, off_diag, pair_mask):
    rows_n = lax.axis_size("row")
    leaves = lax.axis_size("leaf")
    levels_n = leaves.bit_length() - 1
    leaf_index = lax.axis_index("leaf")
    width_all = inv_diag.shape[3]
    right_all = rhs[0, 0]
    inverse_all = inv_diag[0, 0]
    panels = off_diag[0, 0]
    live_pairs = pair_mask[0, 0].astype(jnp.bfloat16)
    known_parts = []
    outputs = []
    offset = 0
    for ancestor in range(levels_n + 1):
        height = width_all // (2**ancestor * rows_n)
        own_rhs = right_all[offset : offset + height]
        own_inv = inverse_all[offset : offset + height]
        offset += height
        if ancestor > 0:
            stacked = jnp.concatenate(
                [
                    known_parts[source] * live_pairs[ancestor * (ancestor - 1) // 2 + source]
                    for source in range(ancestor)
                ],
                axis=0,
            )
            first_col = column_start(ancestor, width_all)
            span_cols = stacked.shape[0]
            update = jnp.dot(
                panels[:, first_col : first_col + span_cols],
                stacked,
                preferred_element_type=jnp.float32,
            )
        if ancestor > 0:
            current = update
            for bit_pos in reversed(range(ancestor)):
                half_rows = current.shape[0] // 2
                upper_half = leaf_index // 2**bit_pos % 2 == 1
                kept_rows = jnp.where(upper_half, current[half_rows:], current[:half_rows])
                sent_rows = jnp.where(upper_half, current[:half_rows], current[half_rows:])
                current = kept_rows + partner_2(
                    sent_rows.astype(jnp.bfloat16), "leaf", bit_pos
                ).astype(sent_rows.dtype)
            reduced = (own_rhs.astype(jnp.float32) - current).astype(jnp.bfloat16)
        else:
            reduced = own_rhs
        gathered = lax.all_gather(reduced, "row", axis=0, tiled=True)
        for bit_pos in range(ancestor):
            partner = partner_2(gathered, "leaf", bit_pos)
            upper_half = leaf_index // 2**bit_pos % 2 == 1
            gathered = jnp.where(
                upper_half,
                jnp.concatenate([partner, gathered], axis=0),
                jnp.concatenate([gathered, partner], axis=0),
            )
        solved = jnp.dot(own_inv, gathered, preferred_element_type=jnp.float32)
        outputs.append(solved)
        if ancestor < levels_n:
            leaf_part = lax.all_gather(solved.astype(jnp.bfloat16), "row", axis=0, tiled=True)
            known_parts.append(leaf_part)
    return jnp.concatenate(outputs, axis=0)[None, None]


def dot32(left, right):
    return jnp.dot(left, right, preferred_element_type=jnp.float32)


GATHERS = ["z0a", "z0b", "y0a", "y0b", "z1a", "z1b", "y1a", "y1b", "z2", "z3"]
SWAPS = ["b1a", "b1b", "b2", "b3", "d1", "d2", "d3", "u1a", "u1b", "u2", "u3", "y1a", "y1b", "y3"]
LOCALS = ["z0a", "z0b", "d0", "p1", "p2", "p3", "d1", "d2", "d3", "b1a", "b1b", "b2", "b3"]


def tree_kernel(
    rows_n, leaves_n,
    mask, rhs, inv, pan, out,
    d0, d1, d2, d3, p1, p2, p3, b1, b2, b3,
    z0, z1, z2, z3, y0, y1, y2,
    u1, u2, u3, u1s, u2s, u3s, u1r, u2r, u3r, y1s, y2s, y3s, y3r,
    up_sem, down_sem, land_sem, swap_send, swap_recv, local_sem, spread_send, spread_recv,
):
    leaf = lax.axis_index("leaf")
    row = lax.axis_index("row")
    height = p1.shape[0]
    right_n = u2.shape[1]
    chunk = right_n // CHUNKS
    heights = [height // 2**m for m in range(TREE_LEVELS + 1)]
    starts = [sum(heights[:m]) for m in range(TREE_LEVELS + 1)]
    wide = LANES
    suffix = "ab"
    pending = []
    place = [leaf % 2**m for m in range(TREE_LEVELS + 1)]
    own_chunk = leaf % 2

    def block_of(position):
        return 2 * (position % 2) + position // 2 % 2

    def at_cols(index):
        return pl.ds(pl.multiple_of(index * wide, wide), wide)

    def level_rows(m):
        return pl.ds(starts[m], heights[m])

    barrier = pltpu.get_barrier_semaphore()

    for e in range(1, rows_n):
        for d in range(4):
            pl.semaphore_signal(
                barrier, inc=1, device_id=(leaf - place[2] + (place[2] + d) % 4, (row + e) % rows_n),
                device_id_type=MESH)
    for d in range(1, leaves_n):
        pl.semaphore_signal(barrier, inc=1, device_id=((leaf + d) % leaves_n, row), device_id_type=MESH)

    def local(name, src, dst):
        return pltpu.make_async_copy(src, dst, local_sem.at[LOCALS.index(name)])

    local_copies = {}
    for c in range(CHUNKS):
        local_copies["z0" + suffix[c]] = local(
            "z0" + suffix[c], rhs.at[pl.ds(0, height), pl.ds(c * chunk, chunk)], z0.at[c, row])
    local_copies["d0"] = local("d0", inv.at[pl.ds(0, height)], d0)
    for m, held in ((1, p1), (2, p2), (3, p3)):
        local_copies["p%d" % m] = local(
            "p%d" % m, pan.at[:, pl.ds(column_start(m, d0.shape[1]), held.shape[1])], held)
    for m, held in ((1, d1), (2, d2), (3, d3)):
        local_copies["d%d" % m] = local("d%d" % m, inv.at[level_rows(m)], held.at[place[m]])
    for c in range(CHUNKS):
        local_copies["b1" + suffix[c]] = local(
            "b1" + suffix[c], rhs.at[level_rows(1), at_cols(2 * c + place[1])], b1.at[c, place[1]])
    local_copies["b2"] = local("b2", rhs.at[level_rows(2), at_cols(block_of(place[2]))], b2.at[place[2]])
    local_copies["b3"] = local("b3", rhs.at[level_rows(3), at_cols(block_of(place[3]))], b3.at[place[3]])
    for name in LOCALS:
        local_copies[name].start()

    pl.semaphore_wait(barrier, 4 * (rows_n - 1) + leaves_n - 1)

    def begin(can, make):
        if can is None:
            make().start()
        else:
            @pl.when(can)
            def _():
                make().start()
        pending.append((can, make))

    def hop(name, src, dst, step, source, way):
        k = GATHERS.index(name)
        sem = up_sem if way > 0 else down_sem
        return pltpu.make_async_remote_copy(
            src_ref=src, dst_ref=dst, send_sem=sem.at[k, step], recv_sem=land_sem.at[k, source],
            device_id=(leaf, row + way), device_id_type=MESH)

    flying = {}

    def hop_begin(way, can, make):
        if way in flying:
            before, earlier = flying[way]

            @pl.when(before)
            def _():
                earlier().wait_send()

        @pl.when(can)
        def _():
            make().start()

        flying[way] = (can, make)

    def gather_start(name, slot, src=None):
        for way, can in ((1, row < rows_n - 1), (-1, row > 0)):
            def make(way=way):
                return hop(name, slot(row) if src is None else src, slot(row), 0, row, way)

            hop_begin(way, can, make)

    def gather_step(name, slot, step):
        for way, can in ((1, row < rows_n - 1), (-1, row > 0)):
            source = row - way * step
            there = (source >= 0) if way > 0 else (source < rows_n)

            def make(way=way, source=source):
                return hop(name, slot(source), slot(source), step, source, way)

            @pl.when(there)
            def _(make=make):
                make().wait_recv()

            if step < rows_n - 1:
                hop_begin(way, jnp.logical_and(there, can), make)

    def direct(name, slot, e):
        k = GATHERS.index(name)
        return pltpu.make_async_remote_copy(
            src_ref=slot(row), dst_ref=slot(row), send_sem=up_sem.at[k, e], recv_sem=land_sem.at[k, e],
            device_id=(leaf, (row + e) % rows_n), device_id_type=MESH)

    def direct_start(name, slot, can):
        for e in range(1, rows_n):
            begin(can, lambda e=e: direct(name, slot, e))

    def direct_wait(name, slot):
        k = GATHERS.index(name)
        for e in range(1, rows_n):
            there = slot((row - e + rows_n) % rows_n)
            pltpu.make_async_remote_copy(
                src_ref=there, dst_ref=there, send_sem=up_sem.at[k, e], recv_sem=land_sem.at[k, e],
                device_id=(leaf, (row + e) % rows_n), device_id_type=MESH).wait_recv()

    def peer(m, d):
        size = 2**m
        return leaf - place[m] + (place[m] + d) % size

    def swap(name, m, d, src, dst):
        k = SWAPS.index(name)
        return pltpu.make_async_remote_copy(
            src_ref=src, dst_ref=dst, send_sem=swap_send.at[k, d], recv_sem=swap_recv.at[k, d],
            device_id=(peer(m, d), row), device_id_type=MESH)

    def swap_start(name, m, src, dst, when=None):
        size = 2**m
        for d in range(1, size):
            target = (place[m] + d) % size

            def make(d=d, target=target):
                return swap(name, m, d, src(target), dst(place[m], d))

            begin(None if when is None else when(target), make)

    def swap_wait(name, m, src, dst):
        size = 2**m
        for d in range(1, size):
            sender = (place[m] - d + size) % size
            swap(name, m, d, src(place[m]), dst(sender, d)).wait_recv()

    def z0_slot(c):
        return lambda q: z0.at[c, q]

    def y0_slot(c):
        return lambda q: y0.at[c, q]

    def z1_slot(c):
        return lambda q: z1.at[c, :, q]

    def y1_slot(c):
        return lambda q: y1.at[c, q]

    def z2_slot(q):
        return z2.at[:, q]

    def z3_slot(q):
        return z3.at[:, q]

    for c in range(CHUNKS):
        gather_start("z0" + suffix[c], z0_slot(c), rhs.at[pl.ds(0, height), pl.ds(c * chunk, chunk)])

    fixed = []
    for c in range(CHUNKS):
        fixed.append((
            "b1" + suffix[c], 1,
            lambda target, c=c: rhs.at[level_rows(1), at_cols(2 * c + target)],
            lambda sender, d, c=c: b1.at[c, sender]))
    fixed.append(("d1", 1, lambda target: inv.at[level_rows(1)], lambda sender, d: d1.at[sender]))
    fixed.append(("b2", 2, lambda target: rhs.at[level_rows(2), at_cols(block_of(target))], lambda sender, d: b2.at[sender]))
    fixed.append(("d2", 2, lambda target: inv.at[level_rows(2)], lambda sender, d: d2.at[sender]))
    fixed.append(("b3", 3, lambda target: rhs.at[level_rows(3), at_cols(block_of(target))], lambda sender, d: b3.at[sender]))
    fixed.append(("d3", 3, lambda target: inv.at[level_rows(3)], lambda sender, d: d3.at[sender]))
    for entry in fixed[: CHUNKS + 1]:
        swap_start(*entry)

    def live(pair):
        return mask[pair].astype(jnp.float32)

    def cols_of(c):
        return pl.ds(c * chunk, chunk)

    for step in range(1, rows_n - 1):
        for c in range(CHUNKS):
            gather_step("z0" + suffix[c], z0_slot(c), step)
    local_copies["d0"].wait()
    whole = d0.shape[1]
    for c in range(CHUNKS):
        local_copies["z0" + suffix[c]].wait()
        gather_step("z0" + suffix[c], z0_slot(c), rows_n - 1)
        solved = dot32(d0[...], z0[c].reshape(whole, chunk))
        y0[c, row] = solved.astype(jnp.bfloat16)
        gather_start("y0" + suffix[c], y0_slot(c))
        out[pl.ds(0, height), cols_of(c)] = solved
    for entry in fixed[CHUNKS + 1 :]:
        swap_start(*entry)
    for step in range(1, rows_n - 1):
        for c in range(CHUNKS):
            gather_step("y0" + suffix[c], y0_slot(c), step)
    for name in ("p1", "p2", "p3"):
        local_copies[name].wait()

    half = whole // 2
    u1_src = [lambda target, c=c: u1s.at[c, :, at_cols(target)] for c in range(CHUNKS)]
    u1_dst = [lambda sender, d, c=c: u1r.at[c, d - 1] for c in range(CHUNKS)]
    y1_src = [lambda target, c=c: y1s.at[c, target] for c in range(CHUNKS)]
    y1_dst = [lambda sender, d, c=c: y1.at[c, row, :, at_cols(sender)] for c in range(CHUNKS)]

    def update_1(c):
        gather_step("y0" + suffix[c], y0_slot(c), rows_n - 1)
        update = dot32(p1[...], y0[c].reshape(whole, chunk)) * live(0)
        u1[c] = update
        u1s[c] = update.astype(jnp.bfloat16)
        swap_start("u1" + suffix[c], 1, u1_src[c], u1_dst[c])

    def reduce_1(c):
        local_copies["b1" + suffix[c]].wait()
        swap_wait(*fixed[c])
        swap_wait("u1" + suffix[c], 1, u1_src[c], u1_dst[c])
        total = u1[c, :, at_cols(place[1])] + u1r[c, 0].astype(jnp.float32)
        reduced = (b1[c].reshape(height, wide).astype(jnp.float32) - total).astype(jnp.bfloat16)
        for s in range(2):
            z1[c, s, row] = reduced[s * heights[1] : (s + 1) * heights[1]]
        gather_start("z1" + suffix[c], z1_slot(c))

    def early_2(c):
        u2[:, cols_of(c)] = dot32(p2[:, :whole], y0[c].reshape(whole, chunk)) * live(1)

    def early_3(c):
        u3[:, cols_of(c)] = dot32(p3[:, :whole], y0[c].reshape(whole, chunk)) * live(3)

    def solve_1(c):
        gather_step("z1" + suffix[c], z1_slot(c), rows_n - 1)
        solved = dot32(d1[...].reshape(height, whole), z1[c].reshape(whole, wide)).astype(jnp.bfloat16)
        y1s[c] = solved.reshape(2, heights[1], wide)
        swap_start("y1" + suffix[c], 1, y1_src[c], y1_dst[c])
        y1[c, row, :, at_cols(place[1])] = y1s[c, place[1]]

    def spread_1(c):
        swap_wait("y1" + suffix[c], 1, y1_src[c], y1_dst[c])
        gather_start("y1" + suffix[c], y1_slot(c))

    u2_src = lambda target: u2s.at[:, at_cols(block_of(target))]
    u2_dst = lambda sender, d: u2r.at[d - 1]

    def update_2(c):
        gather_step("y1" + suffix[c], y1_slot(c), rows_n - 1)
        update = u2[:, cols_of(c)] + dot32(p2[:, whole:], y1[c].reshape(half, chunk)) * live(2)
        u2[:, cols_of(c)] = update
        u2s[:, cols_of(c)] = update.astype(jnp.bfloat16)
        swap_start("u2", 2, u2_src, u2_dst, lambda target: target % 2 == c)

    def later_3(c):
        u3[:, cols_of(c)] += dot32(p3[:, whole : whole + half], y1[c].reshape(half, chunk)) * live(4)

    def reduce_2(c):
        @pl.when(own_chunk == c)
        def _():
            swap_wait("u2", 2, u2_src, u2_dst)
            total = u2[:, at_cols(block_of(place[2]))]
            for d in range(3):
                total = total + u2r[d].astype(jnp.float32)
            reduced = (b2[...].reshape(height, wide).astype(jnp.float32) - total).astype(jnp.bfloat16)
            for s in range(4):
                z2[s, row] = reduced[s * heights[2] : (s + 1) * heights[2]]

        direct_start("z2", z2_slot, own_chunk == c)

    def spread(d, e, position):
        here = leaf - place[2] + (place[2] + d) % 4
        dst = y2.at[(row if position is None else (row - e + rows_n) % rows_n), :,
                    at_cols(block_of(place[2] if position is None else position))]
        src = y2s.at[(place[2] + d) % 4]
        return pltpu.make_async_remote_copy(
            src_ref=src, dst_ref=dst, send_sem=spread_send.at[d, e], recv_sem=spread_recv.at[d, e],
            device_id=(here, (row + e) % rows_n), device_id_type=MESH)

    others = [(d, e) for e in reversed(range(rows_n)) for d in range(4) if d or e]

    def solve_2(c):
        @pl.when(own_chunk == c)
        def _():
            direct_wait("z2", z2_slot)
            solved = dot32(d2[...].reshape(height, whole), z2[...].reshape(whole, wide)).astype(jnp.bfloat16)
            y2s[...] = solved.reshape(4, heights[2], wide)

        for d, e in others:
            begin(own_chunk == c, lambda d=d, e=e: spread(d, e, None))

        @pl.when(own_chunk == c)
        def _():
            y2[row, :, at_cols(block_of(place[2]))] = y2s[place[2]]

    fold = height // 2
    low = lax.broadcasted_iota(jnp.int32, (fold, wide), 1) < wide // 2

    def folded(top, bottom):
        return (
            jnp.where(low, top, pltpu.roll(bottom, wide // 2, 1)),
            jnp.where(low, pltpu.roll(top, wide // 2, 1), bottom),
        )

    u3_src = lambda target: u3s.at[target]
    u3_dst = lambda sender, d: u3r.at[d - 1]

    def update_3(c):
        for d, e in others:
            sender = (place[2] - d + 4) % 4

            @pl.when(sender % 2 == c)
            def _(d=d, e=e, sender=sender):
                spread(d, e, sender).wait_recv()

        known = y2[:, :, c * chunk : (c + 1) * chunk].reshape(whole // 4, chunk)
        update = u3[:, cols_of(c)] + dot32(p3[:, whole + half :], known) * live(5)
        for k in range(2):
            block = update[:, k * wide : (k + 1) * wide]
            sides = folded(block[:fold], block[fold:])
            for side in range(2):
                u3s[4 * side + 2 * k + c] = sides[side].astype(jnp.bfloat16)
        swap_start("u3", 3, u3_src, u3_dst, lambda target: target % 2 == c)

    def reduce_3(c):
        @pl.when(own_chunk == c)
        def _():
            own_b = b3[...].astype(jnp.float32)
            sides = folded(own_b[:4].reshape(fold, wide), own_b[4:].reshape(fold, wide))
            own_b = jnp.where(place[3] < leaves_n // 2, sides[0], sides[1])
            swap_wait("u3", 3, u3_src, u3_dst)
            total = u3s[place[3]].astype(jnp.float32)
            for d in range(leaves_n - 1):
                total = total + u3r[d].astype(jnp.float32)
            reduced = (own_b - total).astype(jnp.bfloat16)
            for s in range(4):
                z3[s, row] = reduced[s * heights[3] : (s + 1) * heights[3]]

        direct_start("z3", z3_slot, own_chunk == c)

    y3_src = lambda target: y3s.at[target]
    y3_dst = lambda sender, d: y3r.at[sender]

    def solve_3():
        direct_wait("z3", z3_slot)
        known = z3[...].reshape(half, wide)
        left = dot32(d3[:, :, :half].reshape(height, half), known)
        right = dot32(d3[:, :, half:].reshape(height, half), known)
        solved = left + pltpu.roll(right, wide // 2, 1)
        low_all = lax.broadcasted_iota(jnp.int32, (height, wide), 1) < wide // 2
        solved = jnp.where(low_all, solved, pltpu.roll(solved, wide // 2, 1))
        y3s[...] = solved.astype(jnp.bfloat16).reshape(leaves_n, heights[3], wide)
        swap_start("y3", 3, y3_src, y3_dst)
        y3r[place[3]] = y3s[place[3]]

    update_1(0)
    early_2(0)
    reduce_1(0)
    early_3(0)
    update_1(1)
    gather_step("z1a", z1_slot(0), 1)
    reduce_1(1)
    early_2(1)
    early_3(1)
    for step in range(2, rows_n - 1):
        gather_step("z1a", z1_slot(0), step)
        gather_step("z1b", z1_slot(1), step - 1)
    local_copies["d1"].wait()
    swap_wait(*fixed[CHUNKS])
    solve_1(0)
    gather_step("z1b", z1_slot(1), rows_n - 2)
    spread_1(0)
    solve_1(1)
    gather_step("y1a", y1_slot(0), 1)
    spread_1(1)
    for step in range(2, rows_n - 1):
        gather_step("y1a", y1_slot(0), step)
        gather_step("y1b", y1_slot(1), step - 1)
    local_copies["b2"].wait()
    swap_wait(*fixed[CHUNKS + 1])
    update_2(0)
    gather_step("y1b", y1_slot(1), rows_n - 2)
    later_3(0)
    reduce_2(0)
    update_2(1)
    local_copies["d2"].wait()
    swap_wait(*fixed[CHUNKS + 2])
    reduce_2(1)
    later_3(1)
    for c in range(CHUNKS):
        out[level_rows(1), cols_of(c)] = y1[c, row].astype(jnp.float32)
    local_copies["b3"].wait()
    swap_wait(*fixed[CHUNKS + 3])
    local_copies["d3"].wait()
    swap_wait(*fixed[CHUNKS + 4])
    solve_2(0)
    solve_2(1)
    update_3(0)
    reduce_3(0)
    update_3(1)
    reduce_3(1)
    out[level_rows(2), :] = y2[row].astype(jnp.float32)
    solve_3()
    swap_wait("y3", 3, y3_src, y3_dst)
    low_out = lax.broadcasted_iota(jnp.int32, (heights[3], wide), 1) < wide // 2
    for k in range(leaves_n // 2):
        first = 2 * (k % 2) + k // 2
        out[level_rows(3), pl.ds(k * wide, wide)] = jnp.where(
            low_out, y3r[first].astype(jnp.float32), y3r[first + leaves_n // 2].astype(jnp.float32))

    pending.extend(flying.values())
    for can, make in pending:
        if can is None:
            make().wait_send()
        else:
            @pl.when(can)
            def _(make=make):
                make().wait_send()


def fits(rows_n, leaves_n, rhs, inv_diag, off_diag):
    whole = inv_diag.shape[3]
    right_n = rhs.shape[3]
    return (
        leaves_n == 2**TREE_LEVELS
        and rows_n > 2
        and whole % (leaves_n * rows_n * ROW_TILE) == 0
        and whole % (4 * LANES) == 0
        and right_n == 4 * LANES
    )


def tree_shards(rhs, inv_diag, off_diag, pair_mask):
    rows_n = lax.axis_size("row")
    leaves_n = lax.axis_size("leaf")
    whole = inv_diag.shape[3]
    right_n = rhs.shape[3]
    height = off_diag.shape[2]
    chunk = right_n // CHUNKS
    hs = [height // 2**m for m in range(TREE_LEVELS + 1)]
    bf16, f32 = jnp.bfloat16, jnp.float32
    vm = pltpu.VMEM
    scratch = [
        vm((height, whole), bf16),
        vm((2, hs[1], whole), bf16), vm((4, hs[2], whole), bf16), vm((8, hs[3], whole), bf16),
        vm((height, whole), bf16), vm((height, whole + whole // 2), bf16),
        vm((height, whole + whole // 2 + whole // 4), bf16),
        vm((CHUNKS, 2, hs[1], LANES), bf16), vm((4, hs[2], LANES), bf16), vm((8, hs[3], LANES), bf16),
        vm((CHUNKS, rows_n, height, chunk), bf16),
        vm((CHUNKS, 2, rows_n, hs[1], LANES), bf16),
        vm((4, rows_n, hs[2], LANES), bf16),
        vm((4, rows_n, hs[3], LANES), bf16),
        vm((CHUNKS, rows_n, height, chunk), bf16),
        vm((CHUNKS, rows_n, hs[1], chunk), bf16),
        vm((rows_n, hs[2], right_n), bf16),
        vm((CHUNKS, height, chunk), f32), vm((height, right_n), f32), vm((height, right_n), f32),
        vm((CHUNKS, height, chunk), bf16), vm((height, right_n), bf16),
        vm((leaves_n, height // 2, LANES), bf16),
        vm((CHUNKS, 1, height, LANES), bf16), vm((3, height, LANES), bf16),
        vm((leaves_n - 1, height // 2, LANES), bf16),
        vm((CHUNKS, 2, hs[1], LANES), bf16), vm((4, hs[2], LANES), bf16),
        vm((leaves_n, hs[3], LANES), bf16), vm((leaves_n, hs[3], LANES), bf16),
        pltpu.SemaphoreType.DMA((len(GATHERS), rows_n)),
        pltpu.SemaphoreType.DMA((len(GATHERS), rows_n)),
        pltpu.SemaphoreType.DMA((len(GATHERS), rows_n)),
        pltpu.SemaphoreType.DMA((len(SWAPS), leaves_n)),
        pltpu.SemaphoreType.DMA((len(SWAPS), leaves_n)),
        pltpu.SemaphoreType.DMA((len(LOCALS),)),
        pltpu.SemaphoreType.DMA((4, rows_n)),
        pltpu.SemaphoreType.DMA((4, rows_n)),
    ]
    pack = rhs.shape[2]
    flops = 2 * right_n * (pack * whole + height * off_diag.shape[3])
    moved = 2 * (pack * whole + height * off_diag.shape[3] + 3 * pack * right_n)
    solved = pl.pallas_call(
        functools.partial(tree_kernel, rows_n, leaves_n),
        out_shape=jax.ShapeDtypeStruct((pack, right_n), f32),
        in_specs=[pl.BlockSpec(memory_space=pltpu.SMEM)] + [pl.BlockSpec(memory_space=pltpu.HBM)] * 3,
        out_specs=pl.BlockSpec(memory_space=pltpu.VMEM),
        scratch_shapes=scratch,
        compiler_params=pltpu.CompilerParams(
            collective_id=0, has_side_effects=True, vmem_limit_bytes=63 * 2**20),
        cost_estimate=pl.CostEstimate(flops=flops, bytes_accessed=moved, transcendentals=0),
    )(pair_mask[0, 0], rhs[0, 0], inv_diag[0, 0], off_diag[0, 0])
    return solved[None, None]


def solution(mesh):
    in_specs = (
        P("leaf", "row", None, None),
        P("leaf", "row", None, None),
        P("leaf", "row", None, None),
        P("leaf", "row", None),
    )
    out_specs = P("leaf", "row", None, None)

    def run(rhs, inv_diag, off_diag, pair_mask):
        fit = fits(mesh.shape["row"], mesh.shape["leaf"], rhs, inv_diag, off_diag)
        body = tree_shards if fit else shards
        return jax.shard_map(body, mesh=mesh, in_specs=in_specs, out_specs=out_specs, check_vma=False)(
            rhs, inv_diag, off_diag, pair_mask
        )

    return run
```

```python
import functools

import jax
import jax.numpy as jnp
from jax import lax
from jax.experimental import pallas as pl
from jax.experimental.pallas import tpu as pltpu
from jax.sharding import PartitionSpec as P

LANES = 128
ROW_TILE = 16
CHUNKS = 2
TREE_LEVELS = 3
MESH = pl.DeviceIdType.MESH


def partner_2(block, axis, bit):
    count = lax.axis_size(axis)
    route = []
    for low in range(count):
        high = low | 1 << bit
        if high != low and high < count:
            route += [(low, high), (high, low)]
    return lax.ppermute(block, axis, route)


def column_start(ancestor, width_all):
    offset = 0
    for higher in range(1, ancestor):
        for within in range(higher):
            offset += width_all // 2**within
    return offset


def shards(rhs, inv_diag, off_diag, pair_mask):
    rows_n = lax.axis_size("row")
    leaves = lax.axis_size("leaf")
    levels_n = leaves.bit_length() - 1
    leaf_index = lax.axis_index("leaf")
    width_all = inv_diag.shape[3]
    right_all = rhs[0, 0]
    inverse_all = inv_diag[0, 0]
    panels = off_diag[0, 0]
    live_pairs = pair_mask[0, 0].astype(jnp.bfloat16)
    known_parts = []
    outputs = []
    offset = 0
    for ancestor in range(levels_n + 1):
        height = width_all // (2**ancestor * rows_n)
        own_rhs = right_all[offset : offset + height]
        own_inv = inverse_all[offset : offset + height]
        offset += height
        if ancestor > 0:
            stacked = jnp.concatenate(
                [
                    known_parts[source] * live_pairs[ancestor * (ancestor - 1) // 2 + source]
                    for source in range(ancestor)
                ],
                axis=0,
            )
            first_col = column_start(ancestor, width_all)
            span_cols = stacked.shape[0]
            update = jnp.dot(
                panels[:, first_col : first_col + span_cols],
                stacked,
                preferred_element_type=jnp.float32,
            )
        if ancestor > 0:
            current = update
            for bit_pos in reversed(range(ancestor)):
                half_rows = current.shape[0] // 2
                upper_half = leaf_index // 2**bit_pos % 2 == 1
                kept_rows = jnp.where(upper_half, current[half_rows:], current[:half_rows])
                sent_rows = jnp.where(upper_half, current[:half_rows], current[half_rows:])
                current = kept_rows + partner_2(
                    sent_rows.astype(jnp.bfloat16), "leaf", bit_pos
                ).astype(sent_rows.dtype)
            reduced = (own_rhs.astype(jnp.float32) - current).astype(jnp.bfloat16)
        else:
            reduced = own_rhs
        gathered = lax.all_gather(reduced, "row", axis=0, tiled=True)
        for bit_pos in range(ancestor):
            partner = partner_2(gathered, "leaf", bit_pos)
            upper_half = leaf_index // 2**bit_pos % 2 == 1
            gathered = jnp.where(
                upper_half,
                jnp.concatenate([partner, gathered], axis=0),
                jnp.concatenate([gathered, partner], axis=0),
            )
        solved = jnp.dot(own_inv, gathered, preferred_element_type=jnp.float32)
        outputs.append(solved)
        if ancestor < levels_n:
            leaf_part = lax.all_gather(solved.astype(jnp.bfloat16), "row", axis=0, tiled=True)
            known_parts.append(leaf_part)
    return jnp.concatenate(outputs, axis=0)[None, None]


def dot32(left, right):
    return jnp.dot(left, right, preferred_element_type=jnp.float32)


GATHERS = ["z0a", "z0b", "y0a", "y0b", "z1a", "z1b", "y1a", "y1b", "z2", "z3"]
SWAPS = ["b1a", "b1b", "b2", "b3", "d1", "d2", "d3", "d2p", "d3p", "u1a", "u1b", "u2", "u3", "y1a", "y1b", "y3"]
LOCALS = ["z0a", "z0b", "d0", "p1", "p2", "p3", "d1", "d2", "d3", "b1a", "b1b", "b2", "b3"]


def tree_kernel(
    rows_n, leaves_n,
    mask, rhs, inv, pan, out,
    d0, d1, d2, d3, p1, p2, p3, b1, b2, b3,
    z0, z1, z2, z3, y0, y1, y2,
    u1, u2, u3, u1s, u2s, u3s, u1r, u2r, u3r, y1s, y2s, y3s, y3r,
    up_sem, down_sem, land_sem, swap_send, swap_recv, local_sem, spread_send, spread_recv,
):
    leaf = lax.axis_index("leaf")
    row = lax.axis_index("row")
    height = p1.shape[0]
    right_n = u2.shape[1]
    chunk = right_n // CHUNKS
    heights = [height // 2**m for m in range(TREE_LEVELS + 1)]
    starts = [sum(heights[:m]) for m in range(TREE_LEVELS + 1)]
    wide = LANES
    suffix = "ab"
    pending = []
    place = [leaf % 2**m for m in range(TREE_LEVELS + 1)]
    own_chunk = leaf % 2

    def block_of(position):
        return 2 * (position % 2) + position // 2 % 2

    def at_cols(index):
        return pl.ds(pl.multiple_of(index * wide, wide), wide)

    def level_rows(m):
        return pl.ds(starts[m], heights[m])

    barrier = pltpu.get_barrier_semaphore()

    for e in range(1, rows_n):
        for d in range(4):
            pl.semaphore_signal(
                barrier, inc=1, device_id=(leaf - place[2] + (place[2] + d) % 4, (row + e) % rows_n),
                device_id_type=MESH)
    for d in range(1, leaves_n):
        pl.semaphore_signal(barrier, inc=1, device_id=((leaf + d) % leaves_n, row), device_id_type=MESH)

    def local(name, src, dst):
        return pltpu.make_async_copy(src, dst, local_sem.at[LOCALS.index(name)])

    local_copies = {}
    for c in range(CHUNKS):
        local_copies["z0" + suffix[c]] = local(
            "z0" + suffix[c], rhs.at[pl.ds(0, height), pl.ds(c * chunk, chunk)], z0.at[c, row])
    local_copies["d0"] = local("d0", inv.at[pl.ds(0, height)], d0)
    for m, held in ((1, p1), (2, p2), (3, p3)):
        local_copies["p%d" % m] = local(
            "p%d" % m, pan.at[:, pl.ds(column_start(m, d0.shape[1]), held.shape[1])], held)
    for m, held in ((1, d1), (2, d2), (3, d3)):
        local_copies["d%d" % m] = local("d%d" % m, inv.at[level_rows(m)], held.at[place[m]])
    for c in range(CHUNKS):
        local_copies["b1" + suffix[c]] = local(
            "b1" + suffix[c], rhs.at[level_rows(1), at_cols(2 * c + place[1])], b1.at[c, place[1]])
    local_copies["b2"] = local("b2", rhs.at[level_rows(2), at_cols(block_of(place[2]))], b2.at[place[2]])
    local_copies["b3"] = local("b3", rhs.at[level_rows(3), at_cols(block_of(place[3]))], b3.at[place[3]])
    for name in LOCALS:
        local_copies[name].start()

    pl.semaphore_wait(barrier, 4 * (rows_n - 1) + leaves_n - 1)

    def begin(can, make):
        if can is None:
            make().start()
        else:
            @pl.when(can)
            def _():
                make().start()
        pending.append((can, make))

    def hop(name, src, dst, step, source, order, way):
        k = GATHERS.index(name)
        sem = (up_sem, down_sem)[order]
        return pltpu.make_async_remote_copy(
            src_ref=src, dst_ref=dst, send_sem=sem.at[k, step], recv_sem=land_sem.at[k, source],
            device_id=(leaf, row + way), device_id_type=MESH)

    lead = 1 - 2 * (leaf % 2)
    ways = [(order, lead if order == 0 else -lead) for order in range(2)]

    def inside(index):
        return jnp.logical_and(index >= 0, index < rows_n)

    def gather_start(name, slot, src=None):
        for order, way in ways:
            can = inside(row + way)

            def make(order=order, way=way):
                return hop(name, slot(row) if src is None else src, slot(row), 0, row, order, way)

            @pl.when(can)
            def _(make=make):
                make().start()

            pending.append((can, make))

    def gather_step(name, slot, step):
        for order, way in ways:
            can = inside(row + way)
            source = row - way * step
            there = inside(source)

            def make(order=order, way=way, source=source):
                return hop(name, slot(source), slot(source), step, source, order, way)

            @pl.when(there)
            def _(make=make):
                make().wait_recv()

            if step < rows_n - 1:
                both = jnp.logical_and(there, can)

                @pl.when(both)
                def _(make=make):
                    make().start()

                pending.append((both, make))

    def direct(name, slot, e):
        k = GATHERS.index(name)
        return pltpu.make_async_remote_copy(
            src_ref=slot(row), dst_ref=slot(row), send_sem=up_sem.at[k, e], recv_sem=land_sem.at[k, e],
            device_id=(leaf, (row + e) % rows_n), device_id_type=MESH)

    def direct_start(name, slot, can):
        for e in range(1, rows_n):
            begin(can, lambda e=e: direct(name, slot, e))

    def direct_wait(name, slot):
        k = GATHERS.index(name)
        for e in range(1, rows_n):
            there = slot((row - e + rows_n) % rows_n)
            pltpu.make_async_remote_copy(
                src_ref=there, dst_ref=there, send_sem=up_sem.at[k, e], recv_sem=land_sem.at[k, e],
                device_id=(leaf, (row + e) % rows_n), device_id_type=MESH).wait_recv()

    def peer(m, d):
        size = 2**m
        return leaf - place[m] + (place[m] + d) % size

    def swap(name, m, d, src, dst, line=None):
        k = SWAPS.index(name)
        line = d if line is None else line
        return pltpu.make_async_remote_copy(
            src_ref=src, dst_ref=dst, send_sem=swap_send.at[k, line], recv_sem=swap_recv.at[k, line],
            device_id=(peer(m, d), row), device_id_type=MESH)

    def swap_start(name, m, src, dst, when=None, only=None):
        size = 2**m
        for d in only or range(1, size):
            target = (place[m] + d) % size

            def make(d=d, target=target):
                return swap(name, m, d, src(target), dst(place[m], d))

            begin(None if when is None else when(target), make)

    def swap_wait(name, m, src, dst, only=None):
        size = 2**m
        for d in only or range(1, size):
            sender = (place[m] - d + size) % size
            swap(name, m, d, src(place[m]), dst(sender, d)).wait_recv()

    def z0_slot(c):
        return lambda q: z0.at[c, q]

    def y0_slot(c):
        return lambda q: y0.at[c, q]

    def z1_slot(c):
        return lambda q: z1.at[c, :, q]

    def y1_slot(c):
        return lambda q: y1.at[c, q]

    def z2_slot(q):
        return z2.at[:, q]

    def z3_slot(q):
        return z3.at[:, q]

    for c in range(CHUNKS):
        gather_start("z0" + suffix[c], z0_slot(c), rhs.at[pl.ds(0, height), pl.ds(c * chunk, chunk)])

    fixed = []
    for c in range(CHUNKS):
        fixed.append((
            "b1" + suffix[c], 1,
            lambda target, c=c: rhs.at[level_rows(1), at_cols(2 * c + target)],
            lambda sender, d, c=c: b1.at[c, sender]))
    fixed.append(("d1", 1, lambda target: inv.at[level_rows(1)], lambda sender, d: d1.at[sender]))
    fixed.append(("b2", 2, lambda target: rhs.at[level_rows(2), at_cols(block_of(target))], lambda sender, d: b2.at[sender]))
    fixed.append(("d2", 2, lambda target: inv.at[level_rows(2)], lambda sender, d: d2.at[sender]))
    fixed.append(("b3", 3, lambda target: rhs.at[level_rows(3), at_cols(block_of(target))], lambda sender, d: b3.at[sender]))
    fixed.append(("d3", 3, lambda target: inv.at[level_rows(3)], lambda sender, d: d3.at[sender]))
    D2, D3 = CHUNKS + 2, CHUNKS + 4
    for k, entry in enumerate(fixed):
        if k not in (D2, D3):
            swap_start(*entry)

    def hand_over(name, held, i, mine):
        at = 2 * i + (place[1] if mine else 1 - place[1])
        return swap(name, 1, 1, held.at[at], held.at[at], i)

    def hand_all(name, held):
        for i in range(held.shape[0] // 2):
            begin(None, lambda i=i: hand_over(name, held, i, True))

    def taken_all(name, held):
        for i in range(held.shape[0] // 2):
            hand_over(name, held, i, False).wait_recv()

    def live(pair):
        return mask[pair].astype(jnp.float32)

    def cols_of(c):
        return pl.ds(c * chunk, chunk)

    pieces = [(D2, 2), (D3, 2), (D3, 4), (D3, 6)]
    for step in range(1, rows_n - 1):
        for c in range(CHUNKS):
            gather_step("z0" + suffix[c], z0_slot(c), step)
            if pieces:
                entry, d = pieces.pop(0)
                swap_start(*fixed[entry], only=[d])
    for entry, d in pieces:
        swap_start(*fixed[entry], only=[d])
    local_copies["d0"].wait()
    whole = d0.shape[1]
    for c in range(CHUNKS):
        local_copies["z0" + suffix[c]].wait()
        gather_step("z0" + suffix[c], z0_slot(c), rows_n - 1)
        solved = dot32(d0[...], z0[c].reshape(whole, chunk))
        y0[c, row] = solved.astype(jnp.bfloat16)
        gather_start("y0" + suffix[c], y0_slot(c))
        out[pl.ds(0, height), cols_of(c)] = solved
    for step in range(1, rows_n - 1):
        for c in range(CHUNKS):
            gather_step("y0" + suffix[c], y0_slot(c), step)
    for name in ("p1", "p2", "p3", "d2", "d3"):
        local_copies[name].wait()
    swap_wait(*fixed[D2], only=[2])
    swap_wait(*fixed[D3], only=[2, 4, 6])
    hand_all("d2p", d2)
    hand_all("d3p", d3)

    half = whole // 2
    u1_src = [lambda target, c=c: u1s.at[c, :, at_cols(target)] for c in range(CHUNKS)]
    u1_dst = [lambda sender, d, c=c: u1r.at[c, d - 1] for c in range(CHUNKS)]
    y1_src = [lambda target, c=c: y1s.at[c, target] for c in range(CHUNKS)]
    y1_dst = [lambda sender, d, c=c: y1.at[c, row, :, at_cols(sender)] for c in range(CHUNKS)]

    def update_1(c):
        gather_step("y0" + suffix[c], y0_slot(c), rows_n - 1)
        update = dot32(p1[...], y0[c].reshape(whole, chunk)) * live(0)
        u1[c] = update
        u1s[c] = update.astype(jnp.bfloat16)
        swap_start("u1" + suffix[c], 1, u1_src[c], u1_dst[c])

    def reduce_1(c):
        local_copies["b1" + suffix[c]].wait()
        swap_wait(*fixed[c])
        swap_wait("u1" + suffix[c], 1, u1_src[c], u1_dst[c])
        total = u1[c, :, at_cols(place[1])] + u1r[c, 0].astype(jnp.float32)
        reduced = (b1[c].reshape(height, wide).astype(jnp.float32) - total).astype(jnp.bfloat16)
        for s in range(2):
            z1[c, s, row] = reduced[s * heights[1] : (s + 1) * heights[1]]
        gather_start("z1" + suffix[c], z1_slot(c))

    def early_2(c):
        u2[:, cols_of(c)] = dot32(p2[:, :whole], y0[c].reshape(whole, chunk)) * live(1)

    def early_3(c):
        u3[:, cols_of(c)] = dot32(p3[:, :whole], y0[c].reshape(whole, chunk)) * live(3)

    def solve_1(c):
        gather_step("z1" + suffix[c], z1_slot(c), rows_n - 1)
        solved = dot32(d1[...].reshape(height, whole), z1[c].reshape(whole, wide)).astype(jnp.bfloat16)
        y1s[c] = solved.reshape(2, heights[1], wide)
        swap_start("y1" + suffix[c], 1, y1_src[c], y1_dst[c])
        y1[c, row, :, at_cols(place[1])] = y1s[c, place[1]]

    def spread_1(c):
        swap_wait("y1" + suffix[c], 1, y1_src[c], y1_dst[c])
        gather_start("y1" + suffix[c], y1_slot(c))

    u2_src = lambda target: u2s.at[:, at_cols(block_of(target))]
    u2_dst = lambda sender, d: u2r.at[d - 1]

    def update_2(c):
        gather_step("y1" + suffix[c], y1_slot(c), rows_n - 1)
        update = u2[:, cols_of(c)] + dot32(p2[:, whole:], y1[c].reshape(half, chunk)) * live(2)
        u2[:, cols_of(c)] = update
        u2s[:, cols_of(c)] = update.astype(jnp.bfloat16)
        swap_start("u2", 2, u2_src, u2_dst, lambda target: target % 2 == c)

    def later_3(c):
        u3[:, cols_of(c)] += dot32(p3[:, whole : whole + half], y1[c].reshape(half, chunk)) * live(4)

    def reduce_2(c):
        @pl.when(own_chunk == c)
        def _():
            swap_wait("u2", 2, u2_src, u2_dst)
            total = u2[:, at_cols(block_of(place[2]))]
            for d in range(3):
                total = total + u2r[d].astype(jnp.float32)
            reduced = (b2[...].reshape(height, wide).astype(jnp.float32) - total).astype(jnp.bfloat16)
            for s in range(4):
                z2[s, row] = reduced[s * heights[2] : (s + 1) * heights[2]]

        direct_start("z2", z2_slot, own_chunk == c)

    def spread(d, e, position):
        here = leaf - place[2] + (place[2] + d) % 4
        dst = y2.at[(row if position is None else (row - e + rows_n) % rows_n), :,
                    at_cols(block_of(place[2] if position is None else position))]
        src = y2s.at[(place[2] + d) % 4]
        return pltpu.make_async_remote_copy(
            src_ref=src, dst_ref=dst, send_sem=spread_send.at[d, e], recv_sem=spread_recv.at[d, e],
            device_id=(here, (row + e) % rows_n), device_id_type=MESH)

    others = [(d, e) for e in reversed(range(rows_n)) for d in range(4) if d or e]

    def solve_2(c):
        @pl.when(own_chunk == c)
        def _():
            direct_wait("z2", z2_slot)
            solved = dot32(d2[...].reshape(height, whole), z2[...].reshape(whole, wide)).astype(jnp.bfloat16)
            y2s[...] = solved.reshape(4, heights[2], wide)

        for d, e in others:
            begin(own_chunk == c, lambda d=d, e=e: spread(d, e, None))

        @pl.when(own_chunk == c)
        def _():
            y2[row, :, at_cols(block_of(place[2]))] = y2s[place[2]]

    fold = height // 2
    low = lax.broadcasted_iota(jnp.int32, (fold, wide), 1) < wide // 2

    def folded(top, bottom):
        return (
            jnp.where(low, top, pltpu.roll(bottom, wide // 2, 1)),
            jnp.where(low, pltpu.roll(top, wide // 2, 1), bottom),
        )

    u3_src = lambda target: u3s.at[target]
    u3_dst = lambda sender, d: u3r.at[d - 1]

    def update_3(c):
        for d, e in others:
            sender = (place[2] - d + 4) % 4

            @pl.when(sender % 2 == c)
            def _(d=d, e=e, sender=sender):
                spread(d, e, sender).wait_recv()

        known = y2[:, :, c * chunk : (c + 1) * chunk].reshape(whole // 4, chunk)
        update = u3[:, cols_of(c)] + dot32(p3[:, whole + half :], known) * live(5)
        for k in range(2):
            block = update[:, k * wide : (k + 1) * wide]
            sides = folded(block[:fold], block[fold:])
            for side in range(2):
                u3s[4 * side + 2 * k + c] = sides[side].astype(jnp.bfloat16)
        swap_start("u3", 3, u3_src, u3_dst, lambda target: target % 2 == c)

    def reduce_3(c):
        @pl.when(own_chunk == c)
        def _():
            own_b = b3[...].astype(jnp.float32)
            sides = folded(own_b[:4].reshape(fold, wide), own_b[4:].reshape(fold, wide))
            own_b = jnp.where(place[3] < leaves_n // 2, sides[0], sides[1])
            swap_wait("u3", 3, u3_src, u3_dst)
            total = u3s[place[3]].astype(jnp.float32)
            for d in range(leaves_n - 1):
                total = total + u3r[d].astype(jnp.float32)
            reduced = (own_b - total).astype(jnp.bfloat16)
            for s in range(4):
                z3[s, row] = reduced[s * heights[3] : (s + 1) * heights[3]]

        direct_start("z3", z3_slot, own_chunk == c)

    y3_src = lambda target: y3s.at[target]
    y3_dst = lambda sender, d: y3r.at[sender]

    def solve_3():
        direct_wait("z3", z3_slot)
        known = z3[...].reshape(half, wide)
        left = dot32(d3[:, :, :half].reshape(height, half), known)
        right = dot32(d3[:, :, half:].reshape(height, half), known)
        solved = left + pltpu.roll(right, wide // 2, 1)
        low_all = lax.broadcasted_iota(jnp.int32, (height, wide), 1) < wide // 2
        solved = jnp.where(low_all, solved, pltpu.roll(solved, wide // 2, 1))
        y3s[...] = solved.astype(jnp.bfloat16).reshape(leaves_n, heights[3], wide)
        swap_start("y3", 3, y3_src, y3_dst)
        y3r[place[3]] = y3s[place[3]]

    update_1(0)
    early_2(0)
    reduce_1(0)
    early_3(0)
    update_1(1)
    gather_step("z1a", z1_slot(0), 1)
    reduce_1(1)
    early_2(1)
    early_3(1)
    for step in range(2, rows_n - 1):
        gather_step("z1a", z1_slot(0), step)
        gather_step("z1b", z1_slot(1), step - 1)
    local_copies["d1"].wait()
    swap_wait(*fixed[CHUNKS])
    solve_1(0)
    gather_step("z1b", z1_slot(1), rows_n - 2)
    spread_1(0)
    solve_1(1)
    gather_step("y1a", y1_slot(0), 1)
    spread_1(1)
    for step in range(2, rows_n - 1):
        gather_step("y1a", y1_slot(0), step)
        gather_step("y1b", y1_slot(1), step - 1)
    local_copies["b2"].wait()
    swap_wait(*fixed[CHUNKS + 1])
    update_2(0)
    gather_step("y1b", y1_slot(1), rows_n - 2)
    later_3(0)
    reduce_2(0)
    update_2(1)
    taken_all("d2p", d2)
    reduce_2(1)
    later_3(1)
    for c in range(CHUNKS):
        out[level_rows(1), cols_of(c)] = y1[c, row].astype(jnp.float32)
    local_copies["b3"].wait()
    swap_wait(*fixed[CHUNKS + 3])
    taken_all("d3p", d3)
    solve_2(0)
    solve_2(1)
    update_3(0)
    reduce_3(0)
    update_3(1)
    reduce_3(1)
    out[level_rows(2), :] = y2[row].astype(jnp.float32)
    solve_3()
    swap_wait("y3", 3, y3_src, y3_dst)
    low_out = lax.broadcasted_iota(jnp.int32, (heights[3], wide), 1) < wide // 2
    for k in range(leaves_n // 2):
        first = 2 * (k % 2) + k // 2
        out[level_rows(3), pl.ds(k * wide, wide)] = jnp.where(
            low_out, y3r[first].astype(jnp.float32), y3r[first + leaves_n // 2].astype(jnp.float32))

    for can, make in pending:
        if can is None:
            make().wait_send()
        else:
            @pl.when(can)
            def _(make=make):
                make().wait_send()


def fits(rows_n, leaves_n, rhs, inv_diag, off_diag):
    whole = inv_diag.shape[3]
    right_n = rhs.shape[3]
    return (
        leaves_n == 2**TREE_LEVELS
        and rows_n > 2
        and whole % (leaves_n * rows_n * ROW_TILE) == 0
        and whole % (4 * LANES) == 0
        and right_n == 4 * LANES
    )


def tree_shards(rhs, inv_diag, off_diag, pair_mask):
    rows_n = lax.axis_size("row")
    leaves_n = lax.axis_size("leaf")
    whole = inv_diag.shape[3]
    right_n = rhs.shape[3]
    height = off_diag.shape[2]
    chunk = right_n // CHUNKS
    hs = [height // 2**m for m in range(TREE_LEVELS + 1)]
    bf16, f32 = jnp.bfloat16, jnp.float32
    vm = pltpu.VMEM
    scratch = [
        vm((height, whole), bf16),
        vm((2, hs[1], whole), bf16), vm((4, hs[2], whole), bf16), vm((8, hs[3], whole), bf16),
        vm((height, whole), bf16), vm((height, whole + whole // 2), bf16),
        vm((height, whole + whole // 2 + whole // 4), bf16),
        vm((CHUNKS, 2, hs[1], LANES), bf16), vm((4, hs[2], LANES), bf16), vm((8, hs[3], LANES), bf16),
        vm((CHUNKS, rows_n, height, chunk), bf16),
        vm((CHUNKS, 2, rows_n, hs[1], LANES), bf16),
        vm((4, rows_n, hs[2], LANES), bf16),
        vm((4, rows_n, hs[3], LANES), bf16),
        vm((CHUNKS, rows_n, height, chunk), bf16),
        vm((CHUNKS, rows_n, hs[1], chunk), bf16),
        vm((rows_n, hs[2], right_n), bf16),
        vm((CHUNKS, height, chunk), f32), vm((height, right_n), f32), vm((height, right_n), f32),
        vm((CHUNKS, height, chunk), bf16), vm((height, right_n), bf16),
        vm((leaves_n, height // 2, LANES), bf16),
        vm((CHUNKS, 1, height, LANES), bf16), vm((3, height, LANES), bf16),
        vm((leaves_n - 1, height // 2, LANES), bf16),
        vm((CHUNKS, 2, hs[1], LANES), bf16), vm((4, hs[2], LANES), bf16),
        vm((leaves_n, hs[3], LANES), bf16), vm((leaves_n, hs[3], LANES), bf16),
        pltpu.SemaphoreType.DMA((len(GATHERS), rows_n)),
        pltpu.SemaphoreType.DMA((len(GATHERS), rows_n)),
        pltpu.SemaphoreType.DMA((len(GATHERS), rows_n)),
        pltpu.SemaphoreType.DMA((len(SWAPS), leaves_n)),
        pltpu.SemaphoreType.DMA((len(SWAPS), leaves_n)),
        pltpu.SemaphoreType.DMA((len(LOCALS),)),
        pltpu.SemaphoreType.DMA((4, rows_n)),
        pltpu.SemaphoreType.DMA((4, rows_n)),
    ]
    pack = rhs.shape[2]
    flops = 2 * right_n * (pack * whole + height * off_diag.shape[3])
    moved = 2 * (pack * whole + height * off_diag.shape[3] + 3 * pack * right_n)
    solved = pl.pallas_call(
        functools.partial(tree_kernel, rows_n, leaves_n),
        out_shape=jax.ShapeDtypeStruct((pack, right_n), f32),
        in_specs=[pl.BlockSpec(memory_space=pltpu.SMEM)] + [pl.BlockSpec(memory_space=pltpu.HBM)] * 3,
        out_specs=pl.BlockSpec(memory_space=pltpu.VMEM),
        scratch_shapes=scratch,
        compiler_params=pltpu.CompilerParams(
            collective_id=0, has_side_effects=True, vmem_limit_bytes=125 * 2**19),
        cost_estimate=pl.CostEstimate(flops=flops, bytes_accessed=moved, transcendentals=0),
    )(pair_mask[0, 0], rhs[0, 0], inv_diag[0, 0], off_diag[0, 0])
    return solved[None, None]


def solution(mesh):
    in_specs = (
        P("leaf", "row", None, None),
        P("leaf", "row", None, None),
        P("leaf", "row", None, None),
        P("leaf", "row", None),
    )
    out_specs = P("leaf", "row", None, None)

    def run(rhs, inv_diag, off_diag, pair_mask):
        fit = fits(mesh.shape["row"], mesh.shape["leaf"], rhs, inv_diag, off_diag)
        body = tree_shards if fit else shards
        return jax.shard_map(body, mesh=mesh, in_specs=in_specs, out_specs=out_specs, check_vma=False)(
            rhs, inv_diag, off_diag, pair_mask
        )

    return run
```

```python
import functools

import jax
import jax.numpy as jnp
from jax import lax
from jax.experimental import pallas as pl
from jax.experimental.pallas import tpu as pltpu
from jax.sharding import PartitionSpec as P

LANES = 128
ROW_TILE = 16
CHUNKS = 2
TREE_LEVELS = 3
MESH = pl.DeviceIdType.MESH


def partner_2(block, axis, bit):
    count = lax.axis_size(axis)
    route = []
    for low in range(count):
        high = low | 1 << bit
        if high != low and high < count:
            route += [(low, high), (high, low)]
    return lax.ppermute(block, axis, route)


def column_start(ancestor, width_all):
    offset = 0
    for higher in range(1, ancestor):
        for within in range(higher):
            offset += width_all // 2**within
    return offset


def shards(rhs, inv_diag, off_diag, pair_mask):
    rows_n = lax.axis_size("row")
    leaves = lax.axis_size("leaf")
    levels_n = leaves.bit_length() - 1
    leaf_index = lax.axis_index("leaf")
    width_all = inv_diag.shape[3]
    right_all = rhs[0, 0]
    inverse_all = inv_diag[0, 0]
    panels = off_diag[0, 0]
    live_pairs = pair_mask[0, 0].astype(jnp.bfloat16)
    known_parts = []
    outputs = []
    offset = 0
    for ancestor in range(levels_n + 1):
        height = width_all // (2**ancestor * rows_n)
        own_rhs = right_all[offset : offset + height]
        own_inv = inverse_all[offset : offset + height]
        offset += height
        if ancestor > 0:
            stacked = jnp.concatenate(
                [
                    known_parts[source] * live_pairs[ancestor * (ancestor - 1) // 2 + source]
                    for source in range(ancestor)
                ],
                axis=0,
            )
            first_col = column_start(ancestor, width_all)
            span_cols = stacked.shape[0]
            update = jnp.dot(
                panels[:, first_col : first_col + span_cols],
                stacked,
                preferred_element_type=jnp.float32,
            )
        if ancestor > 0:
            current = update
            for bit_pos in reversed(range(ancestor)):
                half_rows = current.shape[0] // 2
                upper_half = leaf_index // 2**bit_pos % 2 == 1
                kept_rows = jnp.where(upper_half, current[half_rows:], current[:half_rows])
                sent_rows = jnp.where(upper_half, current[:half_rows], current[half_rows:])
                current = kept_rows + partner_2(
                    sent_rows.astype(jnp.bfloat16), "leaf", bit_pos
                ).astype(sent_rows.dtype)
            reduced = (own_rhs.astype(jnp.float32) - current).astype(jnp.bfloat16)
        else:
            reduced = own_rhs
        gathered = lax.all_gather(reduced, "row", axis=0, tiled=True)
        for bit_pos in range(ancestor):
            partner = partner_2(gathered, "leaf", bit_pos)
            upper_half = leaf_index // 2**bit_pos % 2 == 1
            gathered = jnp.where(
                upper_half,
                jnp.concatenate([partner, gathered], axis=0),
                jnp.concatenate([gathered, partner], axis=0),
            )
        solved = jnp.dot(own_inv, gathered, preferred_element_type=jnp.float32)
        outputs.append(solved)
        if ancestor < levels_n:
            leaf_part = lax.all_gather(solved.astype(jnp.bfloat16), "row", axis=0, tiled=True)
            known_parts.append(leaf_part)
    return jnp.concatenate(outputs, axis=0)[None, None]


def dot32(left, right):
    return jnp.dot(left, right, preferred_element_type=jnp.float32)


GATHERS = ["z0a", "z0b", "y0a", "y0b", "z1a", "z1b", "y1a", "y1b", "z2", "z3"]
SWAPS = ["b1a", "b1b", "b2", "b3", "d1", "d2", "d3", "d2p", "d3p", "u1a", "u1b", "u2", "u3", "y1a", "y1b", "y3"]
LOCALS = ["z0a", "z0b", "d0", "p1", "p2", "p3", "d1", "d2", "d3", "b1a", "b1b", "b2", "b3"]


def tree_kernel(
    rows_n, leaves_n,
    mask, rhs, inv, pan, out,
    d0, d1, d2, d3, p1, p2, p3, b1, b2, b3,
    z0, z1, z2, z3, y0, y1, y2,
    acc, u1, u2, u3, u1s, u2s, u3s, u1r, u2r, u3r, y1s, y2s, y3s, y3r,
    up_sem, down_sem, land_sem, swap_send, swap_recv, local_sem, spread_send, spread_recv,
):
    leaf = lax.axis_index("leaf")
    row = lax.axis_index("row")
    height = p1.shape[0]
    right_n = u2.shape[1]
    chunk = right_n // CHUNKS
    heights = [height // 2**m for m in range(TREE_LEVELS + 1)]
    starts = [sum(heights[:m]) for m in range(TREE_LEVELS + 1)]
    wide = LANES
    suffix = "ab"
    pending = []
    place = [leaf % 2**m for m in range(TREE_LEVELS + 1)]
    own_chunk = leaf % 2

    def block_of(position):
        return 2 * (position % 2) + position // 2 % 2

    def at_cols(index):
        return pl.ds(pl.multiple_of(index * wide, wide), wide)

    def level_rows(m):
        return pl.ds(starts[m], heights[m])

    barrier = pltpu.get_barrier_semaphore()

    for e in range(1, rows_n):
        for d in range(4):
            pl.semaphore_signal(
                barrier, inc=1, device_id=(leaf - place[2] + (place[2] + d) % 4, (row + e) % rows_n),
                device_id_type=MESH)
    for d in range(1, leaves_n):
        pl.semaphore_signal(barrier, inc=1, device_id=((leaf + d) % leaves_n, row), device_id_type=MESH)

    def local(name, src, dst):
        return pltpu.make_async_copy(src, dst, local_sem.at[LOCALS.index(name)])

    local_copies = {}
    for c in range(CHUNKS):
        local_copies["z0" + suffix[c]] = local(
            "z0" + suffix[c], rhs.at[pl.ds(0, height), pl.ds(c * chunk, chunk)], z0.at[c, row])
    local_copies["d0"] = local("d0", inv.at[pl.ds(0, height)], d0)
    for m, held in ((1, p1), (2, p2), (3, p3)):
        local_copies["p%d" % m] = local(
            "p%d" % m, pan.at[:, pl.ds(column_start(m, d0.shape[1]), held.shape[1])], held)
    for m, held in ((1, d1), (2, d2), (3, d3)):
        local_copies["d%d" % m] = local("d%d" % m, inv.at[level_rows(m)], held.at[place[m]])
    for c in range(CHUNKS):
        local_copies["b1" + suffix[c]] = local(
            "b1" + suffix[c], rhs.at[level_rows(1), at_cols(2 * c + place[1])], b1.at[c, place[1]])
    local_copies["b2"] = local("b2", rhs.at[level_rows(2), at_cols(block_of(place[2]))], b2.at[place[2]])
    local_copies["b3"] = local("b3", rhs.at[level_rows(3), at_cols(block_of(place[3]))], b3.at[place[3]])
    for name in LOCALS:
        local_copies[name].start()

    pl.semaphore_wait(barrier, 4 * (rows_n - 1) + leaves_n - 1)

    def begin(can, make):
        if can is None:
            make().start()
        else:
            @pl.when(can)
            def _():
                make().start()
        pending.append((can, make))

    def hop(name, src, dst, step, source, order, way):
        k = GATHERS.index(name)
        sem = (up_sem, down_sem)[order]
        return pltpu.make_async_remote_copy(
            src_ref=src, dst_ref=dst, send_sem=sem.at[k, step], recv_sem=land_sem.at[k, source],
            device_id=(leaf, row + way), device_id_type=MESH)

    lead = 1 - 2 * (leaf % 2)
    ways = [(order, lead if order == 0 else -lead) for order in range(2)]

    def inside(index):
        return jnp.logical_and(index >= 0, index < rows_n)

    def gather_start(name, slot, src=None):
        for order, way in ways:
            can = inside(row + way)

            def make(order=order, way=way):
                return hop(name, slot(row) if src is None else src, slot(row), 0, row, order, way)

            @pl.when(can)
            def _(make=make):
                make().start()

            pending.append((can, make))

    def arrived(step, then):
        for _, way in ways:
            source = row - way * step

            @pl.when(inside(source))
            def _(source=source):
                then(source)

    def gather_step(name, slot, step, then=None):
        for order, way in ways:
            can = inside(row + way)
            source = row - way * step
            there = inside(source)

            def make(order=order, way=way, source=source):
                return hop(name, slot(source), slot(source), step, source, order, way)

            @pl.when(there)
            def _(make=make):
                make().wait_recv()

            if step < rows_n - 1:
                both = jnp.logical_and(there, can)

                @pl.when(both)
                def _(make=make):
                    make().start()

                pending.append((both, make))

        if then is not None:
            arrived(step, then)

    def direct(name, slot, e):
        k = GATHERS.index(name)
        return pltpu.make_async_remote_copy(
            src_ref=slot(row), dst_ref=slot(row), send_sem=up_sem.at[k, e], recv_sem=land_sem.at[k, e],
            device_id=(leaf, (row + e) % rows_n), device_id_type=MESH)

    def direct_start(name, slot, can):
        for e in range(1, rows_n):
            begin(can, lambda e=e: direct(name, slot, e))

    def direct_wait(name, slot):
        k = GATHERS.index(name)
        for e in range(1, rows_n):
            there = slot((row - e + rows_n) % rows_n)
            pltpu.make_async_remote_copy(
                src_ref=there, dst_ref=there, send_sem=up_sem.at[k, e], recv_sem=land_sem.at[k, e],
                device_id=(leaf, (row + e) % rows_n), device_id_type=MESH).wait_recv()

    def peer(m, d):
        size = 2**m
        return leaf - place[m] + (place[m] + d) % size

    def swap(name, m, d, src, dst, line=None):
        k = SWAPS.index(name)
        line = d if line is None else line
        return pltpu.make_async_remote_copy(
            src_ref=src, dst_ref=dst, send_sem=swap_send.at[k, line], recv_sem=swap_recv.at[k, line],
            device_id=(peer(m, d), row), device_id_type=MESH)

    def swap_start(name, m, src, dst, when=None, only=None):
        size = 2**m
        for d in only or range(1, size):
            target = (place[m] + d) % size

            def make(d=d, target=target):
                return swap(name, m, d, src(target), dst(place[m], d))

            begin(None if when is None else when(target), make)

    def swap_wait(name, m, src, dst, only=None):
        size = 2**m
        for d in only or range(1, size):
            sender = (place[m] - d + size) % size
            swap(name, m, d, src(place[m]), dst(sender, d)).wait_recv()

    def z0_slot(c):
        return lambda q: z0.at[c, q]

    def y0_slot(c):
        return lambda q: y0.at[c, q]

    def z1_slot(c):
        return lambda q: z1.at[c, :, q]

    def y1_slot(c):
        return lambda q: y1.at[c, q]

    def z2_slot(q):
        return z2.at[:, q]

    def z3_slot(q):
        return z3.at[:, q]

    for c in range(CHUNKS):
        gather_start("z0" + suffix[c], z0_slot(c), rhs.at[pl.ds(0, height), pl.ds(c * chunk, chunk)])

    fixed = []
    for c in range(CHUNKS):
        fixed.append((
            "b1" + suffix[c], 1,
            lambda target, c=c: rhs.at[level_rows(1), at_cols(2 * c + target)],
            lambda sender, d, c=c: b1.at[c, sender]))
    fixed.append(("d1", 1, lambda target: inv.at[level_rows(1)], lambda sender, d: d1.at[sender]))
    fixed.append(("b2", 2, lambda target: rhs.at[level_rows(2), at_cols(block_of(target))], lambda sender, d: b2.at[sender]))
    fixed.append(("d2", 2, lambda target: inv.at[level_rows(2)], lambda sender, d: d2.at[sender]))
    fixed.append(("b3", 3, lambda target: rhs.at[level_rows(3), at_cols(block_of(target))], lambda sender, d: b3.at[sender]))
    fixed.append(("d3", 3, lambda target: inv.at[level_rows(3)], lambda sender, d: d3.at[sender]))
    D2, D3 = CHUNKS + 2, CHUNKS + 4
    for k, entry in enumerate(fixed):
        if k not in (D2, D3):
            swap_start(*entry)

    def hand_over(name, held, i, mine):
        at = 2 * i + (place[1] if mine else 1 - place[1])
        return swap(name, 1, 1, held.at[at], held.at[at], i)

    def hand_all(name, held):
        for i in range(held.shape[0] // 2):
            begin(None, lambda i=i: hand_over(name, held, i, True))

    def taken_all(name, held):
        for i in range(held.shape[0] // 2):
            hand_over(name, held, i, False).wait_recv()

    def live(pair):
        return mask[pair].astype(jnp.float32)

    def cols_of(c):
        return pl.ds(c * chunk, chunk)

    whole = d0.shape[1]

    def shard_cols(source):
        return pl.ds(pl.multiple_of(source * height, LANES), height)

    def add_solved(c):
        def then(source):
            acc[c] += dot32(d0[:, shard_cols(source)], z0[c, source])
        return then

    def add_first(c):
        def then(source):
            u1[c] += dot32(p1[:, shard_cols(source)], y0[c, source]) * live(0)
        return then

    def add_rest(c):
        def then(source):
            u2[:, cols_of(c)] += dot32(p2[:, shard_cols(source)], y0[c, source]) * live(1)
            u3[:, cols_of(c)] += dot32(p3[:, shard_cols(source)], y0[c, source]) * live(3)
        return then

    def add_all(c):
        def then(source):
            add_first(c)(source)
            add_rest(c)(source)
        return then

    for c in range(CHUNKS):
        acc[c] = jnp.zeros_like(acc[c])
        u1[c] = jnp.zeros_like(u1[c])
    u2[...] = jnp.zeros_like(u2)
    u3[...] = jnp.zeros_like(u3)
    local_copies["d0"].wait()
    for c in range(CHUNKS):
        local_copies["z0" + suffix[c]].wait()
        add_solved(c)(row)
    pieces = [(D2, 2), (D3, 2), (D3, 4), (D3, 6)]
    for step in range(1, rows_n - 1):
        for c in range(CHUNKS):
            gather_step("z0" + suffix[c], z0_slot(c), step, add_solved(c))
            if pieces:
                entry, d = pieces.pop(0)
                swap_start(*fixed[entry], only=[d])
    for entry, d in pieces:
        swap_start(*fixed[entry], only=[d])
    for c in range(CHUNKS):
        gather_step("z0" + suffix[c], z0_slot(c), rows_n - 1, add_solved(c))
        solved = acc[c]
        y0[c, row] = solved.astype(jnp.bfloat16)
        gather_start("y0" + suffix[c], y0_slot(c))
        out[pl.ds(0, height), cols_of(c)] = solved
    for name in ("p1", "p2", "p3", "d2", "d3"):
        local_copies[name].wait()
    for c in range(CHUNKS):
        add_all(c)(row)
    for step in range(1, rows_n - 1):
        for c in range(CHUNKS):
            gather_step("y0" + suffix[c], y0_slot(c), step, add_all(c))
        if step == 1:
            swap_wait(*fixed[D2], only=[2])
            swap_wait(*fixed[D3], only=[2, 4, 6])
            hand_all("d2p", d2)
            hand_all("d3p", d3)

    half = whole // 2
    u1_src = [lambda target, c=c: u1s.at[c, :, at_cols(target)] for c in range(CHUNKS)]
    u1_dst = [lambda sender, d, c=c: u1r.at[c, d - 1] for c in range(CHUNKS)]
    y1_src = [lambda target, c=c: y1s.at[c, target] for c in range(CHUNKS)]
    y1_dst = [lambda sender, d, c=c: y1.at[c, row, :, at_cols(sender)] for c in range(CHUNKS)]

    def update_1(c):
        gather_step("y0" + suffix[c], y0_slot(c), rows_n - 1, add_first(c))
        u1s[c] = u1[c].astype(jnp.bfloat16)
        swap_start("u1" + suffix[c], 1, u1_src[c], u1_dst[c])

    def reduce_1(c):
        local_copies["b1" + suffix[c]].wait()
        swap_wait(*fixed[c])
        swap_wait("u1" + suffix[c], 1, u1_src[c], u1_dst[c])
        total = u1[c, :, at_cols(place[1])] + u1r[c, 0].astype(jnp.float32)
        reduced = (b1[c].reshape(height, wide).astype(jnp.float32) - total).astype(jnp.bfloat16)
        for s in range(2):
            z1[c, s, row] = reduced[s * heights[1] : (s + 1) * heights[1]]
        gather_start("z1" + suffix[c], z1_slot(c))

    def solve_1(c):
        gather_step("z1" + suffix[c], z1_slot(c), rows_n - 1)
        solved = dot32(d1[...].reshape(height, whole), z1[c].reshape(whole, wide)).astype(jnp.bfloat16)
        y1s[c] = solved.reshape(2, heights[1], wide)
        swap_start("y1" + suffix[c], 1, y1_src[c], y1_dst[c])
        y1[c, row, :, at_cols(place[1])] = y1s[c, place[1]]

    def spread_1(c):
        swap_wait("y1" + suffix[c], 1, y1_src[c], y1_dst[c])
        gather_start("y1" + suffix[c], y1_slot(c))

    u2_src = lambda target: u2s.at[:, at_cols(block_of(target))]
    u2_dst = lambda sender, d: u2r.at[d - 1]

    def update_2(c):
        gather_step("y1" + suffix[c], y1_slot(c), rows_n - 1)
        update = u2[:, cols_of(c)] + dot32(p2[:, whole:], y1[c].reshape(half, chunk)) * live(2)
        u2[:, cols_of(c)] = update
        u2s[:, cols_of(c)] = update.astype(jnp.bfloat16)
        swap_start("u2", 2, u2_src, u2_dst, lambda target: target % 2 == c)

    def later_3(c):
        u3[:, cols_of(c)] += dot32(p3[:, whole : whole + half], y1[c].reshape(half, chunk)) * live(4)

    def reduce_2(c):
        @pl.when(own_chunk == c)
        def _():
            swap_wait("u2", 2, u2_src, u2_dst)
            total = u2[:, at_cols(block_of(place[2]))]
            for d in range(3):
                total = total + u2r[d].astype(jnp.float32)
            reduced = (b2[...].reshape(height, wide).astype(jnp.float32) - total).astype(jnp.bfloat16)
            for s in range(4):
                z2[s, row] = reduced[s * heights[2] : (s + 1) * heights[2]]

        direct_start("z2", z2_slot, own_chunk == c)

    def spread(d, e, position):
        here = leaf - place[2] + (place[2] + d) % 4
        dst = y2.at[(row if position is None else (row - e + rows_n) % rows_n), :,
                    at_cols(block_of(place[2] if position is None else position))]
        src = y2s.at[(place[2] + d) % 4]
        return pltpu.make_async_remote_copy(
            src_ref=src, dst_ref=dst, send_sem=spread_send.at[d, e], recv_sem=spread_recv.at[d, e],
            device_id=(here, (row + e) % rows_n), device_id_type=MESH)

    others = [(d, e) for e in reversed(range(rows_n)) for d in range(4) if d or e]

    def solve_2(c):
        @pl.when(own_chunk == c)
        def _():
            direct_wait("z2", z2_slot)
            solved = dot32(d2[...].reshape(height, whole), z2[...].reshape(whole, wide)).astype(jnp.bfloat16)
            y2s[...] = solved.reshape(4, heights[2], wide)

        for d, e in others:
            begin(own_chunk == c, lambda d=d, e=e: spread(d, e, None))

        @pl.when(own_chunk == c)
        def _():
            y2[row, :, at_cols(block_of(place[2]))] = y2s[place[2]]

    fold = height // 2
    low = lax.broadcasted_iota(jnp.int32, (fold, wide), 1) < wide // 2

    def folded(top, bottom):
        return (
            jnp.where(low, top, pltpu.roll(bottom, wide // 2, 1)),
            jnp.where(low, pltpu.roll(top, wide // 2, 1), bottom),
        )

    u3_src = lambda target: u3s.at[target]
    u3_dst = lambda sender, d: u3r.at[d - 1]

    def update_3(c):
        for d, e in others:
            sender = (place[2] - d + 4) % 4

            @pl.when(sender % 2 == c)
            def _(d=d, e=e, sender=sender):
                spread(d, e, sender).wait_recv()

        known = y2[:, :, c * chunk : (c + 1) * chunk].reshape(whole // 4, chunk)
        update = u3[:, cols_of(c)] + dot32(p3[:, whole + half :], known) * live(5)
        for k in range(2):
            block = update[:, k * wide : (k + 1) * wide]
            sides = folded(block[:fold], block[fold:])
            for side in range(2):
                u3s[4 * side + 2 * k + c] = sides[side].astype(jnp.bfloat16)
        swap_start("u3", 3, u3_src, u3_dst, lambda target: target % 2 == c)

    def reduce_3(c):
        @pl.when(own_chunk == c)
        def _():
            own_b = b3[...].astype(jnp.float32)
            sides = folded(own_b[:4].reshape(fold, wide), own_b[4:].reshape(fold, wide))
            own_b = jnp.where(place[3] < leaves_n // 2, sides[0], sides[1])
            swap_wait("u3", 3, u3_src, u3_dst)
            total = u3s[place[3]].astype(jnp.float32)
            for d in range(leaves_n - 1):
                total = total + u3r[d].astype(jnp.float32)
            reduced = (own_b - total).astype(jnp.bfloat16)
            for s in range(4):
                z3[s, row] = reduced[s * heights[3] : (s + 1) * heights[3]]

        direct_start("z3", z3_slot, own_chunk == c)

    y3_src = lambda target: y3s.at[target]
    y3_dst = lambda sender, d: y3r.at[sender]

    def solve_3():
        direct_wait("z3", z3_slot)
        known = z3[...].reshape(half, wide)
        left = dot32(d3[:, :, :half].reshape(height, half), known)
        right = dot32(d3[:, :, half:].reshape(height, half), known)
        solved = left + pltpu.roll(right, wide // 2, 1)
        low_all = lax.broadcasted_iota(jnp.int32, (height, wide), 1) < wide // 2
        solved = jnp.where(low_all, solved, pltpu.roll(solved, wide // 2, 1))
        y3s[...] = solved.astype(jnp.bfloat16).reshape(leaves_n, heights[3], wide)
        swap_start("y3", 3, y3_src, y3_dst)
        y3r[place[3]] = y3s[place[3]]

    update_1(0)
    arrived(rows_n - 1, add_rest(0))
    reduce_1(0)
    update_1(1)
    gather_step("z1a", z1_slot(0), 1)
    reduce_1(1)
    arrived(rows_n - 1, add_rest(1))
    for step in range(2, rows_n - 1):
        gather_step("z1a", z1_slot(0), step)
        gather_step("z1b", z1_slot(1), step - 1)
    local_copies["d1"].wait()
    swap_wait(*fixed[CHUNKS])
    solve_1(0)
    gather_step("z1b", z1_slot(1), rows_n - 2)
    spread_1(0)
    solve_1(1)
    gather_step("y1a", y1_slot(0), 1)
    spread_1(1)
    for step in range(2, rows_n - 1):
        gather_step("y1a", y1_slot(0), step)
        gather_step("y1b", y1_slot(1), step - 1)
    local_copies["b2"].wait()
    swap_wait(*fixed[CHUNKS + 1])
    update_2(0)
    gather_step("y1b", y1_slot(1), rows_n - 2)
    later_3(0)
    reduce_2(0)
    update_2(1)
    taken_all("d2p", d2)
    reduce_2(1)
    later_3(1)
    for c in range(CHUNKS):
        out[level_rows(1), cols_of(c)] = y1[c, row].astype(jnp.float32)
    local_copies["b3"].wait()
    swap_wait(*fixed[CHUNKS + 3])
    taken_all("d3p", d3)
    solve_2(0)
    solve_2(1)
    update_3(0)
    reduce_3(0)
    update_3(1)
    reduce_3(1)
    out[level_rows(2), :] = y2[row].astype(jnp.float32)
    solve_3()
    swap_wait("y3", 3, y3_src, y3_dst)
    low_out = lax.broadcasted_iota(jnp.int32, (heights[3], wide), 1) < wide // 2
    for k in range(leaves_n // 2):
        first = 2 * (k % 2) + k // 2
        out[level_rows(3), pl.ds(k * wide, wide)] = jnp.where(
            low_out, y3r[first].astype(jnp.float32), y3r[first + leaves_n // 2].astype(jnp.float32))

    for can, make in pending:
        if can is None:
            make().wait_send()
        else:
            @pl.when(can)
            def _(make=make):
                make().wait_send()


def fits(rows_n, leaves_n, rhs, inv_diag, off_diag):
    whole = inv_diag.shape[3]
    right_n = rhs.shape[3]
    return (
        leaves_n == 2**TREE_LEVELS
        and rows_n > 2
        and whole % (leaves_n * rows_n * ROW_TILE) == 0
        and whole % (rows_n * LANES) == 0
        and whole % (4 * LANES) == 0
        and right_n == 4 * LANES
    )


def tree_shards(rhs, inv_diag, off_diag, pair_mask):
    rows_n = lax.axis_size("row")
    leaves_n = lax.axis_size("leaf")
    whole = inv_diag.shape[3]
    right_n = rhs.shape[3]
    height = off_diag.shape[2]
    chunk = right_n // CHUNKS
    hs = [height // 2**m for m in range(TREE_LEVELS + 1)]
    bf16, f32 = jnp.bfloat16, jnp.float32
    vm = pltpu.VMEM
    scratch = [
        vm((height, whole), bf16),
        vm((2, hs[1], whole), bf16), vm((4, hs[2], whole), bf16), vm((8, hs[3], whole), bf16),
        vm((height, whole), bf16), vm((height, whole + whole // 2), bf16),
        vm((height, whole + whole // 2 + whole // 4), bf16),
        vm((CHUNKS, 2, hs[1], LANES), bf16), vm((4, hs[2], LANES), bf16), vm((8, hs[3], LANES), bf16),
        vm((CHUNKS, rows_n, height, chunk), bf16),
        vm((CHUNKS, 2, rows_n, hs[1], LANES), bf16),
        vm((4, rows_n, hs[2], LANES), bf16),
        vm((4, rows_n, hs[3], LANES), bf16),
        vm((CHUNKS, rows_n, height, chunk), bf16),
        vm((CHUNKS, rows_n, hs[1], chunk), bf16),
        vm((rows_n, hs[2], right_n), bf16),
        vm((CHUNKS, height, chunk), f32),
        vm((CHUNKS, height, chunk), f32), vm((height, right_n), f32), vm((height, right_n), f32),
        vm((CHUNKS, height, chunk), bf16), vm((height, right_n), bf16),
        vm((leaves_n, height // 2, LANES), bf16),
        vm((CHUNKS, 1, height, LANES), bf16), vm((3, height, LANES), bf16),
        vm((leaves_n - 1, height // 2, LANES), bf16),
        vm((CHUNKS, 2, hs[1], LANES), bf16), vm((4, hs[2], LANES), bf16),
        vm((leaves_n, hs[3], LANES), bf16), vm((leaves_n, hs[3], LANES), bf16),
        pltpu.SemaphoreType.DMA((len(GATHERS), rows_n)),
        pltpu.SemaphoreType.DMA((len(GATHERS), rows_n)),
        pltpu.SemaphoreType.DMA((len(GATHERS), rows_n)),
        pltpu.SemaphoreType.DMA((len(SWAPS), leaves_n)),
        pltpu.SemaphoreType.DMA((len(SWAPS), leaves_n)),
        pltpu.SemaphoreType.DMA((len(LOCALS),)),
        pltpu.SemaphoreType.DMA((4, rows_n)),
        pltpu.SemaphoreType.DMA((4, rows_n)),
    ]
    pack = rhs.shape[2]
    flops = 2 * right_n * (pack * whole + height * off_diag.shape[3])
    moved = 2 * (pack * whole + height * off_diag.shape[3] + 3 * pack * right_n)
    solved = pl.pallas_call(
        functools.partial(tree_kernel, rows_n, leaves_n),
        out_shape=jax.ShapeDtypeStruct((pack, right_n), f32),
        in_specs=[pl.BlockSpec(memory_space=pltpu.SMEM)] + [pl.BlockSpec(memory_space=pltpu.HBM)] * 3,
        out_specs=pl.BlockSpec(memory_space=pltpu.VMEM),
        scratch_shapes=scratch,
        compiler_params=pltpu.CompilerParams(
            collective_id=0, has_side_effects=True, vmem_limit_bytes=62 * 2**20),
        cost_estimate=pl.CostEstimate(flops=flops, bytes_accessed=moved, transcendentals=0),
    )(pair_mask[0, 0], rhs[0, 0], inv_diag[0, 0], off_diag[0, 0])
    return solved[None, None]


def solution(mesh):
    in_specs = (
        P("leaf", "row", None, None),
        P("leaf", "row", None, None),
        P("leaf", "row", None, None),
        P("leaf", "row", None),
    )
    out_specs = P("leaf", "row", None, None)

    def run(rhs, inv_diag, off_diag, pair_mask):
        fit = fits(mesh.shape["row"], mesh.shape["leaf"], rhs, inv_diag, off_diag)
        body = tree_shards if fit else shards
        return jax.shard_map(body, mesh=mesh, in_specs=in_specs, out_specs=out_specs, check_vma=False)(
            rhs, inv_diag, off_diag, pair_mask
        )

    return run
```

```python
import functools

import jax
import jax.numpy as jnp
from jax import lax
from jax.experimental import pallas as pl
from jax.experimental.pallas import tpu as pltpu
from jax.sharding import PartitionSpec as P

LANES = 128
ROW_TILE = 16
CHUNKS = 2
TREE_LEVELS = 3
MESH = pl.DeviceIdType.MESH
REACH = 2


def partner_2(block, axis, bit):
    count = lax.axis_size(axis)
    route = []
    for low in range(count):
        high = low | 1 << bit
        if high != low and high < count:
            route += [(low, high), (high, low)]
    return lax.ppermute(block, axis, route)


def column_start(ancestor, width_all):
    offset = 0
    for higher in range(1, ancestor):
        for within in range(higher):
            offset += width_all // 2**within
    return offset


def shards(rhs, inv_diag, off_diag, pair_mask):
    rows_n = lax.axis_size("row")
    leaves = lax.axis_size("leaf")
    levels_n = leaves.bit_length() - 1
    leaf_index = lax.axis_index("leaf")
    width_all = inv_diag.shape[3]
    right_all = rhs[0, 0]
    inverse_all = inv_diag[0, 0]
    panels = off_diag[0, 0]
    live_pairs = pair_mask[0, 0].astype(jnp.bfloat16)
    known_parts = []
    outputs = []
    offset = 0
    for ancestor in range(levels_n + 1):
        height = width_all // (2**ancestor * rows_n)
        own_rhs = right_all[offset : offset + height]
        own_inv = inverse_all[offset : offset + height]
        offset += height
        if ancestor > 0:
            stacked = jnp.concatenate(
                [
                    known_parts[source] * live_pairs[ancestor * (ancestor - 1) // 2 + source]
                    for source in range(ancestor)
                ],
                axis=0,
            )
            first_col = column_start(ancestor, width_all)
            span_cols = stacked.shape[0]
            update = jnp.dot(
                panels[:, first_col : first_col + span_cols],
                stacked,
                preferred_element_type=jnp.float32,
            )
        if ancestor > 0:
            current = update
            for bit_pos in reversed(range(ancestor)):
                half_rows = current.shape[0] // 2
                upper_half = leaf_index // 2**bit_pos % 2 == 1
                kept_rows = jnp.where(upper_half, current[half_rows:], current[:half_rows])
                sent_rows = jnp.where(upper_half, current[:half_rows], current[half_rows:])
                current = kept_rows + partner_2(
                    sent_rows.astype(jnp.bfloat16), "leaf", bit_pos
                ).astype(sent_rows.dtype)
            reduced = (own_rhs.astype(jnp.float32) - current).astype(jnp.bfloat16)
        else:
            reduced = own_rhs
        gathered = lax.all_gather(reduced, "row", axis=0, tiled=True)
        for bit_pos in range(ancestor):
            partner = partner_2(gathered, "leaf", bit_pos)
            upper_half = leaf_index // 2**bit_pos % 2 == 1
            gathered = jnp.where(
                upper_half,
                jnp.concatenate([partner, gathered], axis=0),
                jnp.concatenate([gathered, partner], axis=0),
            )
        solved = jnp.dot(own_inv, gathered, preferred_element_type=jnp.float32)
        outputs.append(solved)
        if ancestor < levels_n:
            leaf_part = lax.all_gather(solved.astype(jnp.bfloat16), "row", axis=0, tiled=True)
            known_parts.append(leaf_part)
    return jnp.concatenate(outputs, axis=0)[None, None]


def dot32(left, right):
    return jnp.dot(left, right, preferred_element_type=jnp.float32)


GATHERS = ["z0a", "z0b", "y0a", "y0b", "z1a", "z1b", "y1a", "y1b", "z2", "z3"]
SWAPS = ["b1a", "b1b", "b2", "b3", "d1", "d2", "d3", "d2p", "d3p", "u1a", "u1b", "u2", "u3", "y1a", "y1b", "y3"]
LOCALS = ["z0a", "z0b", "d0", "p1", "p2", "p3", "d1", "d2", "d3", "b1a", "b1b", "b2", "b3"]


def tree_kernel(
    rows_n, leaves_n,
    mask, rhs, inv, pan, out,
    d0, d1, d2, d3, p1, p2, p3, b1, b2, b3,
    z0, z1, z2, z3, y0, y1, y2,
    acc, u1, u2, u3, u1s, u2s, u3s, u1r, u2r, u3r, y1s, y2s, y3s, y3r,
    up_sem, down_sem, land_sem, swap_send, swap_recv, local_sem, spread_send, spread_recv,
):
    leaf = lax.axis_index("leaf")
    row = lax.axis_index("row")
    height = p1.shape[0]
    right_n = u2.shape[1]
    chunk = right_n // CHUNKS
    heights = [height // 2**m for m in range(TREE_LEVELS + 1)]
    starts = [sum(heights[:m]) for m in range(TREE_LEVELS + 1)]
    wide = LANES
    suffix = "ab"
    pending = []
    place = [leaf % 2**m for m in range(TREE_LEVELS + 1)]
    own_chunk = leaf % 2

    def block_of(position):
        return 2 * (position % 2) + position // 2 % 2

    def at_cols(index):
        return pl.ds(pl.multiple_of(index * wide, wide), wide)

    def level_rows(m):
        return pl.ds(starts[m], heights[m])

    barrier = pltpu.get_barrier_semaphore()

    for e in range(1, rows_n):
        for d in range(4):
            pl.semaphore_signal(
                barrier, inc=1, device_id=(leaf - place[2] + (place[2] + d) % 4, (row + e) % rows_n),
                device_id_type=MESH)
    for d in range(1, leaves_n):
        pl.semaphore_signal(barrier, inc=1, device_id=((leaf + d) % leaves_n, row), device_id_type=MESH)

    def local(name, src, dst):
        return pltpu.make_async_copy(src, dst, local_sem.at[LOCALS.index(name)])

    local_copies = {}
    for c in range(CHUNKS):
        local_copies["z0" + suffix[c]] = local(
            "z0" + suffix[c], rhs.at[pl.ds(0, height), pl.ds(c * chunk, chunk)], z0.at[c, row])
    local_copies["d0"] = local("d0", inv.at[pl.ds(0, height)], d0)
    for m, held in ((1, p1), (2, p2), (3, p3)):
        local_copies["p%d" % m] = local(
            "p%d" % m, pan.at[:, pl.ds(column_start(m, d0.shape[1]), held.shape[1])], held)
    for m, held in ((1, d1), (2, d2), (3, d3)):
        local_copies["d%d" % m] = local("d%d" % m, inv.at[level_rows(m)], held.at[place[m]])
    for c in range(CHUNKS):
        local_copies["b1" + suffix[c]] = local(
            "b1" + suffix[c], rhs.at[level_rows(1), at_cols(2 * c + place[1])], b1.at[c, place[1]])
    local_copies["b2"] = local("b2", rhs.at[level_rows(2), at_cols(block_of(place[2]))], b2.at[place[2]])
    local_copies["b3"] = local("b3", rhs.at[level_rows(3), at_cols(block_of(place[3]))], b3.at[place[3]])
    for name in LOCALS:
        local_copies[name].start()

    pl.semaphore_wait(barrier, 4 * (rows_n - 1) + leaves_n - 1)

    def begin(can, make):
        if can is None:
            make().start()
        else:
            @pl.when(can)
            def _():
                make().start()
        pending.append((can, make))

    def hop(name, src, dst, step, source, order, way, far=1):
        k = GATHERS.index(name)
        sem = (up_sem, down_sem)[order]
        return pltpu.make_async_remote_copy(
            src_ref=src, dst_ref=dst, send_sem=sem.at[k, step], recv_sem=land_sem.at[k, source],
            device_id=(leaf, row + way * far), device_id_type=MESH)

    lead = 1 - 2 * (leaf % 2)
    ways = [(order, lead if order == 0 else -lead) for order in range(2)]

    def inside(index):
        return jnp.logical_and(index >= 0, index < rows_n)

    def gather_start(name, slot, src=None):
        for far, (order, way) in [(far, pair) for far in reversed(range(1, REACH + 1)) for pair in ways]:
            can = inside(row + way * far)

            def make(order=order, way=way, far=far):
                return hop(name, slot(row) if src is None else src, slot(row), far - 1, row, order, way, far)

            begin(can, make)

    def arrived(step, then):
        for _, way in ways:
            source = row - way * step

            @pl.when(inside(source))
            def _(source=source):
                then(source)

    def gather_step(name, slot, step, then=None):
        for order, way in ways:
            can = inside(row + way)
            source = row - way * step
            there = inside(source)

            def make(order=order, way=way, source=source):
                return hop(name, slot(source), slot(source), step, source, order, way)

            @pl.when(there)
            def _(make=make):
                make().wait_recv()

            if REACH <= step < rows_n - 1:
                both = jnp.logical_and(there, can)

                @pl.when(both)
                def _(make=make):
                    make().start()

                pending.append((both, make))

        if then is not None:
            arrived(step, then)

    def direct(name, slot, e):
        k = GATHERS.index(name)
        return pltpu.make_async_remote_copy(
            src_ref=slot(row), dst_ref=slot(row), send_sem=up_sem.at[k, e], recv_sem=land_sem.at[k, e],
            device_id=(leaf, (row + e) % rows_n), device_id_type=MESH)

    def direct_start(name, slot, can):
        for e in range(1, rows_n):
            begin(can, lambda e=e: direct(name, slot, e))

    def direct_wait(name, slot):
        k = GATHERS.index(name)
        for e in range(1, rows_n):
            there = slot((row - e + rows_n) % rows_n)
            pltpu.make_async_remote_copy(
                src_ref=there, dst_ref=there, send_sem=up_sem.at[k, e], recv_sem=land_sem.at[k, e],
                device_id=(leaf, (row + e) % rows_n), device_id_type=MESH).wait_recv()

    def peer(m, d):
        size = 2**m
        return leaf - place[m] + (place[m] + d) % size

    def swap(name, m, d, src, dst, line=None):
        k = SWAPS.index(name)
        line = d if line is None else line
        return pltpu.make_async_remote_copy(
            src_ref=src, dst_ref=dst, send_sem=swap_send.at[k, line], recv_sem=swap_recv.at[k, line],
            device_id=(peer(m, d), row), device_id_type=MESH)

    def swap_start(name, m, src, dst, when=None, only=None):
        size = 2**m
        for d in only or range(1, size):
            target = (place[m] + d) % size

            def make(d=d, target=target):
                return swap(name, m, d, src(target), dst(place[m], d))

            begin(None if when is None else when(target), make)

    def swap_wait(name, m, src, dst, only=None):
        size = 2**m
        for d in only or range(1, size):
            sender = (place[m] - d + size) % size
            swap(name, m, d, src(place[m]), dst(sender, d)).wait_recv()

    def z0_slot(c):
        return lambda q: z0.at[c, q]

    def y0_slot(c):
        return lambda q: y0.at[c, q]

    def z1_slot(c):
        return lambda q: z1.at[c, :, q]

    def y1_slot(c):
        return lambda q: y1.at[c, q]

    def z2_slot(q):
        return z2.at[:, q]

    def z3_slot(q):
        return z3.at[:, q]

    for c in range(CHUNKS):
        gather_start("z0" + suffix[c], z0_slot(c), rhs.at[pl.ds(0, height), pl.ds(c * chunk, chunk)])

    fixed = []
    for c in range(CHUNKS):
        fixed.append((
            "b1" + suffix[c], 1,
            lambda target, c=c: rhs.at[level_rows(1), at_cols(2 * c + target)],
            lambda sender, d, c=c: b1.at[c, sender]))
    fixed.append(("d1", 1, lambda target: inv.at[level_rows(1)], lambda sender, d: d1.at[sender]))
    fixed.append(("b2", 2, lambda target: rhs.at[level_rows(2), at_cols(block_of(target))], lambda sender, d: b2.at[sender]))
    fixed.append(("d2", 2, lambda target: inv.at[level_rows(2)], lambda sender, d: d2.at[sender]))
    fixed.append(("b3", 3, lambda target: rhs.at[level_rows(3), at_cols(block_of(target))], lambda sender, d: b3.at[sender]))
    fixed.append(("d3", 3, lambda target: inv.at[level_rows(3)], lambda sender, d: d3.at[sender]))
    D2, D3 = CHUNKS + 2, CHUNKS + 4
    for k, entry in enumerate(fixed):
        if k not in (D2, D3):
            swap_start(*entry)

    def hand_over(name, held, i, mine):
        at = 2 * i + (place[1] if mine else 1 - place[1])
        return swap(name, 1, 1, held.at[at], held.at[at], i)

    def hand_all(name, held):
        for i in range(held.shape[0] // 2):
            begin(None, lambda i=i: hand_over(name, held, i, True))

    def taken_all(name, held):
        for i in range(held.shape[0] // 2):
            hand_over(name, held, i, False).wait_recv()

    def live(pair):
        return mask[pair].astype(jnp.float32)

    def cols_of(c):
        return pl.ds(c * chunk, chunk)

    whole = d0.shape[1]

    def shard_cols(source):
        return pl.ds(pl.multiple_of(source * height, LANES), height)

    def add_solved(c):
        def then(source):
            acc[c] += dot32(d0[:, shard_cols(source)], z0[c, source])
        return then

    def add_first(c):
        def then(source):
            u1[c] += dot32(p1[:, shard_cols(source)], y0[c, source]) * live(0)
        return then

    def add_rest(c):
        def then(source):
            u2[:, cols_of(c)] += dot32(p2[:, shard_cols(source)], y0[c, source]) * live(1)
            u3[:, cols_of(c)] += dot32(p3[:, shard_cols(source)], y0[c, source]) * live(3)
        return then

    def add_all(c):
        def then(source):
            add_first(c)(source)
            add_rest(c)(source)
        return then

    for c in range(CHUNKS):
        acc[c] = jnp.zeros_like(acc[c])
        u1[c] = jnp.zeros_like(u1[c])
    u2[...] = jnp.zeros_like(u2)
    u3[...] = jnp.zeros_like(u3)
    local_copies["d0"].wait()
    for c in range(CHUNKS):
        local_copies["z0" + suffix[c]].wait()
        add_solved(c)(row)
    pieces = [(D2, 2), (D3, 2), (D3, 4), (D3, 6)]
    for step in range(1, rows_n - 1):
        for c in range(CHUNKS):
            gather_step("z0" + suffix[c], z0_slot(c), step, add_solved(c))
            if pieces:
                entry, d = pieces.pop(0)
                swap_start(*fixed[entry], only=[d])
    for entry, d in pieces:
        swap_start(*fixed[entry], only=[d])
    for c in range(CHUNKS):
        gather_step("z0" + suffix[c], z0_slot(c), rows_n - 1, add_solved(c))
        solved = acc[c]
        y0[c, row] = solved.astype(jnp.bfloat16)
        gather_start("y0" + suffix[c], y0_slot(c))
        out[pl.ds(0, height), cols_of(c)] = y0[c, row]
    for name in ("p1", "p2", "p3", "d2", "d3"):
        local_copies[name].wait()
    for c in range(CHUNKS):
        add_all(c)(row)
    for step in range(1, rows_n - 1):
        for c in range(CHUNKS):
            gather_step("y0" + suffix[c], y0_slot(c), step, add_all(c))
        if step == 1:
            swap_wait(*fixed[D2], only=[2])
            swap_wait(*fixed[D3], only=[2, 4, 6])
            hand_all("d2p", d2)
            hand_all("d3p", d3)

    half = whole // 2
    u1_src = [lambda target, c=c: u1s.at[c, :, at_cols(target)] for c in range(CHUNKS)]
    u1_dst = [lambda sender, d, c=c: u1r.at[c, d - 1] for c in range(CHUNKS)]
    y1_src = [lambda target, c=c: y1s.at[c, target] for c in range(CHUNKS)]
    y1_dst = [lambda sender, d, c=c: y1.at[c, row, :, at_cols(sender)] for c in range(CHUNKS)]

    def update_1(c):
        gather_step("y0" + suffix[c], y0_slot(c), rows_n - 1, add_first(c))
        u1s[c] = u1[c].astype(jnp.bfloat16)
        swap_start("u1" + suffix[c], 1, u1_src[c], u1_dst[c])

    def reduce_1(c):
        local_copies["b1" + suffix[c]].wait()
        swap_wait(*fixed[c])
        swap_wait("u1" + suffix[c], 1, u1_src[c], u1_dst[c])
        total = u1[c, :, at_cols(place[1])] + u1r[c, 0].astype(jnp.float32)
        reduced = (b1[c].reshape(height, wide).astype(jnp.float32) - total).astype(jnp.bfloat16)
        for s in range(2):
            z1[c, s, row] = reduced[s * heights[1] : (s + 1) * heights[1]]
        gather_start("z1" + suffix[c], z1_slot(c))

    def solve_1(c):
        gather_step("z1" + suffix[c], z1_slot(c), rows_n - 1)
        solved = dot32(d1[...].reshape(height, whole), z1[c].reshape(whole, wide)).astype(jnp.bfloat16)
        y1s[c] = solved.reshape(2, heights[1], wide)
        swap_start("y1" + suffix[c], 1, y1_src[c], y1_dst[c])
        y1[c, row, :, at_cols(place[1])] = y1s[c, place[1]]

    def spread_1(c):
        swap_wait("y1" + suffix[c], 1, y1_src[c], y1_dst[c])
        gather_start("y1" + suffix[c], y1_slot(c))

    u2_src = lambda target: u2s.at[:, at_cols(block_of(target))]
    u2_dst = lambda sender, d: u2r.at[d - 1]

    def update_2(c):
        gather_step("y1" + suffix[c], y1_slot(c), rows_n - 1)
        update = u2[:, cols_of(c)] + dot32(p2[:, whole:], y1[c].reshape(half, chunk)) * live(2)
        u2[:, cols_of(c)] = update
        u2s[:, cols_of(c)] = update.astype(jnp.bfloat16)
        swap_start("u2", 2, u2_src, u2_dst, lambda target: target % 2 == c)

    def later_3(c):
        u3[:, cols_of(c)] += dot32(p3[:, whole : whole + half], y1[c].reshape(half, chunk)) * live(4)

    def reduce_2(c):
        @pl.when(own_chunk == c)
        def _():
            swap_wait("u2", 2, u2_src, u2_dst)
            total = u2[:, at_cols(block_of(place[2]))]
            for d in range(3):
                total = total + u2r[d].astype(jnp.float32)
            reduced = (b2[...].reshape(height, wide).astype(jnp.float32) - total).astype(jnp.bfloat16)
            for s in range(4):
                z2[s, row] = reduced[s * heights[2] : (s + 1) * heights[2]]

        direct_start("z2", z2_slot, own_chunk == c)

    def spread(d, e, position):
        here = leaf - place[2] + (place[2] + d) % 4
        dst = y2.at[(row if position is None else (row - e + rows_n) % rows_n), :,
                    at_cols(block_of(place[2] if position is None else position))]
        src = y2s.at[(place[2] + d) % 4]
        return pltpu.make_async_remote_copy(
            src_ref=src, dst_ref=dst, send_sem=spread_send.at[d, e], recv_sem=spread_recv.at[d, e],
            device_id=(here, (row + e) % rows_n), device_id_type=MESH)

    others = [(d, e) for e in reversed(range(rows_n)) for d in range(4) if d or e]

    def solve_2(c):
        @pl.when(own_chunk == c)
        def _():
            direct_wait("z2", z2_slot)
            solved = dot32(d2[...].reshape(height, whole), z2[...].reshape(whole, wide)).astype(jnp.bfloat16)
            y2s[...] = solved.reshape(4, heights[2], wide)

        for d, e in others:
            begin(own_chunk == c, lambda d=d, e=e: spread(d, e, None))

        @pl.when(own_chunk == c)
        def _():
            y2[row, :, at_cols(block_of(place[2]))] = y2s[place[2]]

    fold = height // 2
    low = lax.broadcasted_iota(jnp.int32, (fold, wide), 1) < wide // 2

    def folded(top, bottom):
        return (
            jnp.where(low, top, pltpu.roll(bottom, wide // 2, 1)),
            jnp.where(low, pltpu.roll(top, wide // 2, 1), bottom),
        )

    u3_src = lambda target: u3s.at[target]
    u3_dst = lambda sender, d: u3r.at[d - 1]

    def update_3(c):
        for d, e in others:
            sender = (place[2] - d + 4) % 4

            @pl.when(sender % 2 == c)
            def _(d=d, e=e, sender=sender):
                spread(d, e, sender).wait_recv()

        known = y2[:, :, c * chunk : (c + 1) * chunk].reshape(whole // 4, chunk)
        update = u3[:, cols_of(c)] + dot32(p3[:, whole + half :], known) * live(5)
        for k in range(2):
            block = update[:, k * wide : (k + 1) * wide]
            sides = folded(block[:fold], block[fold:])
            for side in range(2):
                u3s[4 * side + 2 * k + c] = sides[side].astype(jnp.bfloat16)
        swap_start("u3", 3, u3_src, u3_dst, lambda target: target % 2 == c)

    def reduce_3(c):
        @pl.when(own_chunk == c)
        def _():
            own_b = b3[...].astype(jnp.float32)
            sides = folded(own_b[:4].reshape(fold, wide), own_b[4:].reshape(fold, wide))
            own_b = jnp.where(place[3] < leaves_n // 2, sides[0], sides[1])
            swap_wait("u3", 3, u3_src, u3_dst)
            total = u3s[place[3]].astype(jnp.float32)
            for d in range(leaves_n - 1):
                total = total + u3r[d].astype(jnp.float32)
            reduced = (own_b - total).astype(jnp.bfloat16)
            for s in range(4):
                z3[s, row] = reduced[s * heights[3] : (s + 1) * heights[3]]

        direct_start("z3", z3_slot, own_chunk == c)

    y3_src = lambda target: y3s.at[target]
    y3_dst = lambda sender, d: y3r.at[sender]

    def solve_3():
        direct_wait("z3", z3_slot)
        known = z3[...].reshape(half, wide)
        left = dot32(d3[:, :, :half].reshape(height, half), known)
        right = dot32(d3[:, :, half:].reshape(height, half), known)
        solved = left + pltpu.roll(right, wide // 2, 1)
        low_all = lax.broadcasted_iota(jnp.int32, (height, wide), 1) < wide // 2
        solved = jnp.where(low_all, solved, pltpu.roll(solved, wide // 2, 1))
        y3s[...] = solved.astype(jnp.bfloat16).reshape(leaves_n, heights[3], wide)
        swap_start("y3", 3, y3_src, y3_dst)
        y3r[place[3]] = y3s[place[3]]

    update_1(0)
    arrived(rows_n - 1, add_rest(0))
    reduce_1(0)
    update_1(1)
    gather_step("z1a", z1_slot(0), 1)
    reduce_1(1)
    arrived(rows_n - 1, add_rest(1))
    for step in range(2, rows_n - 1):
        gather_step("z1a", z1_slot(0), step)
        gather_step("z1b", z1_slot(1), step - 1)
    local_copies["d1"].wait()
    swap_wait(*fixed[CHUNKS])
    solve_1(0)
    gather_step("z1b", z1_slot(1), rows_n - 2)
    spread_1(0)
    solve_1(1)
    gather_step("y1a", y1_slot(0), 1)
    spread_1(1)
    for step in range(2, rows_n - 1):
        gather_step("y1a", y1_slot(0), step)
        gather_step("y1b", y1_slot(1), step - 1)
    local_copies["b2"].wait()
    swap_wait(*fixed[CHUNKS + 1])
    update_2(0)
    gather_step("y1b", y1_slot(1), rows_n - 2)
    later_3(0)
    reduce_2(0)
    update_2(1)
    taken_all("d2p", d2)
    reduce_2(1)
    later_3(1)
    for c in range(CHUNKS):
        out[level_rows(1), cols_of(c)] = y1[c, row]
    local_copies["b3"].wait()
    swap_wait(*fixed[CHUNKS + 3])
    taken_all("d3p", d3)
    solve_2(0)
    solve_2(1)
    update_3(0)
    reduce_3(0)
    update_3(1)
    reduce_3(1)
    out[level_rows(2), :] = y2[row]
    solve_3()
    swap_wait("y3", 3, y3_src, y3_dst)
    low_out = lax.broadcasted_iota(jnp.int32, (heights[3], wide), 1) < wide // 2
    for k in range(leaves_n // 2):
        first = 2 * (k % 2) + k // 2
        out[level_rows(3), pl.ds(k * wide, wide)] = jnp.where(
            low_out, y3r[first].astype(jnp.float32), y3r[first + leaves_n // 2].astype(jnp.float32)
        ).astype(jnp.bfloat16)

    for can, make in pending:
        if can is None:
            make().wait_send()
        else:
            @pl.when(can)
            def _(make=make):
                make().wait_send()


def fits(rows_n, leaves_n, rhs, inv_diag, off_diag):
    whole = inv_diag.shape[3]
    right_n = rhs.shape[3]
    return (
        leaves_n == 2**TREE_LEVELS
        and rows_n > 2
        and whole % (leaves_n * rows_n * ROW_TILE) == 0
        and whole % (rows_n * LANES) == 0
        and whole % (4 * LANES) == 0
        and right_n == 4 * LANES
    )


def tree_shards(rhs, inv_diag, off_diag, pair_mask):
    rows_n = lax.axis_size("row")
    leaves_n = lax.axis_size("leaf")
    whole = inv_diag.shape[3]
    right_n = rhs.shape[3]
    height = off_diag.shape[2]
    chunk = right_n // CHUNKS
    hs = [height // 2**m for m in range(TREE_LEVELS + 1)]
    bf16, f32 = jnp.bfloat16, jnp.float32
    vm = pltpu.VMEM
    scratch = [
        vm((height, whole), bf16),
        vm((2, hs[1], whole), bf16), vm((4, hs[2], whole), bf16), vm((8, hs[3], whole), bf16),
        vm((height, whole), bf16), vm((height, whole + whole // 2), bf16),
        vm((height, whole + whole // 2 + whole // 4), bf16),
        vm((CHUNKS, 2, hs[1], LANES), bf16), vm((4, hs[2], LANES), bf16), vm((8, hs[3], LANES), bf16),
        vm((CHUNKS, rows_n, height, chunk), bf16),
        vm((CHUNKS, 2, rows_n, hs[1], LANES), bf16),
        vm((4, rows_n, hs[2], LANES), bf16),
        vm((4, rows_n, hs[3], LANES), bf16),
        vm((CHUNKS, rows_n, height, chunk), bf16),
        vm((CHUNKS, rows_n, hs[1], chunk), bf16),
        vm((rows_n, hs[2], right_n), bf16),
        vm((CHUNKS, height, chunk), f32),
        vm((CHUNKS, height, chunk), f32), vm((height, right_n), f32), vm((height, right_n), f32),
        vm((CHUNKS, height, chunk), bf16), vm((height, right_n), bf16),
        vm((leaves_n, height // 2, LANES), bf16),
        vm((CHUNKS, 1, height, LANES), bf16), vm((3, height, LANES), bf16),
        vm((leaves_n - 1, height // 2, LANES), bf16),
        vm((CHUNKS, 2, hs[1], LANES), bf16), vm((4, hs[2], LANES), bf16),
        vm((leaves_n, hs[3], LANES), bf16), vm((leaves_n, hs[3], LANES), bf16),
        pltpu.SemaphoreType.DMA((len(GATHERS), rows_n)),
        pltpu.SemaphoreType.DMA((len(GATHERS), rows_n)),
        pltpu.SemaphoreType.DMA((len(GATHERS), rows_n)),
        pltpu.SemaphoreType.DMA((len(SWAPS), leaves_n)),
        pltpu.SemaphoreType.DMA((len(SWAPS), leaves_n)),
        pltpu.SemaphoreType.DMA((len(LOCALS),)),
        pltpu.SemaphoreType.DMA((4, rows_n)),
        pltpu.SemaphoreType.DMA((4, rows_n)),
    ]
    pack = rhs.shape[2]
    flops = 2 * right_n * (pack * whole + height * off_diag.shape[3])
    moved = 2 * (pack * whole + height * off_diag.shape[3] + 3 * pack * right_n)
    solved = pl.pallas_call(
        functools.partial(tree_kernel, rows_n, leaves_n),
        out_shape=jax.ShapeDtypeStruct((pack, right_n), bf16),
        in_specs=[pl.BlockSpec(memory_space=pltpu.SMEM)] + [pl.BlockSpec(memory_space=pltpu.HBM)] * 3,
        out_specs=pl.BlockSpec(memory_space=pltpu.VMEM),
        scratch_shapes=scratch,
        compiler_params=pltpu.CompilerParams(
            collective_id=0, has_side_effects=True, vmem_limit_bytes=62 * 2**20),
        cost_estimate=pl.CostEstimate(flops=flops, bytes_accessed=moved, transcendentals=0),
    )(pair_mask[0, 0], rhs[0, 0], inv_diag[0, 0], off_diag[0, 0])
    return solved.astype(f32)[None, None]


def solution(mesh):
    in_specs = (
        P("leaf", "row", None, None),
        P("leaf", "row", None, None),
        P("leaf", "row", None, None),
        P("leaf", "row", None),
    )
    out_specs = P("leaf", "row", None, None)

    def run(rhs, inv_diag, off_diag, pair_mask):
        fit = fits(mesh.shape["row"], mesh.shape["leaf"], rhs, inv_diag, off_diag)
        body = tree_shards if fit else shards
        return jax.shard_map(body, mesh=mesh, in_specs=in_specs, out_specs=out_specs, check_vma=False)(
            rhs, inv_diag, off_diag, pair_mask
        )

    return run
```

```python
import functools

import jax
import jax.numpy as jnp
from jax import lax
from jax.experimental import pallas as pl
from jax.experimental.pallas import tpu as pltpu
from jax.sharding import PartitionSpec as P

LANES = 128
ROW_TILE = 16
CHUNKS = 2
TREE_LEVELS = 3
MESH = pl.DeviceIdType.MESH
REACH = 1


def partner_2(block, axis, bit):
    count = lax.axis_size(axis)
    route = []
    for low in range(count):
        high = low | 1 << bit
        if high != low and high < count:
            route += [(low, high), (high, low)]
    return lax.ppermute(block, axis, route)


def column_start(ancestor, width_all):
    offset = 0
    for higher in range(1, ancestor):
        for within in range(higher):
            offset += width_all // 2**within
    return offset


def shards(rhs, inv_diag, off_diag, pair_mask):
    rows_n = lax.axis_size("row")
    leaves = lax.axis_size("leaf")
    levels_n = leaves.bit_length() - 1
    leaf_index = lax.axis_index("leaf")
    width_all = inv_diag.shape[3]
    right_all = rhs[0, 0]
    inverse_all = inv_diag[0, 0]
    panels = off_diag[0, 0]
    live_pairs = pair_mask[0, 0].astype(jnp.bfloat16)
    known_parts = []
    outputs = []
    offset = 0
    for ancestor in range(levels_n + 1):
        height = width_all // (2**ancestor * rows_n)
        own_rhs = right_all[offset : offset + height]
        own_inv = inverse_all[offset : offset + height]
        offset += height
        if ancestor > 0:
            stacked = jnp.concatenate(
                [
                    known_parts[source] * live_pairs[ancestor * (ancestor - 1) // 2 + source]
                    for source in range(ancestor)
                ],
                axis=0,
            )
            first_col = column_start(ancestor, width_all)
            span_cols = stacked.shape[0]
            update = jnp.dot(
                panels[:, first_col : first_col + span_cols],
                stacked,
                preferred_element_type=jnp.float32,
            )
        if ancestor > 0:
            current = update
            for bit_pos in reversed(range(ancestor)):
                half_rows = current.shape[0] // 2
                upper_half = leaf_index // 2**bit_pos % 2 == 1
                kept_rows = jnp.where(upper_half, current[half_rows:], current[:half_rows])
                sent_rows = jnp.where(upper_half, current[:half_rows], current[half_rows:])
                current = kept_rows + partner_2(
                    sent_rows.astype(jnp.bfloat16), "leaf", bit_pos
                ).astype(sent_rows.dtype)
            reduced = (own_rhs.astype(jnp.float32) - current).astype(jnp.bfloat16)
        else:
            reduced = own_rhs
        gathered = lax.all_gather(reduced, "row", axis=0, tiled=True)
        for bit_pos in range(ancestor):
            partner = partner_2(gathered, "leaf", bit_pos)
            upper_half = leaf_index // 2**bit_pos % 2 == 1
            gathered = jnp.where(
                upper_half,
                jnp.concatenate([partner, gathered], axis=0),
                jnp.concatenate([gathered, partner], axis=0),
            )
        solved = jnp.dot(own_inv, gathered, preferred_element_type=jnp.float32)
        outputs.append(solved)
        if ancestor < levels_n:
            leaf_part = lax.all_gather(solved.astype(jnp.bfloat16), "row", axis=0, tiled=True)
            known_parts.append(leaf_part)
    return jnp.concatenate(outputs, axis=0)[None, None]


def dot32(left, right):
    return jnp.dot(left, right, preferred_element_type=jnp.float32)


GATHERS = ["z0a", "z0b", "y0a", "y0b", "z1a", "z1b", "y1a", "y1b", "z2", "z3"]
SWAPS = ["b1a", "b1b", "b2", "b3", "d1", "d2", "d3", "d2p", "d3p", "u1a", "u1b", "u2", "u3", "y1a", "y1b", "y3"]
LOCALS = ["z0a", "z0b", "d0", "p1", "p2", "p3", "d1", "d2", "d3", "b1a", "b1b", "b2", "b3"]


def tree_kernel(
    rows_n, leaves_n,
    mask, rhs, inv, pan, out,
    d0, d1, d2, d3, p1, p2, p3, b1, b2, b3,
    z0, z1, z2, z3, y0, y1, y2,
    acc, u1, u2, u3, u1s, u2s, u3s, u1r, u2r, u3r, y1s, y2s, y3s, y3r,
    up_sem, down_sem, land_sem, swap_send, swap_recv, local_sem, spread_send, spread_recv,
):
    leaf = lax.axis_index("leaf")
    row = lax.axis_index("row")
    height = p1.shape[0]
    right_n = u2.shape[1]
    chunk = right_n // CHUNKS
    heights = [height // 2**m for m in range(TREE_LEVELS + 1)]
    starts = [sum(heights[:m]) for m in range(TREE_LEVELS + 1)]
    wide = LANES
    suffix = "ab"
    pending = []
    place = [leaf % 2**m for m in range(TREE_LEVELS + 1)]
    own_chunk = leaf % 2

    def block_of(position):
        return 2 * (position % 2) + position // 2 % 2

    def at_cols(index):
        return pl.ds(pl.multiple_of(index * wide, wide), wide)

    def level_rows(m):
        return pl.ds(starts[m], heights[m])

    barrier = pltpu.get_barrier_semaphore()

    for e in range(1, rows_n):
        for d in range(4):
            pl.semaphore_signal(
                barrier, inc=1, device_id=(leaf - place[2] + (place[2] + d) % 4, (row + e) % rows_n),
                device_id_type=MESH)
    for d in range(1, leaves_n):
        pl.semaphore_signal(barrier, inc=1, device_id=((leaf + d) % leaves_n, row), device_id_type=MESH)

    def local(name, src, dst):
        return pltpu.make_async_copy(src, dst, local_sem.at[LOCALS.index(name)])

    local_copies = {}
    for c in range(CHUNKS):
        local_copies["z0" + suffix[c]] = local(
            "z0" + suffix[c], rhs.at[pl.ds(0, height), pl.ds(c * chunk, chunk)], z0.at[c, row])
    local_copies["d0"] = local("d0", inv.at[pl.ds(0, height)], d0)
    for m, held in ((1, p1), (2, p2), (3, p3)):
        local_copies["p%d" % m] = local(
            "p%d" % m, pan.at[:, pl.ds(column_start(m, d0.shape[1]), held.shape[1])], held)
    for m, held in ((1, d1), (2, d2), (3, d3)):
        local_copies["d%d" % m] = local("d%d" % m, inv.at[level_rows(m)], held.at[place[m]])
    for c in range(CHUNKS):
        local_copies["b1" + suffix[c]] = local(
            "b1" + suffix[c], rhs.at[level_rows(1), at_cols(2 * c + place[1])], b1.at[c, place[1]])
    local_copies["b2"] = local("b2", rhs.at[level_rows(2), at_cols(block_of(place[2]))], b2.at[place[2]])
    local_copies["b3"] = local("b3", rhs.at[level_rows(3), at_cols(block_of(place[3]))], b3.at[place[3]])
    for name in LOCALS:
        local_copies[name].start()

    pl.semaphore_wait(barrier, 4 * (rows_n - 1) + leaves_n - 1)

    def begin(can, make):
        if can is None:
            make().start()
        else:
            @pl.when(can)
            def _():
                make().start()
        pending.append((can, make))

    def hop(name, src, dst, step, source, order, way, far=1):
        k = GATHERS.index(name)
        sem = (up_sem, down_sem)[order]
        return pltpu.make_async_remote_copy(
            src_ref=src, dst_ref=dst, send_sem=sem.at[k, step], recv_sem=land_sem.at[k, source],
            device_id=(leaf, row + way * far), device_id_type=MESH)

    lead = 1 - 2 * (leaf % 2)
    ways = [(order, lead if order == 0 else -lead) for order in range(2)]

    def inside(index):
        return jnp.logical_and(index >= 0, index < rows_n)

    def gather_start(name, slot, src=None, gate=True):
        for far, (order, way) in [(far, pair) for far in reversed(range(1, REACH + 1)) for pair in ways]:
            can = jnp.logical_and(inside(row + way * far), gate)

            def make(order=order, way=way, far=far):
                return hop(name, slot(row) if src is None else src, slot(row), far - 1, row, order, way, far)

            begin(can, make)

    def arrived(step, then):
        for _, way in ways:
            source = row - way * step

            @pl.when(inside(source))
            def _(source=source):
                then(source)

    def gather_step(name, slot, step, then=None, gate=True):
        for order, way in ways:
            can = inside(row + way)
            source = row - way * step
            there = jnp.logical_and(inside(source), gate)

            def make(order=order, way=way, source=source):
                return hop(name, slot(source), slot(source), step, source, order, way)

            @pl.when(there)
            def _(make=make):
                make().wait_recv()

            if REACH <= step < rows_n - 1:
                both = jnp.logical_and(there, can)

                @pl.when(both)
                def _(make=make):
                    make().start()

                pending.append((both, make))

        if then is not None:
            arrived(step, then)

    def peer(m, d):
        size = 2**m
        return leaf - place[m] + (place[m] + d) % size

    def swap(name, m, d, src, dst, line=None):
        k = SWAPS.index(name)
        line = d if line is None else line
        return pltpu.make_async_remote_copy(
            src_ref=src, dst_ref=dst, send_sem=swap_send.at[k, line], recv_sem=swap_recv.at[k, line],
            device_id=(peer(m, d), row), device_id_type=MESH)

    def swap_start(name, m, src, dst, when=None, only=None):
        size = 2**m
        for d in only or range(1, size):
            target = (place[m] + d) % size

            def make(d=d, target=target):
                return swap(name, m, d, src(target), dst(place[m], d))

            begin(None if when is None else when(target), make)

    def swap_wait(name, m, src, dst, only=None):
        size = 2**m
        for d in only or range(1, size):
            sender = (place[m] - d + size) % size
            swap(name, m, d, src(place[m]), dst(sender, d)).wait_recv()

    def z0_slot(c):
        return lambda q: z0.at[c, q]

    def y0_slot(c):
        return lambda q: y0.at[c, q]

    def z1_slot(c):
        return lambda q: z1.at[c, :, q]

    def y1_slot(c):
        return lambda q: y1.at[c, q]

    def z2_slot(q):
        return z2.at[:, q]

    def z3_slot(q):
        return z3.at[:, q]

    for c in range(CHUNKS):
        gather_start("z0" + suffix[c], z0_slot(c), rhs.at[pl.ds(0, height), pl.ds(c * chunk, chunk)])

    fixed = []
    for c in range(CHUNKS):
        fixed.append((
            "b1" + suffix[c], 1,
            lambda target, c=c: rhs.at[level_rows(1), at_cols(2 * c + target)],
            lambda sender, d, c=c: b1.at[c, sender]))
    fixed.append(("d1", 1, lambda target: inv.at[level_rows(1)], lambda sender, d: d1.at[sender]))
    fixed.append(("b2", 2, lambda target: rhs.at[level_rows(2), at_cols(block_of(target))], lambda sender, d: b2.at[sender]))
    fixed.append(("d2", 2, lambda target: inv.at[level_rows(2)], lambda sender, d: d2.at[sender]))
    fixed.append(("b3", 3, lambda target: rhs.at[level_rows(3), at_cols(block_of(target))], lambda sender, d: b3.at[sender]))
    fixed.append(("d3", 3, lambda target: inv.at[level_rows(3)], lambda sender, d: d3.at[sender]))
    D2, D3 = CHUNKS + 2, CHUNKS + 4
    for k, entry in enumerate(fixed):
        if k not in (D2, D3):
            swap_start(*entry)

    def hand_over(name, held, i, mine):
        at = 2 * i + (place[1] if mine else 1 - place[1])
        return swap(name, 1, 1, held.at[at], held.at[at], i)

    def hand_all(name, held):
        for i in range(held.shape[0] // 2):
            begin(None, lambda i=i: hand_over(name, held, i, True))

    def taken_all(name, held):
        for i in range(held.shape[0] // 2):
            hand_over(name, held, i, False).wait_recv()

    def live(pair):
        return mask[pair].astype(jnp.float32)

    def cols_of(c):
        return pl.ds(c * chunk, chunk)

    whole = d0.shape[1]

    def shard_cols(source):
        return pl.ds(pl.multiple_of(source * height, LANES), height)

    def add_solved(c):
        def then(source):
            acc[c] += dot32(d0[:, shard_cols(source)], z0[c, source])
        return then

    def add_first(c):
        def then(source):
            u1[c] += dot32(p1[:, shard_cols(source)], y0[c, source]) * live(0)
        return then

    def add_rest(c):
        def then(source):
            u2[:, cols_of(c)] += dot32(p2[:, shard_cols(source)], y0[c, source]) * live(1)
            u3[:, cols_of(c)] += dot32(p3[:, shard_cols(source)], y0[c, source]) * live(3)
        return then

    def add_all(c):
        def then(source):
            add_first(c)(source)
            add_rest(c)(source)
        return then

    for c in range(CHUNKS):
        acc[c] = jnp.zeros_like(acc[c])
        u1[c] = jnp.zeros_like(u1[c])
    u2[...] = jnp.zeros_like(u2)
    u3[...] = jnp.zeros_like(u3)
    local_copies["d0"].wait()
    for c in range(CHUNKS):
        local_copies["z0" + suffix[c]].wait()
        add_solved(c)(row)
    pieces = [(D2, 2), (D3, 2), (D3, 4), (D3, 6)]
    for step in range(1, rows_n - 1):
        for c in range(CHUNKS):
            gather_step("z0" + suffix[c], z0_slot(c), step, add_solved(c))
            if pieces:
                entry, d = pieces.pop(0)
                swap_start(*fixed[entry], only=[d])
    for entry, d in pieces:
        swap_start(*fixed[entry], only=[d])
    for c in range(CHUNKS):
        gather_step("z0" + suffix[c], z0_slot(c), rows_n - 1, add_solved(c))
        solved = acc[c]
        y0[c, row] = solved.astype(jnp.bfloat16)
        gather_start("y0" + suffix[c], y0_slot(c))
        out[pl.ds(0, height), cols_of(c)] = y0[c, row]
    for name in ("p1", "p2", "p3", "d2", "d3"):
        local_copies[name].wait()
    for c in range(CHUNKS):
        add_all(c)(row)
    for step in range(1, rows_n - 1):
        for c in range(CHUNKS):
            gather_step("y0" + suffix[c], y0_slot(c), step, add_all(c))
        if step == 1:
            swap_wait(*fixed[D2], only=[2])
            swap_wait(*fixed[D3], only=[2, 4, 6])
            hand_all("d2p", d2)
            hand_all("d3p", d3)

    half = whole // 2
    u1_src = [lambda target, c=c: u1s.at[c, :, at_cols(target)] for c in range(CHUNKS)]
    u1_dst = [lambda sender, d, c=c: u1r.at[c, d - 1] for c in range(CHUNKS)]
    y1_src = [lambda target, c=c: y1s.at[c, target] for c in range(CHUNKS)]
    y1_dst = [lambda sender, d, c=c: y1.at[c, row, :, at_cols(sender)] for c in range(CHUNKS)]

    def update_1(c):
        gather_step("y0" + suffix[c], y0_slot(c), rows_n - 1, add_first(c))
        u1s[c] = u1[c].astype(jnp.bfloat16)
        swap_start("u1" + suffix[c], 1, u1_src[c], u1_dst[c])

    def reduce_1(c):
        local_copies["b1" + suffix[c]].wait()
        swap_wait(*fixed[c])
        swap_wait("u1" + suffix[c], 1, u1_src[c], u1_dst[c])
        total = u1[c, :, at_cols(place[1])] + u1r[c, 0].astype(jnp.float32)
        reduced = (b1[c].reshape(height, wide).astype(jnp.float32) - total).astype(jnp.bfloat16)
        for s in range(2):
            z1[c, s, row] = reduced[s * heights[1] : (s + 1) * heights[1]]
        gather_start("z1" + suffix[c], z1_slot(c))

    def solve_1(c):
        gather_step("z1" + suffix[c], z1_slot(c), rows_n - 1)
        solved = dot32(d1[...].reshape(height, whole), z1[c].reshape(whole, wide)).astype(jnp.bfloat16)
        y1s[c] = solved.reshape(2, heights[1], wide)
        swap_start("y1" + suffix[c], 1, y1_src[c], y1_dst[c])
        y1[c, row, :, at_cols(place[1])] = y1s[c, place[1]]

    def spread_1(c):
        swap_wait("y1" + suffix[c], 1, y1_src[c], y1_dst[c])
        gather_start("y1" + suffix[c], y1_slot(c))

    u2_src = lambda target: u2s.at[:, at_cols(block_of(target))]
    u2_dst = lambda sender, d: u2r.at[d - 1]

    def update_2(c):
        gather_step("y1" + suffix[c], y1_slot(c), rows_n - 1)
        update = u2[:, cols_of(c)] + dot32(p2[:, whole:], y1[c].reshape(half, chunk)) * live(2)
        u2[:, cols_of(c)] = update
        u2s[:, cols_of(c)] = update.astype(jnp.bfloat16)
        swap_start("u2", 2, u2_src, u2_dst, lambda target: target % 2 == c)

    def later_3(c):
        u3[:, cols_of(c)] += dot32(p3[:, whole : whole + half], y1[c].reshape(half, chunk)) * live(4)

    def reduce_2(c):
        @pl.when(own_chunk == c)
        def _():
            swap_wait("u2", 2, u2_src, u2_dst)
            total = u2[:, at_cols(block_of(place[2]))]
            for d in range(3):
                total = total + u2r[d].astype(jnp.float32)
            reduced = (b2[...].reshape(height, wide).astype(jnp.float32) - total).astype(jnp.bfloat16)
            for s in range(4):
                z2[s, row] = reduced[s * heights[2] : (s + 1) * heights[2]]

        gather_start("z2", z2_slot, gate=own_chunk == c)

    def spread(d, e, position):
        here = leaf - place[2] + (place[2] + d) % 4
        dst = y2.at[(row if position is None else (row - e + rows_n) % rows_n), :,
                    at_cols(block_of(place[2] if position is None else position))]
        src = y2s.at[(place[2] + d) % 4]
        return pltpu.make_async_remote_copy(
            src_ref=src, dst_ref=dst, send_sem=spread_send.at[d, e], recv_sem=spread_recv.at[d, e],
            device_id=(here, (row + e) % rows_n), device_id_type=MESH)

    others = [(d, e) for e in reversed(range(rows_n)) for d in range(4) if d or e]

    def solve_2(c):
        gather_step("z2", z2_slot, rows_n - 1, gate=own_chunk == c)

        @pl.when(own_chunk == c)
        def _():
            solved = dot32(d2[...].reshape(height, whole), z2[...].reshape(whole, wide)).astype(jnp.bfloat16)
            y2s[...] = solved.reshape(4, heights[2], wide)

        for d, e in others:
            begin(own_chunk == c, lambda d=d, e=e: spread(d, e, None))

        @pl.when(own_chunk == c)
        def _():
            y2[row, :, at_cols(block_of(place[2]))] = y2s[place[2]]

    fold = height // 2
    low = lax.broadcasted_iota(jnp.int32, (fold, wide), 1) < wide // 2

    def folded(top, bottom):
        return (
            jnp.where(low, top, pltpu.roll(bottom, wide // 2, 1)),
            jnp.where(low, pltpu.roll(top, wide // 2, 1), bottom),
        )

    u3_src = lambda target: u3s.at[target]
    u3_dst = lambda sender, d: u3r.at[d - 1]

    def update_3(c):
        for d, e in others:
            sender = (place[2] - d + 4) % 4

            @pl.when(sender % 2 == c)
            def _(d=d, e=e, sender=sender):
                spread(d, e, sender).wait_recv()

        known = y2[:, :, c * chunk : (c + 1) * chunk].reshape(whole // 4, chunk)
        update = u3[:, cols_of(c)] + dot32(p3[:, whole + half :], known) * live(5)
        for k in range(2):
            block = update[:, k * wide : (k + 1) * wide]
            sides = folded(block[:fold], block[fold:])
            for side in range(2):
                u3s[4 * side + 2 * k + c] = sides[side].astype(jnp.bfloat16)
        swap_start("u3", 3, u3_src, u3_dst, lambda target: target % 2 == c)

    def reduce_3(c):
        @pl.when(own_chunk == c)
        def _():
            own_b = b3[...].astype(jnp.float32)
            sides = folded(own_b[:4].reshape(fold, wide), own_b[4:].reshape(fold, wide))
            own_b = jnp.where(place[3] < leaves_n // 2, sides[0], sides[1])
            swap_wait("u3", 3, u3_src, u3_dst)
            total = u3s[place[3]].astype(jnp.float32)
            for d in range(leaves_n - 1):
                total = total + u3r[d].astype(jnp.float32)
            reduced = (own_b - total).astype(jnp.bfloat16)
            for s in range(4):
                z3[s, row] = reduced[s * heights[3] : (s + 1) * heights[3]]

        gather_start("z3", z3_slot, gate=own_chunk == c)

    y3_src = lambda target: y3s.at[target]
    y3_dst = lambda sender, d: y3r.at[sender]

    def solve_3():
        gather_step("z3", z3_slot, rows_n - 1)
        known = z3[...].reshape(half, wide)
        left = dot32(d3[:, :, :half].reshape(height, half), known)
        right = dot32(d3[:, :, half:].reshape(height, half), known)
        solved = left + pltpu.roll(right, wide // 2, 1)
        low_all = lax.broadcasted_iota(jnp.int32, (height, wide), 1) < wide // 2
        solved = jnp.where(low_all, solved, pltpu.roll(solved, wide // 2, 1))
        y3s[...] = solved.astype(jnp.bfloat16).reshape(leaves_n, heights[3], wide)
        swap_start("y3", 3, y3_src, y3_dst)
        y3r[place[3]] = y3s[place[3]]

    update_1(0)
    arrived(rows_n - 1, add_rest(0))
    reduce_1(0)
    update_1(1)
    gather_step("z1a", z1_slot(0), 1)
    reduce_1(1)
    arrived(rows_n - 1, add_rest(1))
    for step in range(2, rows_n - 1):
        gather_step("z1a", z1_slot(0), step)
        gather_step("z1b", z1_slot(1), step - 1)
    local_copies["d1"].wait()
    swap_wait(*fixed[CHUNKS])
    solve_1(0)
    gather_step("z1b", z1_slot(1), rows_n - 2)
    spread_1(0)
    solve_1(1)
    gather_step("y1a", y1_slot(0), 1)
    spread_1(1)
    for step in range(2, rows_n - 1):
        gather_step("y1a", y1_slot(0), step)
        gather_step("y1b", y1_slot(1), step - 1)
    local_copies["b2"].wait()
    swap_wait(*fixed[CHUNKS + 1])
    update_2(0)
    gather_step("y1b", y1_slot(1), rows_n - 2)
    later_3(0)
    reduce_2(0)
    gather_step("z2", z2_slot, 1, gate=own_chunk == 0)
    update_2(1)
    for step in range(2, rows_n - 1):
        gather_step("z2", z2_slot, step, gate=own_chunk == 0)
    taken_all("d2p", d2)
    reduce_2(1)
    later_3(1)
    for step in range(1, rows_n - 1):
        gather_step("z2", z2_slot, step, gate=own_chunk == 1)
    for c in range(CHUNKS):
        out[level_rows(1), cols_of(c)] = y1[c, row]
    local_copies["b3"].wait()
    swap_wait(*fixed[CHUNKS + 3])
    taken_all("d3p", d3)
    solve_2(0)
    solve_2(1)
    update_3(0)
    reduce_3(0)
    gather_step("z3", z3_slot, 1, gate=own_chunk == 0)
    update_3(1)
    for step in range(2, rows_n - 1):
        gather_step("z3", z3_slot, step, gate=own_chunk == 0)
    reduce_3(1)
    for step in range(1, rows_n - 1):
        gather_step("z3", z3_slot, step, gate=own_chunk == 1)
    out[level_rows(2), :] = y2[row]
    solve_3()
    swap_wait("y3", 3, y3_src, y3_dst)
    low_out = lax.broadcasted_iota(jnp.int32, (heights[3], wide), 1) < wide // 2
    for k in range(leaves_n // 2):
        first = 2 * (k % 2) + k // 2
        out[level_rows(3), pl.ds(k * wide, wide)] = jnp.where(
            low_out, y3r[first].astype(jnp.float32), y3r[first + leaves_n // 2].astype(jnp.float32)
        ).astype(jnp.bfloat16)

    for can, make in pending:
        if can is None:
            make().wait_send()
        else:
            @pl.when(can)
            def _(make=make):
                make().wait_send()


def fits(rows_n, leaves_n, rhs, inv_diag, off_diag):
    whole = inv_diag.shape[3]
    right_n = rhs.shape[3]
    return (
        leaves_n == 2**TREE_LEVELS
        and rows_n > 2
        and whole % (leaves_n * rows_n * ROW_TILE) == 0
        and whole % (rows_n * LANES) == 0
        and whole % (4 * LANES) == 0
        and right_n == 4 * LANES
    )


def tree_shards(rhs, inv_diag, off_diag, pair_mask):
    rows_n = lax.axis_size("row")
    leaves_n = lax.axis_size("leaf")
    whole = inv_diag.shape[3]
    right_n = rhs.shape[3]
    height = off_diag.shape[2]
    chunk = right_n // CHUNKS
    hs = [height // 2**m for m in range(TREE_LEVELS + 1)]
    bf16, f32 = jnp.bfloat16, jnp.float32
    vm = pltpu.VMEM
    scratch = [
        vm((height, whole), bf16),
        vm((2, hs[1], whole), bf16), vm((4, hs[2], whole), bf16), vm((8, hs[3], whole), bf16),
        vm((height, whole), bf16), vm((height, whole + whole // 2), bf16),
        vm((height, whole + whole // 2 + whole // 4), bf16),
        vm((CHUNKS, 2, hs[1], LANES), bf16), vm((4, hs[2], LANES), bf16), vm((8, hs[3], LANES), bf16),
        vm((CHUNKS, rows_n, height, chunk), bf16),
        vm((CHUNKS, 2, rows_n, hs[1], LANES), bf16),
        vm((4, rows_n, hs[2], LANES), bf16),
        vm((4, rows_n, hs[3], LANES), bf16),
        vm((CHUNKS, rows_n, height, chunk), bf16),
        vm((CHUNKS, rows_n, hs[1], chunk), bf16),
        vm((rows_n, hs[2], right_n), bf16),
        vm((CHUNKS, height, chunk), f32),
        vm((CHUNKS, height, chunk), f32), vm((height, right_n), f32), vm((height, right_n), f32),
        vm((CHUNKS, height, chunk), bf16), vm((height, right_n), bf16),
        vm((leaves_n, height // 2, LANES), bf16),
        vm((CHUNKS, 1, height, LANES), bf16), vm((3, height, LANES), bf16),
        vm((leaves_n - 1, height // 2, LANES), bf16),
        vm((CHUNKS, 2, hs[1], LANES), bf16), vm((4, hs[2], LANES), bf16),
        vm((leaves_n, hs[3], LANES), bf16), vm((leaves_n, hs[3], LANES), bf16),
        pltpu.SemaphoreType.DMA((len(GATHERS), rows_n)),
        pltpu.SemaphoreType.DMA((len(GATHERS), rows_n)),
        pltpu.SemaphoreType.DMA((len(GATHERS), rows_n)),
        pltpu.SemaphoreType.DMA((len(SWAPS), leaves_n)),
        pltpu.SemaphoreType.DMA((len(SWAPS), leaves_n)),
        pltpu.SemaphoreType.DMA((len(LOCALS),)),
        pltpu.SemaphoreType.DMA((4, rows_n)),
        pltpu.SemaphoreType.DMA((4, rows_n)),
    ]
    pack = rhs.shape[2]
    flops = 2 * right_n * (pack * whole + height * off_diag.shape[3])
    moved = 2 * (pack * whole + height * off_diag.shape[3] + 3 * pack * right_n)
    solved = pl.pallas_call(
        functools.partial(tree_kernel, rows_n, leaves_n),
        out_shape=jax.ShapeDtypeStruct((pack, right_n), bf16),
        in_specs=[pl.BlockSpec(memory_space=pltpu.SMEM)] + [pl.BlockSpec(memory_space=pltpu.HBM)] * 3,
        out_specs=pl.BlockSpec(memory_space=pltpu.VMEM),
        scratch_shapes=scratch,
        compiler_params=pltpu.CompilerParams(
            collective_id=0, has_side_effects=True, vmem_limit_bytes=62 * 2**20),
        cost_estimate=pl.CostEstimate(flops=flops, bytes_accessed=moved, transcendentals=0),
    )(pair_mask[0, 0], rhs[0, 0], inv_diag[0, 0], off_diag[0, 0])
    return solved.astype(f32)[None, None]


def solution(mesh):
    in_specs = (
        P("leaf", "row", None, None),
        P("leaf", "row", None, None),
        P("leaf", "row", None, None),
        P("leaf", "row", None),
    )
    out_specs = P("leaf", "row", None, None)

    def run(rhs, inv_diag, off_diag, pair_mask):
        fit = fits(mesh.shape["row"], mesh.shape["leaf"], rhs, inv_diag, off_diag)
        body = tree_shards if fit else shards
        return jax.shard_map(body, mesh=mesh, in_specs=in_specs, out_specs=out_specs, check_vma=False)(
            rhs, inv_diag, off_diag, pair_mask
        )

    return run
```

```python
import functools

import jax
import jax.numpy as jnp
from jax import lax
from jax.experimental import pallas as pl
from jax.experimental.pallas import tpu as pltpu
from jax.sharding import PartitionSpec as P

LANES = 128
ROW_TILE = 16
CHUNKS = 2
TREE_LEVELS = 3
MESH = pl.DeviceIdType.MESH


def partner_2(block, axis, bit):
    count = lax.axis_size(axis)
    route = []
    for low in range(count):
        high = low | 1 << bit
        if high != low and high < count:
            route += [(low, high), (high, low)]
    return lax.ppermute(block, axis, route)


def column_start(ancestor, width_all):
    offset = 0
    for higher in range(1, ancestor):
        for within in range(higher):
            offset += width_all // 2**within
    return offset


def shards(rhs, inv_diag, off_diag, pair_mask):
    rows_n = lax.axis_size("row")
    leaves = lax.axis_size("leaf")
    levels_n = leaves.bit_length() - 1
    leaf_index = lax.axis_index("leaf")
    width_all = inv_diag.shape[3]
    right_all = rhs[0, 0]
    inverse_all = inv_diag[0, 0]
    panels = off_diag[0, 0]
    live_pairs = pair_mask[0, 0].astype(jnp.bfloat16)
    known_parts = []
    outputs = []
    offset = 0
    for ancestor in range(levels_n + 1):
        height = width_all // (2**ancestor * rows_n)
        own_rhs = right_all[offset : offset + height]
        own_inv = inverse_all[offset : offset + height]
        offset += height
        if ancestor > 0:
            stacked = jnp.concatenate(
                [
                    known_parts[source] * live_pairs[ancestor * (ancestor - 1) // 2 + source]
                    for source in range(ancestor)
                ],
                axis=0,
            )
            first_col = column_start(ancestor, width_all)
            span_cols = stacked.shape[0]
            update = jnp.dot(
                panels[:, first_col : first_col + span_cols],
                stacked,
                preferred_element_type=jnp.float32,
            )
        if ancestor > 0:
            current = update
            for bit_pos in reversed(range(ancestor)):
                half_rows = current.shape[0] // 2
                upper_half = leaf_index // 2**bit_pos % 2 == 1
                kept_rows = jnp.where(upper_half, current[half_rows:], current[:half_rows])
                sent_rows = jnp.where(upper_half, current[:half_rows], current[half_rows:])
                current = kept_rows + partner_2(
                    sent_rows.astype(jnp.bfloat16), "leaf", bit_pos
                ).astype(sent_rows.dtype)
            reduced = (own_rhs.astype(jnp.float32) - current).astype(jnp.bfloat16)
        else:
            reduced = own_rhs
        gathered = lax.all_gather(reduced, "row", axis=0, tiled=True)
        for bit_pos in range(ancestor):
            partner = partner_2(gathered, "leaf", bit_pos)
            upper_half = leaf_index // 2**bit_pos % 2 == 1
            gathered = jnp.where(
                upper_half,
                jnp.concatenate([partner, gathered], axis=0),
                jnp.concatenate([gathered, partner], axis=0),
            )
        solved = jnp.dot(own_inv, gathered, preferred_element_type=jnp.float32)
        outputs.append(solved)
        if ancestor < levels_n:
            leaf_part = lax.all_gather(solved.astype(jnp.bfloat16), "row", axis=0, tiled=True)
            known_parts.append(leaf_part)
    return jnp.concatenate(outputs, axis=0)[None, None]


def dot32(left, right):
    return jnp.dot(left, right, preferred_element_type=jnp.float32)


GATHERS = ["z0a", "z0b", "y0a", "y0b", "z1a", "z1b", "y1a", "y1b", "z2", "z3"]
SWAPS = ["b1a", "b1b", "b2", "b3", "d1", "d2", "d3", "d2p", "d3p", "u1a", "u1b", "u2", "u3", "y1a", "y1b", "y3"]
LOCALS = ["z0a", "z0b", "d0", "p1", "p2", "p3", "d1", "d2", "d3", "b1a", "b1b", "b2", "b3"]


def tree_kernel(
    rows_n, leaves_n,
    mask, rhs, inv, pan, out,
    d0, d1, d2, d3, p1, p2, p3, b1, b2, b3,
    z0, z1, z2, z3, y0, y1, y2,
    acc, u1, u2, u3, u1s, u2s, u3s, u1r, u2r, u3r, y1s, y2s, y3s, y3r,
    up_sem, down_sem, land_sem, swap_send, swap_recv, local_sem, spread_send, spread_recv,
):
    leaf = lax.axis_index("leaf")
    row = lax.axis_index("row")
    height = p1.shape[0]
    right_n = u2.shape[1]
    chunk = right_n // CHUNKS
    heights = [height // 2**m for m in range(TREE_LEVELS + 1)]
    starts = [sum(heights[:m]) for m in range(TREE_LEVELS + 1)]
    wide = LANES
    suffix = "ab"
    pending = []
    place = [leaf % 2**m for m in range(TREE_LEVELS + 1)]
    own_chunk = leaf % 2

    def block_of(position):
        return 2 * (position % 2) + position // 2 % 2

    def at_cols(index):
        return pl.ds(pl.multiple_of(index * wide, wide), wide)

    def level_rows(m):
        return pl.ds(starts[m], heights[m])

    barrier = pltpu.get_barrier_semaphore()

    for e in range(1, rows_n):
        for d in range(4):
            pl.semaphore_signal(
                barrier, inc=1, device_id=(leaf - place[2] + (place[2] + d) % 4, (row + e) % rows_n),
                device_id_type=MESH)
    for d in range(1, leaves_n):
        pl.semaphore_signal(barrier, inc=1, device_id=((leaf + d) % leaves_n, row), device_id_type=MESH)

    def local(name, src, dst):
        return pltpu.make_async_copy(src, dst, local_sem.at[LOCALS.index(name)])

    local_copies = {}
    for c in range(CHUNKS):
        local_copies["z0" + suffix[c]] = local(
            "z0" + suffix[c], rhs.at[pl.ds(0, height), pl.ds(c * chunk, chunk)], z0.at[c, row])
    local_copies["d0"] = local("d0", inv.at[pl.ds(0, height)], d0)
    for m, held in ((1, p1), (2, p2), (3, p3)):
        local_copies["p%d" % m] = local(
            "p%d" % m, pan.at[:, pl.ds(column_start(m, d0.shape[1]), held.shape[1])], held)
    for m, held in ((1, d1), (2, d2), (3, d3)):
        local_copies["d%d" % m] = local("d%d" % m, inv.at[level_rows(m)], held.at[place[m]])
    for c in range(CHUNKS):
        local_copies["b1" + suffix[c]] = local(
            "b1" + suffix[c], rhs.at[level_rows(1), at_cols(2 * c + place[1])], b1.at[c, place[1]])
    local_copies["b2"] = local("b2", rhs.at[level_rows(2), at_cols(block_of(place[2]))], b2.at[place[2]])
    local_copies["b3"] = local("b3", rhs.at[level_rows(3), at_cols(block_of(place[3]))], b3.at[place[3]])
    for name in LOCALS:
        local_copies[name].start()

    pl.semaphore_wait(barrier, 4 * (rows_n - 1) + leaves_n - 1)

    def begin(can, make):
        if can is None:
            make().start()
        else:
            @pl.when(can)
            def _():
                make().start()
        pending.append((can, make))

    def hop(name, src, dst, step, source, order, way):
        k = GATHERS.index(name)
        sem = (up_sem, down_sem)[order]
        return pltpu.make_async_remote_copy(
            src_ref=src, dst_ref=dst, send_sem=sem.at[k, step], recv_sem=land_sem.at[k, source],
            device_id=(leaf, row + way), device_id_type=MESH)

    lead = 1 - 2 * (leaf % 2)
    ways = [(order, lead if order == 0 else -lead) for order in range(2)]

    def inside(index):
        return jnp.logical_and(index >= 0, index < rows_n)

    def gather_start(name, slot, src=None):
        for order, way in ways:
            can = inside(row + way)

            def make(order=order, way=way):
                return hop(name, slot(row) if src is None else src, slot(row), 0, row, order, way)

            @pl.when(can)
            def _(make=make):
                make().start()

            pending.append((can, make))

    def arrived(step, then):
        for _, way in ways:
            source = row - way * step

            @pl.when(inside(source))
            def _(source=source):
                then(source)

    def gather_step(name, slot, step, then=None):
        for order, way in ways:
            can = inside(row + way)
            source = row - way * step
            there = inside(source)

            def make(order=order, way=way, source=source):
                return hop(name, slot(source), slot(source), step, source, order, way)

            @pl.when(there)
            def _(make=make):
                make().wait_recv()

            if step < rows_n - 1:
                both = jnp.logical_and(there, can)

                @pl.when(both)
                def _(make=make):
                    make().start()

                pending.append((both, make))

        if then is not None:
            arrived(step, then)

    def direct(name, slot, e):
        k = GATHERS.index(name)
        return pltpu.make_async_remote_copy(
            src_ref=slot(row), dst_ref=slot(row), send_sem=up_sem.at[k, e], recv_sem=land_sem.at[k, e],
            device_id=(leaf, (row + e) % rows_n), device_id_type=MESH)

    def direct_start(name, slot, can):
        for e in range(1, rows_n):
            begin(can, lambda e=e: direct(name, slot, e))

    def direct_wait(name, slot):
        k = GATHERS.index(name)
        for e in range(1, rows_n):
            there = slot((row - e + rows_n) % rows_n)
            pltpu.make_async_remote_copy(
                src_ref=there, dst_ref=there, send_sem=up_sem.at[k, e], recv_sem=land_sem.at[k, e],
                device_id=(leaf, (row + e) % rows_n), device_id_type=MESH).wait_recv()

    def peer(m, d):
        size = 2**m
        return leaf - place[m] + (place[m] + d) % size

    def swap(name, m, d, src, dst, line=None):
        k = SWAPS.index(name)
        line = d if line is None else line
        return pltpu.make_async_remote_copy(
            src_ref=src, dst_ref=dst, send_sem=swap_send.at[k, line], recv_sem=swap_recv.at[k, line],
            device_id=(peer(m, d), row), device_id_type=MESH)

    def swap_start(name, m, src, dst, when=None, only=None):
        size = 2**m
        for d in only or range(1, size):
            target = (place[m] + d) % size

            def make(d=d, target=target):
                return swap(name, m, d, src(target), dst(place[m], d))

            begin(None if when is None else when(target), make)

    def swap_wait(name, m, src, dst, only=None):
        size = 2**m
        for d in only or range(1, size):
            sender = (place[m] - d + size) % size
            swap(name, m, d, src(place[m]), dst(sender, d)).wait_recv()

    def z0_slot(c):
        return lambda q: z0.at[c, q]

    def y0_slot(c):
        return lambda q: y0.at[c, q]

    def z1_slot(c):
        return lambda q: z1.at[c, :, q]

    def y1_slot(c):
        return lambda q: y1.at[c, q]

    def z2_slot(q):
        return z2.at[:, q]

    def z3_slot(q):
        return z3.at[:, q]

    for c in range(CHUNKS):
        gather_start("z0" + suffix[c], z0_slot(c), rhs.at[pl.ds(0, height), pl.ds(c * chunk, chunk)])

    fixed = []
    for c in range(CHUNKS):
        fixed.append((
            "b1" + suffix[c], 1,
            lambda target, c=c: rhs.at[level_rows(1), at_cols(2 * c + target)],
            lambda sender, d, c=c: b1.at[c, sender]))
    fixed.append(("d1", 1, lambda target: inv.at[level_rows(1)], lambda sender, d: d1.at[sender]))
    fixed.append(("b2", 2, lambda target: rhs.at[level_rows(2), at_cols(block_of(target))], lambda sender, d: b2.at[sender]))
    fixed.append(("d2", 2, lambda target: inv.at[level_rows(2)], lambda sender, d: d2.at[sender]))
    fixed.append(("b3", 3, lambda target: rhs.at[level_rows(3), at_cols(block_of(target))], lambda sender, d: b3.at[sender]))
    fixed.append(("d3", 3, lambda target: inv.at[level_rows(3)], lambda sender, d: d3.at[sender]))
    D2, D3 = CHUNKS + 2, CHUNKS + 4
    for k, entry in enumerate(fixed):
        if k not in (D2, D3):
            swap_start(*entry)

    def hand_over(name, held, i, mine):
        at = 2 * i + (place[1] if mine else 1 - place[1])
        return swap(name, 1, 1, held.at[at], held.at[at], i)

    def hand_all(name, held):
        for i in range(held.shape[0] // 2):
            begin(None, lambda i=i: hand_over(name, held, i, True))

    def taken_all(name, held):
        for i in range(held.shape[0] // 2):
            hand_over(name, held, i, False).wait_recv()

    def live(pair):
        return mask[pair].astype(jnp.float32)

    def cols_of(c):
        return pl.ds(c * chunk, chunk)

    whole = d0.shape[1]

    def shard_cols(source):
        return pl.ds(pl.multiple_of(source * height, LANES), height)

    def add_solved(c):
        def then(source):
            acc[c] += dot32(d0[:, shard_cols(source)], z0[c, source])
        return then

    def add_first(c):
        def then(source):
            u1[c] += dot32(p1[:, shard_cols(source)], y0[c, source]) * live(0)
        return then

    def add_rest(c):
        def then(source):
            u2[:, cols_of(c)] += dot32(p2[:, shard_cols(source)], y0[c, source]) * live(1)
            u3[:, cols_of(c)] += dot32(p3[:, shard_cols(source)], y0[c, source]) * live(3)
        return then

    def add_all(c):
        def then(source):
            add_first(c)(source)
            add_rest(c)(source)
        return then

    for c in range(CHUNKS):
        acc[c] = jnp.zeros_like(acc[c])
        u1[c] = jnp.zeros_like(u1[c])
    u2[...] = jnp.zeros_like(u2)
    u3[...] = jnp.zeros_like(u3)
    local_copies["d0"].wait()
    for c in range(CHUNKS):
        local_copies["z0" + suffix[c]].wait()
        add_solved(c)(row)
    pieces = [(D2, 2), (D3, 2), (D3, 4), (D3, 6)]
    for step in range(1, rows_n - 1):
        for c in range(CHUNKS):
            gather_step("z0" + suffix[c], z0_slot(c), step, add_solved(c))
            if pieces:
                entry, d = pieces.pop(0)
                swap_start(*fixed[entry], only=[d])
    for entry, d in pieces:
        swap_start(*fixed[entry], only=[d])
    for c in range(CHUNKS):
        gather_step("z0" + suffix[c], z0_slot(c), rows_n - 1, add_solved(c))
        solved = acc[c]
        y0[c, row] = solved.astype(jnp.bfloat16)
        gather_start("y0" + suffix[c], y0_slot(c))
        out[pl.ds(0, height), cols_of(c)] = y0[c, row]
    for name in ("p1", "p2", "p3", "d2", "d3"):
        local_copies[name].wait()
    for c in range(CHUNKS):
        add_all(c)(row)
    for step in range(1, rows_n - 1):
        for c in range(CHUNKS):
            gather_step("y0" + suffix[c], y0_slot(c), step, add_all(c))
        if step == 1:
            swap_wait(*fixed[D2], only=[2])
            swap_wait(*fixed[D3], only=[2, 4, 6])
            hand_all("d2p", d2)
            hand_all("d3p", d3)

    half = whole // 2
    u1_src = [lambda target, c=c: u1s.at[c, :, at_cols(target)] for c in range(CHUNKS)]
    u1_dst = [lambda sender, d, c=c: u1r.at[c, d - 1] for c in range(CHUNKS)]
    y1_src = [lambda target, c=c: y1s.at[c, target] for c in range(CHUNKS)]
    y1_dst = [lambda sender, d, c=c: y1.at[c, row, :, at_cols(sender)] for c in range(CHUNKS)]

    def update_1(c):
        gather_step("y0" + suffix[c], y0_slot(c), rows_n - 1, add_first(c))
        u1s[c] = u1[c].astype(jnp.bfloat16)
        swap_start("u1" + suffix[c], 1, u1_src[c], u1_dst[c])

    def reduce_1(c):
        local_copies["b1" + suffix[c]].wait()
        swap_wait(*fixed[c])
        swap_wait("u1" + suffix[c], 1, u1_src[c], u1_dst[c])
        total = u1[c, :, at_cols(place[1])] + u1r[c, 0].astype(jnp.float32)
        reduced = (b1[c].reshape(height, wide).astype(jnp.float32) - total).astype(jnp.bfloat16)
        for s in range(2):
            z1[c, s, row] = reduced[s * heights[1] : (s + 1) * heights[1]]
        gather_start("z1" + suffix[c], z1_slot(c))

    def solve_1(c):
        gather_step("z1" + suffix[c], z1_slot(c), rows_n - 1)
        solved = dot32(d1[...].reshape(height, whole), z1[c].reshape(whole, wide)).astype(jnp.bfloat16)
        y1s[c] = solved.reshape(2, heights[1], wide)
        swap_start("y1" + suffix[c], 1, y1_src[c], y1_dst[c])
        y1[c, row, :, at_cols(place[1])] = y1s[c, place[1]]

    def spread_1(c):
        swap_wait("y1" + suffix[c], 1, y1_src[c], y1_dst[c])
        gather_start("y1" + suffix[c], y1_slot(c))

    u2_src = lambda target: u2s.at[:, at_cols(block_of(target))]
    u2_dst = lambda sender, d: u2r.at[d - 1]

    def update_2(c):
        gather_step("y1" + suffix[c], y1_slot(c), rows_n - 1)
        update = u2[:, cols_of(c)] + dot32(p2[:, whole:], y1[c].reshape(half, chunk)) * live(2)
        u2[:, cols_of(c)] = update
        u2s[:, cols_of(c)] = update.astype(jnp.bfloat16)
        swap_start("u2", 2, u2_src, u2_dst, lambda target: target % 2 == c)

    def later_3(c):
        u3[:, cols_of(c)] += dot32(p3[:, whole : whole + half], y1[c].reshape(half, chunk)) * live(4)

    def reduce_2(c):
        @pl.when(own_chunk == c)
        def _():
            swap_wait("u2", 2, u2_src, u2_dst)
            total = u2[:, at_cols(block_of(place[2]))]
            for d in range(3):
                total = total + u2r[d].astype(jnp.float32)
            reduced = (b2[...].reshape(height, wide).astype(jnp.float32) - total).astype(jnp.bfloat16)
            for s in range(4):
                z2[s, row] = reduced[s * heights[2] : (s + 1) * heights[2]]

        direct_start("z2", z2_slot, own_chunk == c)

    def spread(d, e, position):
        here = leaf - place[2] + (place[2] + d) % 4
        dst = y2.at[(row if position is None else (row - e + rows_n) % rows_n), :,
                    at_cols(block_of(place[2] if position is None else position))]
        src = y2s.at[(place[2] + d) % 4]
        return pltpu.make_async_remote_copy(
            src_ref=src, dst_ref=dst, send_sem=spread_send.at[d, e], recv_sem=spread_recv.at[d, e],
            device_id=(here, (row + e) % rows_n), device_id_type=MESH)

    others = [(d, e) for e in reversed(range(rows_n)) for d in range(4) if d or e]

    def solve_2(c):
        @pl.when(own_chunk == c)
        def _():
            direct_wait("z2", z2_slot)
            solved = dot32(d2[...].reshape(height, whole), z2[...].reshape(whole, wide)).astype(jnp.bfloat16)
            y2s[...] = solved.reshape(4, heights[2], wide)

        for d, e in others:
            begin(own_chunk == c, lambda d=d, e=e: spread(d, e, None))

        @pl.when(own_chunk == c)
        def _():
            y2[row, :, at_cols(block_of(place[2]))] = y2s[place[2]]

    fold = height // 2
    low = lax.broadcasted_iota(jnp.int32, (fold, wide), 1) < wide // 2

    def folded(top, bottom):
        return (
            jnp.where(low, top, pltpu.roll(bottom, wide // 2, 1)),
            jnp.where(low, pltpu.roll(top, wide // 2, 1), bottom),
        )

    u3_src = lambda target: u3s.at[target]
    u3_dst = lambda sender, d: u3r.at[d - 1]

    def update_3(c):
        for d, e in others:
            sender = (place[2] - d + 4) % 4

            @pl.when(sender % 2 == c)
            def _(d=d, e=e, sender=sender):
                spread(d, e, sender).wait_recv()

        known = y2[:, :, c * chunk : (c + 1) * chunk].reshape(whole // 4, chunk)
        update = u3[:, cols_of(c)] + dot32(p3[:, whole + half :], known) * live(5)
        for k in range(2):
            block = update[:, k * wide : (k + 1) * wide]
            sides = folded(block[:fold], block[fold:])
            for side in range(2):
                u3s[4 * side + 2 * k + c] = sides[side].astype(jnp.bfloat16)
        swap_start("u3", 3, u3_src, u3_dst, lambda target: target % 2 == c)

    def reduce_3(c):
        @pl.when(own_chunk == c)
        def _():
            own_b = b3[...].astype(jnp.float32)
            sides = folded(own_b[:4].reshape(fold, wide), own_b[4:].reshape(fold, wide))
            own_b = jnp.where(place[3] < leaves_n // 2, sides[0], sides[1])
            swap_wait("u3", 3, u3_src, u3_dst)
            total = u3s[place[3]].astype(jnp.float32)
            for d in range(leaves_n - 1):
                total = total + u3r[d].astype(jnp.float32)
            reduced = (own_b - total).astype(jnp.bfloat16)
            for s in range(4):
                z3[s, row] = reduced[s * heights[3] : (s + 1) * heights[3]]

        direct_start("z3", z3_slot, own_chunk == c)

    y3_src = lambda target: y3s.at[target]
    y3_dst = lambda sender, d: y3r.at[sender]

    def solve_3():
        direct_wait("z3", z3_slot)
        known = z3[...].reshape(half, wide)
        left = dot32(d3[:, :, :half].reshape(height, half), known)
        right = dot32(d3[:, :, half:].reshape(height, half), known)
        solved = left + pltpu.roll(right, wide // 2, 1)
        low_all = lax.broadcasted_iota(jnp.int32, (height, wide), 1) < wide // 2
        solved = jnp.where(low_all, solved, pltpu.roll(solved, wide // 2, 1))
        y3s[...] = solved.astype(jnp.bfloat16).reshape(leaves_n, heights[3], wide)
        swap_start("y3", 3, y3_src, y3_dst)
        y3r[place[3]] = y3s[place[3]]

    update_1(0)
    arrived(rows_n - 1, add_rest(0))
    reduce_1(0)
    update_1(1)
    gather_step("z1a", z1_slot(0), 1)
    reduce_1(1)
    for step in range(2, rows_n - 1):
        gather_step("z1a", z1_slot(0), step)
        gather_step("z1b", z1_slot(1), step - 1)
    arrived(rows_n - 1, add_rest(1))
    local_copies["d1"].wait()
    swap_wait(*fixed[CHUNKS])
    solve_1(0)
    gather_step("z1b", z1_slot(1), rows_n - 2)
    spread_1(0)
    solve_1(1)
    gather_step("y1a", y1_slot(0), 1)
    spread_1(1)
    for step in range(2, rows_n - 1):
        gather_step("y1a", y1_slot(0), step)
        gather_step("y1b", y1_slot(1), step - 1)
    local_copies["b2"].wait()
    swap_wait(*fixed[CHUNKS + 1])
    update_2(0)
    gather_step("y1b", y1_slot(1), rows_n - 2)
    later_3(0)
    reduce_2(0)
    update_2(1)
    taken_all("d2p", d2)
    reduce_2(1)
    later_3(1)
    for c in range(CHUNKS):
        out[level_rows(1), cols_of(c)] = y1[c, row]
    local_copies["b3"].wait()
    swap_wait(*fixed[CHUNKS + 3])
    taken_all("d3p", d3)
    solve_2(0)
    solve_2(1)
    update_3(0)
    reduce_3(0)
    update_3(1)
    reduce_3(1)
    out[level_rows(2), :] = y2[row]
    solve_3()
    swap_wait("y3", 3, y3_src, y3_dst)
    low_out = lax.broadcasted_iota(jnp.int32, (heights[3], wide), 1) < wide // 2
    for k in range(leaves_n // 2):
        first = 2 * (k % 2) + k // 2
        out[level_rows(3), pl.ds(k * wide, wide)] = jnp.where(
            low_out, y3r[first].astype(jnp.float32), y3r[first + leaves_n // 2].astype(jnp.float32)
        ).astype(jnp.bfloat16)

    for can, make in pending:
        if can is None:
            make().wait_send()
        else:
            @pl.when(can)
            def _(make=make):
                make().wait_send()


def fits(rows_n, leaves_n, rhs, inv_diag, off_diag):
    whole = inv_diag.shape[3]
    right_n = rhs.shape[3]
    return (
        leaves_n == 2**TREE_LEVELS
        and rows_n > 2
        and whole % (leaves_n * rows_n * ROW_TILE) == 0
        and whole % (rows_n * LANES) == 0
        and whole % (4 * LANES) == 0
        and right_n == 4 * LANES
    )


def tree_shards(rhs, inv_diag, off_diag, pair_mask):
    rows_n = lax.axis_size("row")
    leaves_n = lax.axis_size("leaf")
    whole = inv_diag.shape[3]
    right_n = rhs.shape[3]
    height = off_diag.shape[2]
    chunk = right_n // CHUNKS
    hs = [height // 2**m for m in range(TREE_LEVELS + 1)]
    bf16, f32 = jnp.bfloat16, jnp.float32
    vm = pltpu.VMEM
    scratch = [
        vm((height, whole), bf16),
        vm((2, hs[1], whole), bf16), vm((4, hs[2], whole), bf16), vm((8, hs[3], whole), bf16),
        vm((height, whole), bf16), vm((height, whole + whole // 2), bf16),
        vm((height, whole + whole // 2 + whole // 4), bf16),
        vm((CHUNKS, 2, hs[1], LANES), bf16), vm((4, hs[2], LANES), bf16), vm((8, hs[3], LANES), bf16),
        vm((CHUNKS, rows_n, height, chunk), bf16),
        vm((CHUNKS, 2, rows_n, hs[1], LANES), bf16),
        vm((4, rows_n, hs[2], LANES), bf16),
        vm((4, rows_n, hs[3], LANES), bf16),
        vm((CHUNKS, rows_n, height, chunk), bf16),
        vm((CHUNKS, rows_n, hs[1], chunk), bf16),
        vm((rows_n, hs[2], right_n), bf16),
        vm((CHUNKS, height, chunk), f32),
        vm((CHUNKS, height, chunk), f32), vm((height, right_n), f32), vm((height, right_n), f32),
        vm((CHUNKS, height, chunk), bf16), vm((height, right_n), bf16),
        vm((leaves_n, height // 2, LANES), bf16),
        vm((CHUNKS, 1, height, LANES), bf16), vm((3, height, LANES), bf16),
        vm((leaves_n - 1, height // 2, LANES), bf16),
        vm((CHUNKS, 2, hs[1], LANES), bf16), vm((4, hs[2], LANES), bf16),
        vm((leaves_n, hs[3], LANES), bf16), vm((leaves_n, hs[3], LANES), bf16),
        pltpu.SemaphoreType.DMA((len(GATHERS), rows_n)),
        pltpu.SemaphoreType.DMA((len(GATHERS), rows_n)),
        pltpu.SemaphoreType.DMA((len(GATHERS), rows_n)),
        pltpu.SemaphoreType.DMA((len(SWAPS), leaves_n)),
        pltpu.SemaphoreType.DMA((len(SWAPS), leaves_n)),
        pltpu.SemaphoreType.DMA((len(LOCALS),)),
        pltpu.SemaphoreType.DMA((4, rows_n)),
        pltpu.SemaphoreType.DMA((4, rows_n)),
    ]
    pack = rhs.shape[2]
    flops = 2 * right_n * (pack * whole + height * off_diag.shape[3])
    moved = 2 * (pack * whole + height * off_diag.shape[3] + 3 * pack * right_n)
    solved = pl.pallas_call(
        functools.partial(tree_kernel, rows_n, leaves_n),
        out_shape=jax.ShapeDtypeStruct((pack, right_n), bf16),
        in_specs=[pl.BlockSpec(memory_space=pltpu.SMEM)] + [pl.BlockSpec(memory_space=pltpu.HBM)] * 3,
        out_specs=pl.BlockSpec(memory_space=pltpu.VMEM),
        scratch_shapes=scratch,
        compiler_params=pltpu.CompilerParams(
            collective_id=0, has_side_effects=True, vmem_limit_bytes=62 * 2**20),
        cost_estimate=pl.CostEstimate(flops=flops, bytes_accessed=moved, transcendentals=0),
    )(pair_mask[0, 0], rhs[0, 0], inv_diag[0, 0], off_diag[0, 0])
    return solved.astype(f32)[None, None]


def solution(mesh):
    in_specs = (
        P("leaf", "row", None, None),
        P("leaf", "row", None, None),
        P("leaf", "row", None, None),
        P("leaf", "row", None),
    )
    out_specs = P("leaf", "row", None, None)

    def run(rhs, inv_diag, off_diag, pair_mask):
        fit = fits(mesh.shape["row"], mesh.shape["leaf"], rhs, inv_diag, off_diag)
        body = tree_shards if fit else shards
        return jax.shard_map(body, mesh=mesh, in_specs=in_specs, out_specs=out_specs, check_vma=False)(
            rhs, inv_diag, off_diag, pair_mask
        )

    return run
```
